128 devices in a mesh: seq: 4 (over y_lo, core), fsdp: 32 (over y_hi, x, z).
Axes of the slice: x: 4, y: 4 (y_hi: 2, y_lo: 2; y = y_hi * 2 + y_lo), z: 4, core: 2. Of those that a mesh axis runs over, the one named last changes fastest.
Arguments:
- tokens: bfloat16 [32, 1024, 1024], P('fsdp', 'seq'), may hold values from -6 to 6
- norm1_gain: bfloat16 [1024], P(('seq', 'fsdp')), may hold values from 0.099609375 to 1.8984375
- query_weight: bfloat16 [1024, 1024], P(('seq', 'fsdp')), may hold values from -0.1875 to 0.1875
- key_weight: bfloat16 [1024, 512], P(('seq', 'fsdp')), may hold values from -0.1875 to 0.1875
- value_weight: bfloat16 [1024, 512], P(('seq', 'fsdp')), may hold values from -0.1875 to 0.1875
- output_weight: bfloat16 [1024, 1024], P(('seq', 'fsdp')), may hold values from -1.5 to 1.5
- norm2_gain: bfloat16 [1024], P(('seq', 'fsdp')), may hold values from 0.099609375 to 1.8984375
- router_weight: bfloat16 [1024, 32], P(('seq', 'fsdp')), may hold values from -0.09375 to 0.09375
- expert_gate: bfloat16 [32, 1024, 512], P('fsdp', 'seq'), may hold values from -0.1875 to 0.1875
- expert_up: bfloat16 [32, 1024, 512], P('fsdp', 'seq'), may hold values from -0.1875 to 0.1875
- expert_down: bfloat16 [32, 512, 1024], P('fsdp', 'seq'), may hold values from -1 to 1
- routes: int32 [32, 1024, 8], P('fsdp', 'seq'), may hold values from 0 to 31, all different within a row; in each aligned block of 256 rows (0 to 255, 256 to 511, ..., all dimensions but the last counted through in order) at most 80 rows name the same one
- cotangent: bfloat16 [32, 1024, 1024], P('fsdp', 'seq'), may hold values from -6 to 6
Outputs:
- output: bfloat16 [32, 1024, 1024], P('fsdp', 'seq')
- grad_tokens: float32 [32, 1024, 1024], P('fsdp', 'seq')
- grad_norm1_gain: float32 [1024], P(('seq', 'fsdp'))
- grad_query_weight: float32 [1024, 1024], P(('seq', 'fsdp'))
- grad_key_weight: float32 [1024, 512], P(('seq', 'fsdp'))
- grad_value_weight: float32 [1024, 512], P(('seq', 'fsdp'))
- grad_output_weight: float32 [1024, 1024], P(('seq', 'fsdp'))
- grad_norm2_gain: float32 [1024], P(('seq', 'fsdp'))
- grad_router_weight: float32 [1024, 32], P(('seq', 'fsdp'))
- grad_expert_gate: float32 [32, 1024, 512], P('fsdp', 'seq')
- grad_expert_up: float32 [32, 1024, 512], P('fsdp', 'seq')
- grad_expert_down: float32 [32, 512, 1024], P('fsdp', 'seq')
The draws below stay inside these ranges and needn't reach their ends.
Inputs may be any that keep to these rules, and one draw needn't show every extreme that they name: `routes`: each row names 8 different experts. In each aligned block of 256 rows (the tokens of one device) no expert is named by more than 80 rows, a bound that some block reaches.
All inputs are finite; a program needn't handle non-finite values.
Results may differ from the reference program's by a relative error of at most 0.02.
Values may be sent and summed in bfloat16 or wider, within the bound.
No kernel may reach another device: no remote copies, remote signals or barrier semaphores. Data moves between devices by JAX's collectives and lax.ppermute only.
A program may use at most 192 MiB of HBM per device.

```python
import math
import jax
import jax.numpy as jnp
import numpy as np
from jax import lax

D = 1024
HEADS = 16
KV_HEADS = 8
HEAD = 64
FF = 512
EXPERTS = 32
TOPK = 8
TOK_DEV = 256
LENGTH = 1024
SEQS = 32
QD = 1024
KD = 512
CAP = 80


def shard_levels(stream_key, shape, cuts, smallest, high):
    def one(axis_at, parts):
        draws = jax.random.uniform(jax.random.fold_in(jax.random.fold_in(stream_key, 6), axis_at), (parts,), jnp.float32, smallest / len(cuts), high / len(cuts))
        return jnp.repeat(jnp.exp(draws), shape[axis_at] // parts).reshape((-1,) + (1,) * (len(shape) - axis_at - 1))

    loudness = one(*cuts[0])
    for cut in cuts[1:]:
        loudness = loudness * one(*cut)
    return loudness


def routed_block(key, own, number, rows, amount, top, reach, skew):
    ranking = jax.random.permutation(key, amount)
    crowded, usual = load_shares(amount, rows * top, reach, skew, True), load_shares(amount, rows * top, reach, skew, False)
    places = jnp.arange(amount)

    def named(sizes, rotation):
        used = int((sizes > 0).sum())
        fixed = max(1, used // 4)
        passed = fixed + (places - fixed + rotation * (used - fixed)) % max(1, amount - fixed)
        return jnp.zeros((amount,), jnp.int32).at[ranking[jnp.where(places < fixed, places, passed)]].set(jnp.asarray(sizes, jnp.int32))

    sizes = jnp.where(number % 4 == 0, named(crowded, number // 4), named(usual, number - number // 4 - 1))
    mixed = jax.random.permutation(jax.random.fold_in(own, 3), amount)
    donor, sink = mixed[0:amount // 2 * 2:2], mixed[1:amount // 2 * 2:2]
    slack = jnp.minimum(sizes[donor] - 1, reach - sizes[sink]) // 2
    slack = jnp.where((donor == ranking[0]) | (sink == ranking[0]) | (sizes[sink] == 0), 0, jnp.maximum(slack, 0))
    passed = jax.random.randint(jax.random.fold_in(own, 4), (amount // 2,), 0, 1 << 20) % (slack + 1)
    sizes = sizes.at[donor].add(-passed).at[sink].add(passed)
    items = jnp.searchsorted(jnp.cumsum(sizes), jnp.arange(rows * top), side="right").astype(jnp.int32)
    table = items.reshape(top, rows).T
    table = table[jax.random.permutation(jax.random.fold_in(own, 1), rows)]
    rotation = jax.random.randint(jax.random.fold_in(own, 2), (rows, 1), 0, top)
    return jnp.take_along_axis(table, (jnp.arange(top)[None, :] + rotation) % top, axis=1)


def load_shares(number_of, total, bound, skew, full):
    portions = [(1 << 20) // math.isqrt(standing ** skew) + 1 for standing in range(1, number_of + 1)]
    largest = bound if full else min(bound, max(-(-total // number_of), total * portions[0] // sum(portions)))
    least = 1 if total - largest >= number_of - 1 else 0
    counts, spare = [largest] + [least] * (number_of - 1), total - largest - least * (number_of - 1)
    while spare > 0:
        movable = [i for i in range(1, number_of) if counts[i] < largest] or [i for i in range(1, number_of) if counts[i] < bound]
        pool, budget = sum([portions[i] for i in movable]), spare
        for i in movable:
            addition = min(bound - counts[i], max(1, budget * portions[i] // pool), spare)
            counts[i] = counts[i] + addition
            spare = spare - addition
    return np.array(counts)


def bell_draw(rng, dims, deviation, bound, shards=(), dtype=jnp.bfloat16):
    values = deviation * jax.random.normal(rng, dims, jnp.float32)
    if shards:
        values = values * shard_levels(rng, dims, shards, -0.22, 0.18)
    return jnp.clip(values, -bound, bound).astype(dtype)


def setup_inputs(seed: int = 0) -> dict:
    splits = jax.random.split(jax.random.key(seed), 14)
    tokens = bell_draw(splits[0], (SEQS, LENGTH, D), 1.0, 6.0, ((0, 32), (1, 4)))
    norm1_gain = jnp.clip(1.0 + 0.18 * jax.random.normal(splits[1], (D,), jnp.float32), 0.099609375, 1.8984375).astype(jnp.bfloat16)
    query_weight = bell_draw(splits[2], (D, QD), D ** -0.5, 0.1875, ((0, 128),))
    key_weight = bell_draw(splits[3], (D, KD), D ** -0.5, 0.1875, ((0, 128),))
    value_weight = bell_draw(splits[4], (D, KD), D ** -0.5, 0.1875, ((0, 128),))
    output_weight = bell_draw(splits[5], (QD, D), (QD // 64) ** -0.5, 1.5, ((0, 128),))
    norm2_gain = jnp.clip(1.0 + 0.18 * jax.random.normal(splits[6], (D,), jnp.float32), 0.099609375, 1.8984375).astype(jnp.bfloat16)
    router_weight = bell_draw(splits[7], (D, EXPERTS), (4 * D) ** -0.5, 0.09375, ((0, 128),))
    expert_gate = bell_draw(splits[8], (EXPERTS, D, FF), D ** -0.5, 0.1875, ((0, 32), (1, 4)))
    expert_up = bell_draw(splits[9], (EXPERTS, D, FF), D ** -0.5, 0.1875, ((0, 32), (1, 4)))
    expert_down = bell_draw(splits[10], (EXPERTS, FF, D), (FF // 16) ** -0.5, 1.0, ((0, 32), (1, 4)))
    routes_keys = jax.random.split(jax.random.fold_in(splits[11], 1), SEQS * LENGTH // TOK_DEV)
    routes_turns = jax.random.permutation(jax.random.fold_in(splits[11], 3), SEQS * LENGTH // TOK_DEV)
    routes = jax.vmap(lambda own, number: routed_block(jax.random.fold_in(splits[11], 2), own, number, TOK_DEV, EXPERTS, TOPK, CAP, 0))(routes_keys, routes_turns).reshape((SEQS, LENGTH, TOPK))
    cotangent = bell_draw(splits[12], (SEQS, LENGTH, D), 1.0, 6.0, ((0, 32), (1, 4)))
    return dict(tokens=tokens, norm1_gain=norm1_gain, query_weight=query_weight, key_weight=key_weight, value_weight=value_weight, output_weight=output_weight, norm2_gain=norm2_gain, router_weight=router_weight, expert_gate=expert_gate, expert_up=expert_up, expert_down=expert_down, routes=routes, cotangent=cotangent)


epsilon = 1e-06
rope_base = 10000.0
highest = lax.Precision.HIGHEST

@jax.custom_vjp
def low(v):
    return lax.optimization_barrier(v.astype(jnp.bfloat16)).astype(jnp.float32)

@jax.custom_vjp
def low_back(v):
    return v

def low_keep(v):
    return (low(v), None)

def low_pass(kept, grad):
    return (grad,)

def back_keep(v):
    return (v, None)

def back_low(kept, grad):
    return (low(grad),)
low.defvjp(low_keep, low_pass)
low_back.defvjp(back_keep, back_low)

def rms_scale(values, gain_vec):
    factor = lax.rsqrt(lax.optimization_barrier(jnp.mean(values * values, axis=-1, keepdims=True)) + epsilon)
    return values * factor * gain_vec

def rope_angles(positions, head_size):
    half_size = head_size // 2
    freqs = rope_base ** (-2.0 * jnp.arange(half_size).astype(jnp.float32) / head_size)
    angles = positions.astype(jnp.float32)[:, None] * freqs[None, :]
    return (jnp.cos(angles), jnp.sin(angles))

def rotate(values, angle_cos, angle_sin):
    half_size = values.shape[-1] // 2
    first_half = values[..., :half_size]
    second_half = values[..., half_size:]
    cos_part = angle_cos[:, None, :]
    sin_part = angle_sin[:, None, :]
    return jnp.concatenate([first_half * cos_part - second_half * sin_part, second_half * cos_part + first_half * sin_part], axis=-1)

def attention(queries, key_rows, value_rows):
    length = queries.shape[0]
    row_block = min(512, length)
    kv_heads = key_rows.shape[1]
    group_size = queries.shape[1] // kv_heads
    head_size = queries.shape[2]
    blocks = queries.reshape(length // row_block, row_block, kv_heads, group_size, head_size)
    starts = (jnp.arange(length // row_block) * row_block).astype(jnp.int32)
    columns = jnp.arange(length).astype(jnp.int32)

    def one_block(pieces):
        query_block, row_start = pieces
        rows = row_start + jnp.arange(row_block).astype(jnp.int32)
        raw = jnp.einsum('qjgd,kjd->jgqk', query_block, key_rows, precision=highest)
        scores = low_back(raw * head_size ** (-0.5))
        scores = jnp.where(columns[None, :] <= rows[:, None], scores, -1e+30)
        row_peak = lax.optimization_barrier(jnp.max(scores, axis=-1, keepdims=True))
        exp_scores = jnp.exp(scores - row_peak)
        attn_probs = exp_scores / lax.optimization_barrier(jnp.sum(exp_scores, axis=-1, keepdims=True))
        return jnp.einsum('jgqk,kjd->qjgd', low(attn_probs), value_rows, precision=highest)
    mixed = lax.map(jax.checkpoint(one_block), (blocks, starts))
    return mixed.reshape(length, kv_heads * group_size * head_size)

def layer(inputs, params, choice_rows):
    gain_one, query_w, key_w, value_w, output_w, gain_two, router_w, gate_w, up_w, down_w = params
    length = inputs.shape[0]
    hidden_one = low(rms_scale(inputs, gain_one))
    angle_cos, angle_sin = rope_angles(jnp.arange(length).astype(jnp.int32), HEAD)
    query_pre = low_back(jnp.dot(hidden_one, query_w, precision=highest))
    queries = low(rotate(query_pre.reshape(length, HEADS, HEAD), angle_cos, angle_sin))
    key_pre = low_back(jnp.dot(hidden_one, key_w, precision=highest))
    key_rows = low(rotate(key_pre.reshape(length, KV_HEADS, HEAD), angle_cos, angle_sin))
    value_rows = low(low_back(jnp.dot(hidden_one, value_w, precision=highest))).reshape(length, KV_HEADS, HEAD)
    mixed = low_back(low(attention(queries, key_rows, value_rows)))
    residual = inputs + low_back(jnp.dot(mixed, output_w, precision=highest))
    hidden_two = low(rms_scale(residual, gain_two))
    logits = low_back(jnp.dot(hidden_two, router_w, precision=highest))
    expert_ids = jnp.arange(EXPERTS).astype(jnp.int32)
    picker = (choice_rows[:, :, None] == expert_ids[None, None, :]).astype(jnp.float32)
    chosen = lax.optimization_barrier(jnp.sum(logits[:, None, :] * picker, axis=-1))
    gates = jax.nn.softmax(chosen, axis=-1)
    slot_cap = length // TOK_DEV * CAP
    flat_expert = choice_rows.reshape(-1).astype(jnp.int32)
    onehot = (flat_expert[:, None] == expert_ids[None, :]).astype(jnp.int32)
    slot_rank = lax.optimization_barrier(jnp.sum((jnp.cumsum(onehot, axis=0) - onehot) * onehot, axis=1)).astype(jnp.int32)
    slot_index = (flat_expert * slot_cap + slot_rank).astype(jnp.int32)
    owners = (jnp.arange(length * TOPK) // TOPK).astype(jnp.int32)
    slot_owner = jnp.zeros((EXPERTS * slot_cap,), jnp.int32).at[slot_index].set(owners)
    slot_used = jnp.zeros((EXPERTS * slot_cap,), jnp.float32).at[slot_index].set(1.0)
    expert_rows = low_back(hidden_two[slot_owner] * slot_used[:, None]).reshape(EXPERTS, slot_cap, D)
    gate_pre = low_back(jnp.einsum('erd,edf->erf', expert_rows, gate_w, precision=highest))
    up_pre = low_back(jnp.einsum('erd,edf->erf', expert_rows, up_w, precision=highest))
    activated = low(jax.nn.silu(gate_pre) * up_pre)
    expert_out = low_back(low(jnp.einsum('erf,efd->erd', activated, down_w, precision=highest)))
    gathered = expert_out.reshape(EXPERTS * slot_cap, D)[slot_index].reshape(length, TOPK, D)
    return residual + lax.optimization_barrier(jnp.sum(gates[:, :, None] * gathered, axis=1))

def reference(tokens, norm1_gain, query_weight, key_weight, value_weight, output_weight, norm2_gain, router_weight, expert_gate, expert_up, expert_down, routes, cotangent):
    params = tuple((weight_arg.astype(jnp.float32) for weight_arg in (norm1_gain, query_weight, key_weight, value_weight, output_weight, norm2_gain, router_weight, expert_gate, expert_up, expert_down)))
    inputs = tokens.astype(jnp.float32)

    def forward(inputs, params):

        def step(carry, pieces):
            seq_rows, choice_rows = pieces
            return (carry, jax.checkpoint(layer)(seq_rows, params, choice_rows))
        return lax.scan(step, None, (inputs, routes))[1]
    result, pullback = jax.vjp(forward, inputs, params)
    grad_inputs, grad_params = pullback(cotangent.astype(jnp.float32))
    return (result.astype(jnp.bfloat16), grad_inputs, grad_params[0], grad_params[1], grad_params[2], grad_params[3], grad_params[4], grad_params[5], grad_params[6], grad_params[7], grad_params[8], grad_params[9])
```

```python
import functools

import jax
import jax.numpy as jnp
from jax import lax
from jax.experimental import pallas as pl
from jax.experimental.pallas import tpu as pltpu
from jax.sharding import Mesh
from jax.sharding import PartitionSpec as P

HEADS = 16
KV_HEADS = 8
HEAD = 64
TOPK = 8
CAP = 80
TOK = 256
D = 1024
FF = 512
EXPERTS = 32
SHARE = 8
SLOTS = SHARE * CAP
BLOCKS = 8
HALF = FF // 2
GROUP = 4
LENGTH = 1024

epsilon = 1e-06
rope_base = 10000.0

AXES = ("ylo", "core", "yhi", "x", "z")
SEQ = ("ylo", "core")
FSDP = ("yhi", "x", "z")
PLANE = ("x", "yhi", "ylo")

f32 = jnp.float32
bf16 = jnp.bfloat16

NT = (((1,), (1,)), ((), ()))
TN = (((0,), (0,)), ((), ()))
VMEM_LIMIT = 56 * 1024 * 1024


def dot(a, b, dims=(((1,), (0,)), ((), ()))):
    return lax.dot_general(a, b, dims, preferred_element_type=f32)


def iota(shape, axis):
    return lax.broadcasted_iota(jnp.int32, shape, axis)


def as_bf16(cond):
    return jnp.where(cond, 1.0, 0.0).astype(bf16)


def head_lanes_rope(head):
    lane = iota((1, 256), 1) % 128
    return (lane >= 32 * head) & (lane < 32 * head + 32)


def head_lanes(head):
    lane = iota((1, 256), 1)
    return (lane >= 64 * head) & (lane < 64 * head + 64)


def spread_keys():
    row, col = iota((128, 256), 0), iota((128, 256), 1)
    source = (col // 128) * 64 + ((col % 128) // 64) * 32 + col % 32
    return row == source, (col % 64) < 32


def spread_values():
    row, col = iota((128, 256), 0), iota((128, 256), 1)
    return row == (col // 128) * 64 + col % 64, (col % 128) < 64


def front_kernel(x_ref, w_ref, gain_ref, cos_ref, sin_ref, q_ref, k_ref, v_ref, o_ref, lse_ref, h_ref):
    wq = w_ref[:, :256]
    wk = dot(w_ref[:, 256:384], as_bf16(spread_keys()[0])).astype(bf16)
    wv = dot(w_ref[:, 384:512], as_bf16(spread_values()[0])).astype(bf16)
    for i in range(4):
        rows = slice(256 * i, 256 * i + 256)
        x = x_ref[rows].astype(f32)
        r = lax.rsqrt(jnp.mean(x * x, axis=-1, keepdims=True) + epsilon)
        h = (x * r * gain_ref[...]).astype(bf16)
        h_ref[rows] = h
        c, s = cos_ref[rows], sin_ref[rows]
        for w, out in ((wq, q_ref), (wk, k_ref)):
            pre = dot(h, w)
            a, b = pre[:, :128], pre[:, 128:]
            out[rows] = jnp.concatenate([a * c - b * s, b * c + a * s], axis=1).astype(bf16)
        v_ref[rows] = dot(h, wv).astype(bf16)
    for i in range(4):
        rows = slice(256 * i, 256 * i + 256)
        n = 256 * (i + 1)
        seen = iota((256, n), 1) <= iota((256, n), 0) + 256 * i
        mixed = jnp.zeros((256, 256), f32)
        logs = jnp.zeros((256, 128), f32)
        for head in range(GROUP):
            q = q_ref[rows] * as_bf16(head_lanes_rope(head))
            scores = jnp.where(seen, dot(q, k_ref[:n], NT) * HEAD**-0.5, -1e30)
            peak = jnp.max(scores, axis=-1, keepdims=True)
            e = jnp.exp(scores - peak)
            total = jnp.sum(e, axis=-1, keepdims=True)
            probs = (e * (1.0 / total)).astype(bf16)
            mixed = mixed + dot(probs, v_ref[:n] * as_bf16(head_lanes(head)))
            logs = jnp.where(iota((256, 128), 1) == head, peak + jnp.log(total), logs)
        o_ref[rows] = mixed.astype(bf16)
        lse_ref[rows] = logs


def front(x_all, w, gain, cos, sin):
    shape = jax.ShapeDtypeStruct
    return pl.pallas_call(
        front_kernel,
        out_shape=(
            shape((LENGTH, 256), bf16),
            shape((LENGTH, 256), bf16),
            shape((LENGTH, 256), bf16),
            shape((LENGTH, 256), bf16),
            shape((LENGTH, 128), f32),
            shape((LENGTH, D), bf16),
        ),
        compiler_params=pltpu.CompilerParams(vmem_limit_bytes=VMEM_LIMIT),
        cost_estimate=pl.CostEstimate(flops=8_000_000_000, bytes_accessed=10_000_000, transcendentals=4_000_000),
        name="front",
    )(x_all, w, gain, cos, sin)


def back_kernel(q_ref, k_ref, v_ref, do_ref, lse_ref, cos_ref, sin_ref, out_ref, dk_ref, dv_ref):
    dk_ref[...] = jnp.zeros_like(dk_ref)
    dv_ref[...] = jnp.zeros_like(dv_ref)
    scale = HEAD**-0.5
    for i in range(4):
        rows = slice(256 * i, 256 * i + 256)
        n = 256 * (i + 1)
        seen = iota((256, n), 1) <= iota((256, n), 0) + 256 * i
        dq = jnp.zeros((256, 256), f32)
        for head in range(GROUP):
            lanes = head_lanes_rope(head)
            q = q_ref[rows] * as_bf16(lanes)
            do = do_ref[rows] * as_bf16(head_lanes(head))
            scores = dot(q, k_ref[:n], NT) * scale - lse_ref[rows, head : head + 1]
            probs = jnp.where(seen, jnp.exp(jnp.where(seen, scores, 0.0)), 0.0)
            dprobs = dot(do, v_ref[:n], NT)
            row_dot = jnp.sum(probs * dprobs, axis=-1, keepdims=True)
            ds = (probs * (dprobs - row_dot)).astype(bf16)
            dq = dq + jnp.where(lanes, dot(ds, k_ref[:n]), 0.0)
            dk_ref[:n] += dot(ds, q, TN)
            dv_ref[:n] += dot(probs.astype(bf16), do, TN)
        c, s = cos_ref[rows], sin_ref[rows]
        a, b = dq[:, :128] * scale, dq[:, 128:] * scale
        out_ref[rows, :256] = jnp.concatenate([a * c + b * s, b * c - a * s], axis=1).astype(bf16)
    keep_keys, first_key = spread_keys()
    keep_values, first_value = spread_values()
    pick_keys = as_bf16(keep_keys & first_key)
    pick_values = as_bf16(keep_values & first_value)
    for i in range(4):
        rows = slice(256 * i, 256 * i + 256)
        c, s = cos_ref[rows], sin_ref[rows]
        a, b = dk_ref[rows, :128] * scale, dk_ref[rows, 128:] * scale
        a, b = a * c + b * s, b * c - a * s
        a, b = a + pltpu.roll(a, 96, 1), b + pltpu.roll(b, 96, 1)
        out_ref[rows, 256:384] = dot(jnp.concatenate([a, b], axis=1).astype(bf16), pick_keys, NT).astype(bf16)
        a, b = dv_ref[rows, :128], dv_ref[rows, 128:]
        a, b = a + pltpu.roll(a, 64, 1), b + pltpu.roll(b, 64, 1)
        out_ref[rows, 384:512] = dot(jnp.concatenate([a, b], axis=1).astype(bf16), pick_values, NT).astype(bf16)


def back(q, k, v, do, lse, cos, sin):
    return pl.pallas_call(
        back_kernel,
        out_shape=jax.ShapeDtypeStruct((LENGTH, 512), bf16),
        scratch_shapes=[pltpu.VMEM((LENGTH, 256), f32), pltpu.VMEM((LENGTH, 256), f32)],
        compiler_params=pltpu.CompilerParams(vmem_limit_bytes=VMEM_LIMIT),
        cost_estimate=pl.CostEstimate(flops=14_000_000_000, bytes_accessed=6_000_000, transcendentals=4_000_000),
        name="back",
    )(q, k, v, do, lse, cos, sin)


def slot_rows(codes, z):
    row = iota((SLOTS, EXPERTS), 0)
    start = (iota((SLOTS, EXPERTS), 1) - SHARE * z) * CAP
    own = (row >= start) & (row < start + CAP)
    place = jnp.sum(jnp.where(own, row - start, 0), axis=1, keepdims=True).astype(f32)
    spread = dot(as_bf16(own), codes, NT)
    return as_bf16(spread == place), own


def slot_columns(codes, z):
    column = iota((EXPERTS, SLOTS), 1)
    start = (iota((EXPERTS, SLOTS), 0) - SHARE * z) * CAP
    own = (column >= start) & (column < start + CAP)
    place = jnp.sum(jnp.where(own, column - start, 0), axis=0, keepdims=True).astype(f32)
    return as_bf16(dot(codes, as_bf16(own)) == place)


def gate_table(logits, codes):
    routed = codes >= 0
    logits = jnp.where(routed, logits, -1e30)
    e = jnp.where(routed, jnp.exp(logits - jnp.max(logits, axis=-1, keepdims=True)), 0.0)
    return e / jnp.sum(e, axis=-1, keepdims=True)


def split(values):
    high = values.astype(bf16)
    return high, (values - high.astype(f32)).astype(bf16)


SCALAR = pl.BlockSpec(memory_space=pltpu.SMEM)
ANYWHERE = pl.BlockSpec(memory_space=pl.ANY)
PAIR = 2 * CAP


def whole(*shape):
    return pl.BlockSpec(shape, lambda e: (0,) * len(shape))


def per_expert(*shape):
    return pl.BlockSpec((1,) + shape, lambda e: (e,) + (0,) * len(shape))


def call(kernel, name, flops, moved, **kwargs):
    return pl.pallas_call(
        kernel,
        compiler_params=pltpu.CompilerParams(vmem_limit_bytes=VMEM_LIMIT),
        cost_estimate=pl.CostEstimate(flops=flops, bytes_accessed=moved, transcendentals=0),
        name=name,
        **kwargs,
    )


def rows_kernel(with_gates, z_ref, *refs):
    z = z_ref[0]
    if with_gates:
        values_refs, codes_refs, router_ref = refs[:2], refs[2:4], refs[4]
        rows_ref, gates_ref = refs[-2:]
    else:
        values_refs, codes_refs, rows_ref = refs[:2], refs[:2], refs[-1]
    for b in range(2):
        codes = codes_refs[b][:, -128:][:, :EXPERTS]
        values = values_refs[b][:, :D]
        place, own = slot_rows(codes, z)
        rows = dot(place, values).astype(bf16)
        for j in range(SHARE):
            rows_ref[j, 0, b * CAP : (b + 1) * CAP] = rows[j * CAP : (j + 1) * CAP]
        if with_gates:
            high, low = split(gate_table(dot(values, router_ref[...]), codes.astype(f32)))
            both = dot(place, high) + dot(place, low)
            gate = jnp.sum(jnp.where(own, both, 0.0), axis=1, keepdims=True)
            for j in range(SHARE):
                gates_ref[j, 0, b * CAP : (b + 1) * CAP] = gate[j * CAP : (j + 1) * CAP]


def rows_of(z, index, pair, codes, router, kept):
    with_gates = router is not None
    full = pl.BlockSpec((TOK, pair[0].shape[1]), lambda e: (0, 0))
    last = pl.BlockSpec((TOK, 128), lambda e: (0, D // 128))
    args, specs = [z, *pair], [SCALAR, full, full]
    if with_gates:
        args += [*codes, router]
        specs += [last, last, pl.BlockSpec((D, EXPERTS), lambda e: (0, 0))]
    widths = [(D, bf16)] + ([(1, f32)] if with_gates else [])
    out_specs = [pl.BlockSpec((SHARE, 1, PAIR, w), lambda e: (0, index, 0, 0)) for w, _ in widths]
    out_shape = [jax.ShapeDtypeStruct((SHARE, 4, PAIR, w), t) for w, t in widths]
    aliases = {}
    if kept is not None:
        aliases = {len(args) + i: i for i in range(len(kept))}
        args += kept
        specs += [ANYWHERE] * len(kept)
    return call(
        functools.partial(rows_kernel, with_gates), "rows", 1_500_000_000, 4_000_000,
        grid=(1,), in_specs=specs, out_specs=out_specs, out_shape=out_shape, input_output_aliases=aliases,
    )(*args)


def down_of(parts):
    return jnp.concatenate(
        [
            jnp.concatenate([parts[0, 128 * j : 128 * j + 128], parts[1, 128 * j : 128 * j + 128]], axis=0)
            for j in range(4)
        ],
        axis=1,
    )


def main_kernel(z_ref, x_ref, gy_ref, gate_ref, w_ref, *refs):
    codes_refs = refs[:8]
    act_ref, dg_ref, du_ref, own_ref, other_ref, kept, dgates, codes_kept = refs[8:]
    e = pl.program_id(0)
    z = z_ref[0]
    x = x_ref[0].reshape(SLOTS, D)
    gate_w = w_ref[:, :512].reshape(D, HALF)
    up_w = w_ref[:, 512:1024].reshape(D, HALF)
    da = dot(gy_ref[0].reshape(SLOTS, D), down_of(w_ref[:, 1024:]), NT)
    g = dot(x, gate_w)
    u = dot(x, up_w)
    gate = gate_ref[0].reshape(SLOTS, 1)
    s = jax.nn.sigmoid(g)
    silu = g * s
    act = silu * u
    dgates[e] = jnp.sum(act * da, axis=1, keepdims=True).reshape(BLOCKS, CAP, 1)
    act_ref[0] = (act * gate).astype(bf16)
    da = da * gate
    dg = (da * u * (s + silu * (1.0 - s))).astype(bf16)
    du = (da * silu).astype(bf16)
    dg_ref[0] = dg
    du_ref[0] = du
    back = dot(dg, gate_w, NT) + dot(du, up_w, NT)
    kept[e] = back.astype(bf16).reshape(BLOCKS, CAP, D)

    @pl.when(e == 0)
    def _():
        for b in range(BLOCKS):
            codes_kept[b] = codes_refs[b][...]

    @pl.when(e == SHARE - 1)
    def _():
        def pair(j, carry):
            for c, out in ((0, own_ref), (1, other_ref)):
                b = 2 * j + c
                codes = codes_kept[b][:, :EXPERTS]
                place = slot_columns(codes, z)
                rows = jnp.concatenate([kept[i, b] for i in range(SHARE)], axis=0)
                out[j, :, :D] = dot(place, rows).astype(bf16)
                _, own = slot_rows(codes, z)
                dgate = jnp.concatenate([dgates[i, b] for i in range(SHARE)], axis=0)
                high, low = split(jnp.where(own, dgate, 0.0))
                scattered = dot(place, high) + dot(place, low)
                out[j, :, D:] = jnp.concatenate([scattered, jnp.zeros((TOK, 128 - EXPERTS), f32)], axis=1).astype(bf16)
            return carry

        lax.fori_loop(0, 4, pair, 0)


def codes_specs():
    return [pl.BlockSpec((TOK, 128), lambda e: (0, D // 128))] * BLOCKS


def main(z, x, gy, gates, weights, codes):
    shape = jax.ShapeDtypeStruct
    hidden = shape((SHARE, SLOTS, HALF), bf16)
    back = shape((4, TOK, D + 128), bf16)
    return call(
        main_kernel, "experts", 17_000_000_000, 45_000_000,
        grid=(SHARE,),
        in_specs=[
            SCALAR, per_expert(4, PAIR, D), per_expert(4, PAIR, D), per_expert(4, PAIR, 1),
            pl.BlockSpec((2, 1536, 256), lambda e: (e, 0, 0)), *codes_specs(),
        ],
        out_specs=[per_expert(SLOTS, HALF)] * 3 + [whole(4, TOK, D + 128)] * 2,
        out_shape=[hidden, hidden, hidden, back, back],
        scratch_shapes=[
            pltpu.VMEM((SHARE, BLOCKS, CAP, D), bf16),
            pltpu.VMEM((SHARE, BLOCKS, CAP, 1), f32),
            pltpu.VMEM((BLOCKS, TOK, 128), bf16),
        ],
    )(z, x, gy, gates, weights, *codes)


def grads_kernel(x_ref, gy_ref, act_ref, dg_ref, du_ref, out_ref):
    x = x_ref[0].reshape(SLOTS, D)
    for i, grad in enumerate((dg_ref, du_ref)):
        made = dot(grad[0], x, TN).astype(bf16)
        out_ref[0, 0, i * HALF : (i + 1) * HALF] = made[:, :512]
        out_ref[0, 1, i * HALF : (i + 1) * HALF] = made[:, 512:]
    made = dot(act_ref[0], gy_ref[0].reshape(SLOTS, D), TN).astype(bf16)
    for i in range(2):
        out_ref[0, i, 512:640] = made[128 * i : 128 * i + 128, :512]
        out_ref[0, i, 640:768] = made[128 * i : 128 * i + 128, 512:]


def grads(x, gy, act, dg, du):
    return call(
        grads_kernel, "expert_grads", 8_000_000_000, 42_000_000,
        grid=(SHARE,),
        in_specs=[per_expert(4, PAIR, D)] * 2 + [per_expert(SLOTS, HALF)] * 3,
        out_specs=per_expert(2, 768, 512),
        out_shape=jax.ShapeDtypeStruct((SHARE, 2, 768, 512), bf16),
    )(x, gy, act, dg, du)


def outs_kernel(z_ref, act_ref, w_ref, *refs):
    codes_refs = refs[:8]
    own_ref, other_ref, kept, codes_kept = refs[8:]
    e = pl.program_id(0)
    z = z_ref[0]
    kept[e] = dot(act_ref[0], down_of(w_ref[...])).astype(bf16).reshape(BLOCKS, CAP, D)

    @pl.when(e == 0)
    def _():
        for b in range(BLOCKS):
            codes_kept[b] = codes_refs[b][...]

    @pl.when(e == SHARE - 1)
    def _():
        def pair(j, carry):
            for c, out in ((0, own_ref), (1, other_ref)):
                b = 2 * j + c
                place = slot_columns(codes_kept[b][:, :EXPERTS], z)
                rows = jnp.concatenate([kept[i, b] for i in range(SHARE)], axis=0)
                out[j] = dot(place, rows).astype(bf16)
            return carry

        lax.fori_loop(0, 4, pair, 0)


def outs(z, act, weights, codes):
    back = jax.ShapeDtypeStruct((4, TOK, D), bf16)
    return call(
        outs_kernel, "expert_outs", 6_000_000_000, 12_000_000,
        grid=(SHARE,),
        in_specs=[
            SCALAR, per_expert(SLOTS, HALF), pl.BlockSpec((2, 512, 256), lambda e: (e, 2, 0)), *codes_specs(),
        ],
        out_specs=[whole(4, TOK, D)] * 2,
        out_shape=[back, back],
        scratch_shapes=[pltpu.VMEM((SHARE, BLOCKS, CAP, D), bf16), pltpu.VMEM((BLOCKS, TOK, 128), bf16)],
    )(z, act, weights, *codes)


def shift(values, axis, by):
    n = 4 if axis in ("x", "z") else 2
    return lax.ppermute(values, axis, [(i, (i + by) % n) for i in range(n)])


def swap(values, axis):
    return shift(values, axis, 1)


def in_order(axis, own, other):
    first = lax.axis_index(axis) == 0
    return jnp.where(first, own, other), jnp.where(first, other, own)


def of_index(axis, zero, one):
    first = lax.axis_index(axis) == 0
    return jnp.where(first, zero, one), jnp.where(first, one, zero)


def gather_seq(values):
    pair = jnp.stack(in_order("ylo", values, swap(values, "ylo")))
    zero, one = in_order("core", pair, swap(pair, "core"))
    return jnp.stack([zero[0], one[0], zero[1], one[1]])


def scatter_seq(values):
    parts = values.astype(bf16).reshape((2, 2) + values.shape[1:])
    keep, send = of_index("core", parts[:, 0], parts[:, 1])
    pair = (keep.astype(f32) + swap(send, "core").astype(f32)).astype(bf16)
    keep, send = of_index("ylo", pair[0], pair[1])
    return keep.astype(f32) + swap(send, "ylo").astype(f32)


def gather_near(values):
    blocks = [values, shift(values, "z", 1), shift(values, "z", -1), shift(values, "z", 2)]
    return [(block, swap(block, "core")) for block in blocks]


def scatter_near(own, other):
    got = swap(other, "core")
    sums = [(own[j].astype(f32) + got[j].astype(f32)).astype(bf16) for j in range(4)]
    parts = [sums[0], shift(sums[1], "z", -1), shift(sums[2], "z", 1), shift(sums[3], "z", 2)]
    return sum(part.astype(f32) for part in parts)


def after(values, *others):
    return lax.optimization_barrier((values, *others))[0]


def on_device(
    tokens, norm1_gain, query_weight, key_weight, value_weight, output_weight, norm2_gain, router_weight,
    expert_gate, expert_up, expert_down, routes, cotangent,
):
    z = lax.axis_index("z").astype(jnp.int32).reshape(1)
    own_tokens = tokens.reshape(TOK, D)
    x_all = gather_seq(own_tokens).reshape(LENGTH, D)

    def halve(weight):
        parts = weight.reshape(TOK, 2, 2, 128)
        mine, theirs = of_index("core", parts[:, :, 0], parts[:, :, 1])
        return mine.reshape(TOK, HALF), theirs.reshape(TOK, HALF)

    gate_mine, gate_theirs = halve(expert_gate)
    up_mine, up_theirs = halve(expert_up)
    got = swap(jnp.stack([gate_theirs, up_theirs]), "core")
    down_part = expert_down.reshape(128, 4, 256).transpose(1, 0, 2).reshape(512, 256)
    expert_w = jnp.concatenate(
        [*in_order("core", gate_mine, got[0]), *in_order("core", up_mine, got[1]), down_part], axis=0
    )
    expert_w = lax.all_gather(expert_w, PLANE, axis=0).reshape(16, 1536, 256)

    query_part = query_weight.reshape(8, 4, GROUP, 2, 32).transpose(1, 0, 3, 2, 4).reshape(4, 8, 256)
    key_part = key_weight.reshape(8, 4, 2, 2, 32).transpose(1, 0, 3, 2, 4).reshape(4, 8, 128)
    value_part = value_weight.reshape(8, 4, 128).transpose(1, 0, 2)
    router_part = router_weight.reshape(8, 2, 4, 4).transpose(0, 3, 2, 1).reshape(8, EXPERTS)
    small = jnp.concatenate(
        [router_part, norm1_gain[:, None], norm2_gain[:, None], jnp.zeros((8, 94), bf16)], axis=1
    )
    packed = jnp.concatenate(
        [query_part, key_part, value_part, jnp.broadcast_to(small[None], (4, 8, 128))], axis=2
    )
    packed = jnp.broadcast_to(packed[:, None], (4, 32, 8, 640)).reshape(128, 8, 640)
    arrived = lax.all_to_all(packed, AXES, split_axis=0, concat_axis=0, tiled=True).reshape(D, 640)
    group_w = arrived[:, :512]
    router_w = arrived[:, 512:544]
    gain_one = arrived[:, 544].astype(f32).reshape(1, D)
    gain_two = arrived[:, 545].astype(f32).reshape(1, D)

    choices = routes.reshape(TOK, TOPK)
    column = jnp.arange(EXPERTS)
    expert_of = (column % 2) * 16 + (column % 8) // 2 * 4 + column // 8
    chosen = jnp.any(choices[:, :, None] == expert_of[None, None, :], axis=1)
    earlier = (jnp.arange(TOK)[None, :] < jnp.arange(TOK)[:, None]).astype(bf16)
    rank = dot(earlier, chosen.astype(bf16))
    own_codes = jnp.where(chosen, rank, -1.0).astype(bf16)
    grad_out = cotangent.reshape(TOK, D)
    gy_pairs = gather_near(jnp.concatenate([grad_out, own_codes, jnp.zeros((TOK, 96), bf16)], axis=1))
    codes = [block for pair in gy_pairs for block in pair]

    lane = jnp.arange(128) % 32
    angles = jnp.arange(LENGTH).astype(f32)[:, None] * (rope_base ** (-2.0 * lane.astype(f32) / HEAD))[None, :]
    cos, sin = jnp.cos(angles), jnp.sin(angles)
    q, k, v, mixed, lse, hidden_all = front(x_all, group_w, gain_one, cos, sin)

    output_part = after(output_weight, arrived)
    output_part = lax.all_to_all(
        jnp.broadcast_to(output_part[None], (32, 8, D)), FSDP, split_axis=0, concat_axis=0, tiled=True
    ).reshape(256, D)
    output_w = gather_seq(output_part).reshape(D, D)

    mixed = lax.all_to_all(mixed.reshape(4, TOK, 256), SEQ, split_axis=0, concat_axis=0, tiled=True)
    mixed = mixed.transpose(1, 0, 2).reshape(TOK, D)

    inputs = own_tokens.astype(f32)
    residual = inputs + dot(mixed, output_w)
    factor_two = lax.rsqrt(jnp.mean(residual * residual, axis=-1, keepdims=True) + epsilon)
    normed_two = residual * factor_two
    hidden_two = (normed_two * gain_two).astype(bf16)
    h_pairs = gather_near(hidden_two)

    gy_rows, rows = None, None
    for j in range(4):
        gy_rows = rows_of(z, j, gy_pairs[j], None, None, gy_rows)
    for j in range(4):
        rows = rows_of(z, j, h_pairs[j], gy_pairs[j], router_w, rows)
    (gy_rows,), (rows, gate_rows) = gy_rows, rows

    act, dg, du, back_own, back_other = main(z, rows, gy_rows, gate_rows, expert_w, codes)
    grad_hidden = scatter_near(back_own, back_other)
    expert_grads = grads(rows, gy_rows, act, dg, du)
    moe_own, moe_other = outs(z, act, expert_w, codes)
    layer_out = (residual + scatter_near(moe_own, moe_other)).astype(bf16).reshape(1, TOK, D)

    gates = gate_table(dot(hidden_two, router_w), own_codes.astype(f32))
    dgates = grad_hidden[:, D : D + EXPERTS]
    dlogits = (gates * (dgates - jnp.sum(gates * dgates, axis=-1, keepdims=True))).astype(bf16)
    grad_router = dot(hidden_two, dlogits, TN)
    grad_hidden = grad_hidden[:, :D] + dot(dlogits, router_w, NT)
    grad_gain_two = jnp.sum(grad_hidden * normed_two, axis=0)
    scaled = grad_hidden * gain_two
    grad_residual = grad_out.astype(f32) + factor_two * (
        scaled - normed_two * jnp.mean(scaled * normed_two, axis=-1, keepdims=True)
    )
    dz = grad_residual.astype(bf16)
    do = dot(dz, output_w, NT).astype(bf16).reshape(TOK, 4, 256).transpose(1, 0, 2)
    do = lax.all_to_all(do, SEQ, split_axis=0, concat_axis=0, tiled=True).reshape(LENGTH, 256)

    expert_grads = lax.psum_scatter(expert_grads.reshape(16 * 768, 512), PLANE, scatter_dimension=0, tiled=True)
    keep, send = of_index("core", expert_grads[:512, :256], expert_grads[:512, 256:])
    both = jnp.stack(in_order("core", keep, swap(send, "core"))).reshape(2, 2, 2, 128, TOK)
    both = both.transpose(1, 4, 2, 0, 3).reshape(2, 1, TOK, FF).astype(f32)
    grad_down = expert_grads[512:].reshape(2, 128, 512).transpose(1, 0, 2).reshape(1, 128, D).astype(f32)

    grad_output = dot(mixed, dz, TN).astype(bf16).reshape(128, 8, D)
    grad_output = lax.all_to_all(grad_output, AXES, split_axis=0, concat_axis=0, tiled=True)
    grad_output = jnp.sum(grad_output.astype(f32), axis=0)

    dqkv = back(q, k, v, do, lse, cos, sin)
    grad_group = dot(hidden_all, dqkv, TN).astype(bf16)
    partial = dot(dqkv, group_w, NT)
    x_float = x_all.astype(f32)
    normed_all = x_float * lax.rsqrt(jnp.mean(x_float * x_float, axis=-1, keepdims=True) + epsilon)
    grad_gain_one = jnp.sum(partial * normed_all, axis=0)
    grad_hidden_one = scatter_seq(partial.reshape(4, TOK, D))
    small = jnp.concatenate([grad_router, grad_gain_two[:, None], grad_gain_one[:, None]], axis=1)
    first = jnp.concatenate([grad_group, small.astype(bf16), jnp.zeros((D, 94), bf16)], axis=1)
    first = lax.all_to_all(first.reshape(128, 8, 640), AXES, split_axis=0, concat_axis=0, tiled=True)
    first = jnp.sum(first.astype(f32).reshape(4, 32, 8, 640), axis=1)
    grad_query = first[:, :, :256].reshape(4, 8, 2, GROUP, 32).transpose(1, 0, 3, 2, 4).reshape(8, D)
    grad_key = first[:, :, 256:384].reshape(4, 8, 2, 2, 32).transpose(1, 0, 3, 2, 4).reshape(8, 512)
    grad_value = first[:, :, 384:512].transpose(1, 0, 2).reshape(8, 512)
    small = jnp.sum(first[:, :, 512:], axis=0)
    grad_router = small[:, :EXPERTS].reshape(8, 4, 4, 2).transpose(0, 3, 2, 1).reshape(8, EXPERTS)

    factor_one = lax.rsqrt(jnp.mean(inputs * inputs, axis=-1, keepdims=True) + epsilon)
    normed_one = inputs * factor_one
    scaled = grad_hidden_one * gain_one
    grad_inputs = grad_residual + factor_one * (
        scaled - normed_one * jnp.mean(scaled * normed_one, axis=-1, keepdims=True)
    )
    return (
        layer_out, grad_inputs.reshape(1, TOK, D), small[:, 33], grad_query, grad_key, grad_value, grad_output,
        small[:, 32], grad_router, both[0], both[1], grad_down,
    )


def solution(mesh):
    fine = Mesh(mesh.devices.reshape(2, 2, 2, 4, 4), AXES)
    tok = P(FSDP, SEQ, None)
    row = P(AXES, None)
    vec = P(AXES)
    in_specs = (tok, vec, row, row, row, row, vec, row, tok, tok, tok, tok, tok)
    out_specs = (tok, tok, vec, row, row, row, row, vec, row, tok, tok, tok)
    return jax.shard_map(on_device, mesh=fine, in_specs=in_specs, out_specs=out_specs, check_vma=False)
```

```python
import functools

import jax
import jax.numpy as jnp
from jax import lax
from jax.experimental import pallas as pl
from jax.experimental.pallas import tpu as pltpu
from jax.sharding import Mesh
from jax.sharding import PartitionSpec as P

HEADS = 16
KV_HEADS = 8
HEAD = 64
TOPK = 8
CAP = 80
TOK = 256
D = 1024
FF = 512
EXPERTS = 32
SHARE = 8
SLOTS = SHARE * CAP
BLOCKS = 8
HALF = FF // 2
GROUP = 4
LENGTH = 1024

epsilon = 1e-06
rope_base = 10000.0

AXES = ("ylo", "core", "yhi", "x", "z")
SEQ = ("ylo", "core")
FSDP = ("yhi", "x", "z")
PLANE = ("x", "yhi", "ylo")

f32 = jnp.float32
bf16 = jnp.bfloat16

NT = (((1,), (1,)), ((), ()))
TN = (((0,), (0,)), ((), ()))
VMEM_LIMIT = 56 * 1024 * 1024


def dot(a, b, dims=(((1,), (0,)), ((), ()))):
    return lax.dot_general(a, b, dims, preferred_element_type=f32)


def iota(shape, axis):
    return lax.broadcasted_iota(jnp.int32, shape, axis)


def as_bf16(cond):
    return jnp.where(cond, 1.0, 0.0).astype(bf16)


def call(kernel, name, flops, moved, **kwargs):
    return pl.pallas_call(
        kernel,
        compiler_params=pltpu.CompilerParams(vmem_limit_bytes=VMEM_LIMIT),
        cost_estimate=pl.CostEstimate(flops=flops, bytes_accessed=moved, transcendentals=0),
        name=name,
        **kwargs,
    )


def shape(*dims, dtype=bf16):
    return jax.ShapeDtypeStruct(dims, dtype)


SCALAR = pl.BlockSpec(memory_space=pltpu.SMEM)
ANYWHERE = pl.BlockSpec(memory_space=pl.ANY)
VECTOR = pl.BlockSpec(memory_space=pltpu.VMEM)


def column_of(row):
    n = row.shape[1]
    step = min(n, 128)
    same = iota((step, step), 0) == iota((step, step), 1)
    parts = [jnp.sum(jnp.where(same, row[:, i : i + step], 0.0), axis=1, keepdims=True) for i in range(0, n, step)]
    return jnp.concatenate(parts, axis=0) if len(parts) > 1 else parts[0]


def row_of(column):
    n = column.shape[0]
    same = iota((128, 128), 0) == iota((128, 128), 1)
    parts = [jnp.sum(jnp.where(same, column[i : i + 128], 0.0), axis=0, keepdims=True) for i in range(0, n, 128)]
    return jnp.concatenate(parts, axis=1)


def codes_kernel(routes_ref, gy_ref, gy_out_ref):
    routes = routes_ref[...]
    expert = iota((TOK, EXPERTS), 1)
    chosen = jnp.zeros((TOK, EXPERTS), jnp.bool_)
    for i in range(TOPK):
        chosen = chosen | (routes[:, i : i + 1] == expert)
    earlier = as_bf16(iota((TOK, TOK), 1) < iota((TOK, TOK), 0))
    codes = jnp.where(chosen, dot(earlier, as_bf16(chosen)), -1.0)
    gy_out_ref[:, :D] = gy_ref[...]
    gy_out_ref[:, D:] = jnp.concatenate([codes, jnp.zeros((TOK, 128 - EXPERTS), f32)], axis=1).astype(bf16)


def with_codes(routes, gy):
    return call(
        codes_kernel, "codes", 50_000_000, 1_500_000, in_specs=[VECTOR] * 2, out_shape=shape(TOK, D + 128)
    )(routes, gy)


def pack_kernel(
    place_ref, query_ref, key_ref, value_ref, router_ref, one_ref, two_ref, gate_ref, up_ref,
    packed_ref, keep_ref, send_ref,
):
    core = place_ref[1]
    lane = iota((8, 128), 1)
    small = jnp.concatenate([router_ref[...].astype(f32), jnp.zeros((8, 96), f32)], axis=1)
    small = jnp.where(lane == 32, column_of(one_ref[...].astype(f32)), small)
    small = jnp.where(lane == 33, column_of(two_ref[...].astype(f32)), small).astype(bf16)
    for s in range(4):
        part = jnp.concatenate(
            [
                query_ref[:, 256 * s : 256 * s + 256],
                key_ref[:, 128 * s : 128 * s + 128],
                value_ref[:, 128 * s : 128 * s + 128],
                small,
            ],
            axis=1,
        )
        for f in range(32):
            packed_ref[32 * s + f] = part
    for i, ref in enumerate((gate_ref, up_ref)):
        for j in range(2):
            keep_ref[i, :, 128 * j : 128 * j + 128] = ref[:, pl.ds(256 * j + 128 * core, 128)]
            send_ref[i, :, 128 * j : 128 * j + 128] = ref[:, pl.ds(256 * j + 128 * (1 - core), 128)]


def pack(place, *args):
    return call(
        pack_kernel, "pack", 100_000_000, 4_000_000,
        in_specs=[SCALAR] + [VECTOR] * len(args),
        out_shape=(shape(128, 8, 640), shape(2, TOK, HALF), shape(2, TOK, HALF)),
    )(place, *args)


def assemble_kernel(place_ref, keep_ref, got_ref, down_ref, out_ref):
    core = place_ref[1]
    for i in range(2):
        out_ref[pl.ds(512 * i + 256 * core, 256)] = keep_ref[i]
        out_ref[pl.ds(512 * i + 256 * (1 - core), 256)] = got_ref[i]
    for j in range(4):
        out_ref[1024 + 128 * j : 1152 + 128 * j] = down_ref[:, 256 * j : 256 * j + 256]


def assemble(place, keep, got, down):
    return call(
        assemble_kernel, "assemble", 1_000_000, 2_000_000,
        in_specs=[SCALAR] + [VECTOR] * 3, out_shape=shape(1536, 256),
    )(place, keep, got, down)


def head_lanes_rope(head):
    lane = iota((1, 256), 1) % 128
    return (lane >= 32 * head) & (lane < 32 * head + 32)


def head_lanes(head):
    lane = iota((1, 256), 1)
    return (lane >= 64 * head) & (lane < 64 * head + 64)


def spread_queries():
    row, col = iota((256, 256), 0), iota((256, 256), 1)
    return row == ((col % 128) // 32) * 64 + (col // 128) * 32 + col % 32


def spread_keys():
    row, col = iota((128, 256), 0), iota((128, 256), 1)
    return row == ((col % 128) // 64) * 64 + (col // 128) * 32 + col % 32, (col % 64) < 32


def spread_values():
    row, col = iota((128, 256), 0), iota((128, 256), 1)
    return row == (col // 128) * 64 + col % 64, (col % 128) < 64


def positions(place_ref):
    ylo, core = place_ref[0], place_ref[1]
    return [(y, c, 2 * y + c) for c in (core, 1 - core) for y in (ylo, 1 - ylo)]


def normed(x):
    return x * lax.rsqrt(jnp.mean(x * x, axis=-1, keepdims=True) + epsilon)


def front_kernel(
    place_ref, x0_ref, x1_ref, x2_ref, x3_ref, w_ref, cos_ref, sin_ref,
    q_ref, k_ref, v_ref, o0_ref, o1_ref, o2_ref, o3_ref, lse_ref, h_ref, gains_ref, o_ref,
):
    gain = row_of(w_ref[:, 512:640].astype(f32)[:, 32:33])
    gains_ref[0:1] = gain
    gains_ref[1:2] = row_of(w_ref[:, 512:640].astype(f32)[:, 33:34])
    wq = dot(w_ref[:, :256], as_bf16(spread_queries())).astype(bf16)
    wk = dot(w_ref[:, 256:384], as_bf16(spread_keys()[0])).astype(bf16)
    wv = dot(w_ref[:, 384:512], as_bf16(spread_values()[0])).astype(bf16)
    for (_, _, at), x_ref in zip(positions(place_ref), (x0_ref, x1_ref, x2_ref, x3_ref)):
        rows = pl.ds(pl.multiple_of(256 * at, 256), 256)
        h = (normed(x_ref[...].astype(f32)) * gain).astype(bf16)
        h_ref[rows] = h
        c, s = cos_ref[rows], sin_ref[rows]
        for w, out in ((wq, q_ref), (wk, k_ref)):
            pre = dot(h, w)
            a, b = pre[:, :128], pre[:, 128:]
            out[rows] = jnp.concatenate([a * c - b * s, b * c + a * s], axis=1).astype(bf16)
        v_ref[rows] = dot(h, wv).astype(bf16)
    for i in range(4):
        rows = slice(256 * i, 256 * i + 256)
        n = 256 * (i + 1)
        seen = iota((256, n), 1) <= iota((256, n), 0) + 256 * i
        mixed = jnp.zeros((256, 256), f32)
        logs = jnp.zeros((256, 128), f32)
        for head in range(GROUP):
            q = q_ref[rows] * as_bf16(head_lanes_rope(head))
            scores = jnp.where(seen, dot(q, k_ref[:n], NT) * HEAD**-0.5, -1e30)
            peak = jnp.max(scores, axis=-1, keepdims=True)
            e = jnp.exp(scores - peak)
            total = jnp.sum(e, axis=-1, keepdims=True)
            probs = (e * (1.0 / total)).astype(bf16)
            mixed = mixed + dot(probs, v_ref[:n] * as_bf16(head_lanes(head)))
            logs = jnp.where(iota((256, 128), 1) == head, peak + jnp.log(total), logs)
        o_ref[i] = mixed.astype(bf16)
        lse_ref[rows] = logs
    for (_, _, at), out in zip(positions(place_ref), (o0_ref, o1_ref, o2_ref, o3_ref)):
        out[...] = o_ref[at]


def front(place, blocks, w, cos, sin):
    return call(
        front_kernel, "front", 8_000_000_000, 10_000_000,
        in_specs=[SCALAR] + [VECTOR] * 7,
        out_shape=(
            shape(LENGTH, 256), shape(LENGTH, 256), shape(LENGTH, 256), *[shape(TOK, 256)] * 4,
            shape(LENGTH, 128, dtype=f32), shape(LENGTH, D), shape(8, D, dtype=f32),
        ),
        scratch_shapes=[pltpu.VMEM((4, TOK, 256), bf16)],
    )(place, *blocks, w, cos, sin)


def output_blocks(own_ref, other_ref):
    return [ref[:, D * i : D * i + D] for ref in (own_ref, other_ref) for i in range(2)]


def mid_kernel(x_ref, m0_ref, m1_ref, m2_ref, m3_ref, own_ref, other_ref, gains_ref, residual_ref, h_ref):
    total = x_ref[...].astype(f32)
    for mixed_ref, w in zip((m0_ref, m1_ref, m2_ref, m3_ref), output_blocks(own_ref, other_ref)):
        total = total + dot(mixed_ref[...], w)
    residual_ref[...] = total
    h_ref[...] = (normed(total) * gains_ref[1:2]).astype(bf16)


def mid(x, mixed, own, other, gains):
    return call(
        mid_kernel, "mid", 1_000_000_000, 5_000_000,
        in_specs=[VECTOR] * 8,
        out_shape=(shape(TOK, D, dtype=f32), shape(TOK, D)),
    )(x, *mixed, own, other, gains)


def turn_kernel(
    place_ref, part0_ref, part1_ref, part2_ref, part3_ref, gy_ref, residual_ref, small_ref, gains_ref,
    m0_ref, m1_ref, m2_ref, m3_ref, own_ref, other_ref,
    do0_ref, do1_ref, do2_ref, do3_ref, grad_ref, keep_ref, send_ref, sums_ref,
):
    parts = (part0_ref, part1_ref, part2_ref, part3_ref)
    summed = sum(part[...].astype(f32) for part in parts)
    residual = residual_ref[...]
    factor = lax.rsqrt(jnp.mean(residual * residual, axis=-1, keepdims=True) + epsilon)
    normal = residual * factor
    gain = gains_ref[1:2]
    h = (normal * gain).astype(bf16)
    router = small_ref[:, 512 : 512 + EXPERTS]
    table = gate_table(dot(h, router), gy_ref[:, D:].astype(f32)[:, :EXPERTS])
    dgates = summed[:, D : D + EXPERTS]
    dlogits = (table * (dgates - jnp.sum(table * dgates, axis=-1, keepdims=True))).astype(bf16)
    dh = summed[:, :D] + dot(dlogits, router, NT)
    grad_gain = column_of(jnp.sum(dh * normal, axis=0, keepdims=True))
    grad_router = dot(h, dlogits, TN)
    sums = jnp.concatenate([grad_router, jnp.zeros((D, 128 - EXPERTS), f32)], axis=1)
    sums_ref[...] = jnp.where(iota((D, 128), 1) == 33, grad_gain, sums)
    scaled = dh * gain
    grad = gy_ref[:, :D].astype(f32) + factor * (scaled - normal * jnp.mean(scaled * normal, axis=-1, keepdims=True))
    grad_ref[...] = grad
    dz = grad.astype(bf16)
    mixed_refs, do_refs = (m0_ref, m1_ref, m2_ref, m3_ref), (do0_ref, do1_ref, do2_ref, do3_ref)
    for i, ((y, _, _), w) in enumerate(zip(positions(place_ref), output_blocks(own_ref, other_ref))):
        do_refs[i][...] = dot(dz, w, NT).astype(bf16)
        out = keep_ref if i < 2 else send_ref
        out[y] = dot(mixed_refs[i][...], dz, TN).astype(bf16)


def turn_back(place, parts, gy, residual, small, gains, mixed, own, other):
    pair = shape(2, TOK, D)
    return call(
        turn_kernel, "turn", 2_000_000_000, 10_000_000,
        in_specs=[SCALAR] + [VECTOR] * 14,
        out_shape=(*[shape(TOK, 256)] * 4, shape(TOK, D, dtype=f32), pair, pair, shape(D, 128, dtype=f32)),
    )(place, *parts, gy, residual, small, gains, *mixed, own, other)


def back_kernel(
    place_ref, q_ref, k_ref, v_ref, do0_ref, do1_ref, do2_ref, do3_ref, lse_ref, cos_ref, sin_ref, w_ref,
    x0_ref, x1_ref, x2_ref, x3_ref, out_ref, keep_ref, send_ref, gain_ref, do_ref, dk_ref, dv_ref,
):
    for (_, _, at), ref in zip(positions(place_ref), (do0_ref, do1_ref, do2_ref, do3_ref)):
        do_ref[at] = ref[...]
    dk_ref[...] = jnp.zeros_like(dk_ref)
    dv_ref[...] = jnp.zeros_like(dv_ref)
    scale = HEAD**-0.5
    place_queries = as_bf16(spread_queries())
    for i in range(4):
        rows = slice(256 * i, 256 * i + 256)
        n = 256 * (i + 1)
        seen = iota((256, n), 1) <= iota((256, n), 0) + 256 * i
        dq = jnp.zeros((256, 256), f32)
        for head in range(GROUP):
            lanes = head_lanes_rope(head)
            q = q_ref[rows] * as_bf16(lanes)
            do = do_ref[i] * as_bf16(head_lanes(head))
            scores = dot(q, k_ref[:n], NT) * scale - lse_ref[rows, head : head + 1]
            probs = jnp.where(seen, jnp.exp(jnp.where(seen, scores, 0.0)), 0.0)
            dprobs = dot(do, v_ref[:n], NT)
            row_dot = jnp.sum(probs * dprobs, axis=-1, keepdims=True)
            ds = (probs * (dprobs - row_dot)).astype(bf16)
            dq = dq + jnp.where(lanes, dot(ds, k_ref[:n]), 0.0)
            dk_ref[:n] += dot(ds, q, TN)
            dv_ref[:n] += dot(probs.astype(bf16), do, TN)
        c, s = cos_ref[rows], sin_ref[rows]
        a, b = dq[:, :128] * scale, dq[:, 128:] * scale
        dq = jnp.concatenate([a * c + b * s, b * c - a * s], axis=1).astype(bf16)
        out_ref[rows, :256] = dot(dq, place_queries, NT).astype(bf16)
    keep_keys, first_key = spread_keys()
    keep_values, first_value = spread_values()
    pick_keys = as_bf16(keep_keys & first_key)
    pick_values = as_bf16(keep_values & first_value)
    for i in range(4):
        rows = slice(256 * i, 256 * i + 256)
        c, s = cos_ref[rows], sin_ref[rows]
        a, b = dk_ref[rows, :128] * scale, dk_ref[rows, 128:] * scale
        a, b = a * c + b * s, b * c - a * s
        a, b = a + pltpu.roll(a, 96, 1), b + pltpu.roll(b, 96, 1)
        out_ref[rows, 256:384] = dot(jnp.concatenate([a, b], axis=1).astype(bf16), pick_keys, NT).astype(bf16)
        a, b = dv_ref[rows, :128], dv_ref[rows, 128:]
        a, b = a + pltpu.roll(a, 64, 1), b + pltpu.roll(b, 64, 1)
        out_ref[rows, 384:512] = dot(jnp.concatenate([a, b], axis=1).astype(bf16), pick_values, NT).astype(bf16)
    w = w_ref[:, :512]
    grad_gain = jnp.zeros((1, D), f32)
    for i, ((y, _, at), x_ref) in enumerate(zip(positions(place_ref), (x0_ref, x1_ref, x2_ref, x3_ref))):
        partial = dot(out_ref[pl.ds(pl.multiple_of(256 * at, 256), 256)], w, NT)
        grad_gain = grad_gain + jnp.sum(partial * normed(x_ref[...].astype(f32)), axis=0, keepdims=True)
        out = keep_ref if i < 2 else send_ref
        out[y] = partial.astype(bf16)
    gain_ref[...] = jnp.broadcast_to(grad_gain, (8, D))


def back(place, q, k, v, do, lse, cos, sin, w, blocks):
    pair = shape(2, TOK, D)
    return call(
        back_kernel, "back", 20_000_000_000, 16_000_000,
        in_specs=[SCALAR] + [VECTOR] * 15,
        out_shape=(shape(LENGTH, 512), pair, pair, shape(8, D, dtype=f32)),
        scratch_shapes=[
            pltpu.VMEM((4, TOK, 256), bf16), pltpu.VMEM((LENGTH, 256), f32), pltpu.VMEM((LENGTH, 256), f32),
        ],
    )(place, q, k, v, *do, lse, cos, sin, w, *blocks)


def projections_kernel(h_ref, dqkv_ref, sums_ref, gain_ref, first_ref):
    first_ref[:, :512] = dot(h_ref[...], dqkv_ref[...], TN).astype(bf16)
    small = jnp.where(iota((D, 128), 1) == 32, column_of(gain_ref[0:1]), sums_ref[...])
    first_ref[:, 512:] = small.astype(bf16)


def projections(h, dqkv, sums, gain):
    return call(
        projections_kernel, "projections", 1_500_000_000, 5_000_000, in_specs=[VECTOR] * 4, out_shape=shape(D, 640)
    )(h, dqkv, sums, gain)


def own_slots(expert, slot, z):
    start = ((expert % 16) // 4 * 2 + expert // 16) * CAP
    own = (expert % 4 == z) & (slot >= start) & (slot < start + CAP)
    return own, jnp.where(own, slot - start, 0)


def slot_tables(z, spread, start):
    own, place = own_slots(iota((EXPERTS, SLOTS), 0), iota((EXPERTS, SLOTS), 1), z)
    spread[...] = as_bf16(own)
    start[...] = jnp.sum(place, axis=0, keepdims=True).astype(f32)


SLOT_TABLES = [pltpu.VMEM((EXPERTS, SLOTS), bf16), pltpu.VMEM((1, SLOTS), f32)]


def gate_table(logits, codes):
    routed = codes >= 0
    logits = jnp.where(routed, logits, -1e30)
    e = jnp.where(routed, jnp.exp(logits - jnp.max(logits, axis=-1, keepdims=True)), 0.0)
    return e / jnp.sum(e, axis=-1, keepdims=True)


def split(values):
    high = values.astype(bf16)
    return high, (values - high.astype(f32)).astype(bf16)


def whole(*shape):
    return pl.BlockSpec(shape, lambda e: (0,) * len(shape))


def per_expert(*shape):
    return pl.BlockSpec((1,) + shape, lambda e: (e,) + (0,) * len(shape))


def rows_kernel(n, with_gates, z_ref, *refs):
    i = pl.program_id(0)
    z = z_ref[0]
    values_refs, refs = refs[:n], refs[n:]
    if with_gates:
        codes_refs, router_ref, refs = refs[:n], refs[n], refs[n + 1 :]
        rows_ref, gates_ref, turn_ref, values, codes, own, start = refs[-7:]
    else:
        rows_ref, turn_ref, values, codes, own, start = refs[-6:]
    for b in range(n):

        @pl.when(i == b)
        def _():
            values[...] = values_refs[b][:, :D]
            codes[...] = codes_refs[b][...] if with_gates else values_refs[b][:, D:]

    @pl.when(i == 0)
    def _():
        turn_ref[...] = jnp.zeros_like(turn_ref)
        mine, offset = own_slots(iota((SLOTS, EXPERTS), 1), iota((SLOTS, EXPERTS), 0), z)
        own[...] = as_bf16(mine)
        start[...] = jnp.sum(offset, axis=1, keepdims=True).astype(f32)

    slots = codes[:, :EXPERTS]
    place = as_bf16(dot(own[...], slots, NT) == start[...])
    rows_ref[:, 0] = dot(place, values[...]).astype(bf16).reshape(SHARE, CAP, D)
    if with_gates:
        table = gate_table(dot(values[...], router_ref[:, :EXPERTS]), slots.astype(f32))
        high, low = split(table)
        both = dot(place, high) + dot(place, low)
        gate = jnp.sum(both * own[...].astype(f32), axis=1, keepdims=True)
        gates_ref[:, 0] = gate.reshape(SHARE, CAP, 1)


def rows_of(z, first, blocks, codes, router, kept, turn):
    n, with_gates = len(blocks), router is not None
    args, specs = [z, *blocks], [SCALAR] + [whole(TOK, blocks[0].shape[1])] * n
    if with_gates:
        args += [*codes, router]
        specs += [pl.BlockSpec((TOK, 128), lambda e: (0, D // 128))] * n + [pl.BlockSpec((D, 128), lambda e: (0, 4))]
    args.append(turn)
    specs.append(ANYWHERE)
    widths = [(D, bf16)] + ([(1, f32)] if with_gates else [])
    out_specs = [pl.BlockSpec((SHARE, 1, CAP, w), lambda e: (0, first + e, 0, 0)) for w, _ in widths]
    out_shape = [shape(SHARE, BLOCKS, CAP, w, dtype=t) for w, t in widths]
    out_specs.append(whole(8, 128))
    out_shape.append(shape(8, 128, dtype=f32))
    aliases = {}
    if kept is not None:
        aliases = {len(args) + i: i for i in range(len(kept))}
        args += kept
        specs += [ANYWHERE] * len(kept)
    *kept, turn = call(
        functools.partial(rows_kernel, n, with_gates), "rows", n * 750_000_000, n * 2_000_000,
        grid=(n,), in_specs=specs, out_specs=out_specs, out_shape=out_shape, input_output_aliases=aliases,
        scratch_shapes=[
            pltpu.VMEM((TOK, D), bf16), pltpu.VMEM((TOK, 128), bf16), pltpu.VMEM((SLOTS, EXPERTS), bf16),
            pltpu.VMEM((SLOTS, 1), f32),
        ],
    )(*args)
    return kept, turn


def down_of(parts):
    return jnp.concatenate(
        [
            jnp.concatenate([parts[0, 128 * j : 128 * j + 128], parts[1, 128 * j : 128 * j + 128]], axis=0)
            for j in range(4)
        ],
        axis=1,
    )


def codes_specs():
    return [pl.BlockSpec((TOK, 128), lambda e: (0, D // 128))] * BLOCKS


PARTS = 2


def main_kernel(z_ref, x_ref, gy_ref, gate_ref, w_ref, *refs):
    codes_refs = refs[:8]
    act_ref, out_ref, own_ref, other_ref, kept, dgates, hidden, codes_kept, spread, start, mine = refs[8:]
    e = pl.program_id(0)

    @pl.when(e == 0)
    def _():
        for b in range(BLOCKS):
            codes_kept[b] = codes_refs[b][...]
        slot_tables(z_ref[0], spread, start)
        own, _ = own_slots(iota((SLOTS, EXPERTS), 1), iota((SLOTS, EXPERTS), 0), z_ref[0])
        mine[...] = own.astype(f32)

    down_w = down_of(w_ref[:, 1024:])
    gate_w = w_ref[:, :512].reshape(D, HALF)
    up_w = w_ref[:, 512:1024].reshape(D, HALF)
    both_w = jnp.concatenate([gate_w, up_w], axis=1)
    step = BLOCKS // PARTS
    for i in range(PARTS):
        blocks, rows = slice(step * i, step * i + step), slice(step * i * CAP, step * (i + 1) * CAP)
        x = x_ref[0, blocks].reshape(step * CAP, D)
        gate = gate_ref[0, blocks].reshape(step * CAP, 1)
        da = dot(gy_ref[0, blocks].reshape(step * CAP, D), down_w, NT)
        g = dot(x, gate_w)
        u = dot(x, up_w)
        s = jax.nn.sigmoid(g)
        silu = g * s
        act = silu * u
        dgates[blocks, e] = jnp.sum(act * da, axis=1, keepdims=True).reshape(step, CAP, 1)
        act_ref[0, rows] = (act * gate).astype(bf16)
        da = da * gate
        hidden[rows, :HALF] = (da * u * (s + silu * (1.0 - s))).astype(bf16)
        hidden[rows, HALF:] = (da * silu).astype(bf16)
        kept[blocks, e] = dot(hidden[rows], both_w, NT).astype(bf16).reshape(step, CAP, D)
    made = dot(hidden[...], x_ref[0].reshape(SLOTS, D), TN).astype(bf16)
    for i in range(2):
        out_ref[0, i, :512] = made[:, 512 * i : 512 * i + 512]
    made = dot(act_ref[0], gy_ref[0].reshape(SLOTS, D), TN).astype(bf16)
    for i in range(2):
        out_ref[0, i, 512:640] = made[128 * i : 128 * i + 128, :512]
        out_ref[0, i, 640:768] = made[128 * i : 128 * i + 128, 512:]

    @pl.when(e == SHARE - 1)
    def _():
        def pair(j, carry):
            for c, out in ((0, own_ref), (1, other_ref)):
                b = 2 * j + c
                place = as_bf16(dot(codes_kept[b][:, :EXPERTS], spread[...]) == start[...])
                out[j, :, :D] = dot(place, kept[b].reshape(SLOTS, D)).astype(bf16)
                high, low = split(mine[...] * dgates[b].reshape(SLOTS, 1))
                scattered = dot(place, high) + dot(place, low)
                out[j, :, D:] = jnp.concatenate([scattered, jnp.zeros((TOK, 128 - EXPERTS), f32)], axis=1).astype(bf16)
            return carry

        lax.fori_loop(0, 4, pair, 0)


def main(z, x, gy, gates, weights, codes):
    back = shape(4, TOK, D + 128)
    return call(
        main_kernel, "experts", 25_000_000_000, 60_000_000,
        grid=(SHARE,),
        in_specs=[
            SCALAR, per_expert(BLOCKS, CAP, D), per_expert(BLOCKS, CAP, D), per_expert(BLOCKS, CAP, 1),
            pl.BlockSpec((2, 1536, 256), lambda e: (e, 0, 0)), *codes_specs(),
        ],
        out_specs=[
            per_expert(SLOTS, HALF), per_expert(2, 768, 512), whole(4, TOK, D + 128), whole(4, TOK, D + 128),
        ],
        out_shape=[shape(SHARE, SLOTS, HALF), shape(SHARE, 2, 768, 512), back, back],
        scratch_shapes=[
            pltpu.VMEM((BLOCKS, SHARE, CAP, D), bf16),
            pltpu.VMEM((BLOCKS, SHARE, CAP, 1), f32),
            pltpu.VMEM((SLOTS, 2 * HALF), bf16),
            pltpu.VMEM((BLOCKS, TOK, 128), bf16),
            *SLOT_TABLES,
            pltpu.VMEM((SLOTS, EXPERTS), f32),
        ],
    )(z, x, gy, gates, weights, *codes)


def outs_kernel(z_ref, act_ref, w_ref, *refs):
    codes_refs = refs[:8]
    own_ref, other_ref, kept, codes_kept, spread, start = refs[8:]
    e = pl.program_id(0)
    kept[:, e] = dot(act_ref[0], down_of(w_ref[...])).astype(bf16).reshape(BLOCKS, CAP, D)

    @pl.when(e == 0)
    def _():
        for b in range(BLOCKS):
            codes_kept[b] = codes_refs[b][...]
        slot_tables(z_ref[0], spread, start)

    @pl.when(e == SHARE - 1)
    def _():
        def pair(j, carry):
            for c, out in ((0, own_ref), (1, other_ref)):
                b = 2 * j + c
                place = as_bf16(dot(codes_kept[b][:, :EXPERTS], spread[...]) == start[...])
                out[j] = dot(place, kept[b].reshape(SLOTS, D)).astype(bf16)
            return carry

        lax.fori_loop(0, 4, pair, 0)


def outs(z, act, weights, codes):
    back = jax.ShapeDtypeStruct((4, TOK, D), bf16)
    return call(
        outs_kernel, "expert_outs", 6_000_000_000, 12_000_000,
        grid=(SHARE,),
        in_specs=[
            SCALAR, per_expert(SLOTS, HALF), pl.BlockSpec((2, 512, 256), lambda e: (e, 2, 0)), *codes_specs(),
        ],
        out_specs=[whole(4, TOK, D)] * 2,
        out_shape=[back, back],
        scratch_shapes=[
            pltpu.VMEM((BLOCKS, SHARE, CAP, D), bf16), pltpu.VMEM((BLOCKS, TOK, 128), bf16), *SLOT_TABLES,
        ],
    )(z, act, weights, *codes)


def finish_kernel(place_ref, mine_ref, got_ref, gate_ref, up_ref, down_ref):
    core = place_ref[1]
    for i, out in enumerate((gate_ref, up_ref)):
        for j in range(2):
            rows = slice(256 * i + 128 * j, 256 * i + 128 * j + 128)
            keep = mine_ref[rows, pl.ds(pl.multiple_of(256 * core, 256), 256)].astype(f32)
            out[:, pl.ds(pl.multiple_of(256 * j + 128 * core, 128), 128)] = keep.T
            got = got_ref[rows].astype(f32)
            out[:, pl.ds(pl.multiple_of(256 * j + 128 * (1 - core), 128), 128)] = got.T
    for j in range(2):
        down_ref[:, 512 * j : 512 * j + 512] = mine_ref[512 + 128 * j : 640 + 128 * j].astype(f32)


def finish(place, mine, got):
    return call(
        finish_kernel, "finish", 1_000_000, 4_000_000,
        in_specs=[SCALAR, VECTOR, VECTOR],
        out_shape=(shape(TOK, FF, dtype=f32), shape(TOK, FF, dtype=f32), shape(128, D, dtype=f32)),
    )(place, mine, got)


def shift(values, axis, by):
    n = 4 if axis in ("x", "z") else 2
    return lax.ppermute(values, axis, [(i, (i + by) % n) for i in range(n)])


def swap(values, axis):
    return shift(values, axis, 1)


def gather_z(values):
    return [values, shift(values, "z", 1), shift(values, "z", -1), shift(values, "z", 2)]


def with_core(blocks):
    return [(block, swap(block, "core")) for block in blocks]


def exchange_seq(own, across, beside, both):
    return [own, swap(across, "ylo"), swap(beside, "core"), swap(swap(both, "ylo"), "core")]


def core_sums(own, other):
    got = swap(other, "core")
    return [(own[j].astype(f32) + got[j].astype(f32)).astype(bf16) for j in range(4)]


def scatter_z(sums):
    return [sums[0], shift(sums[1], "z", -1), shift(sums[2], "z", 1), shift(sums[3], "z", 2)]


def fence(*values):
    return lax.optimization_barrier(values)


def on_device(
    tokens, norm1_gain, query_weight, key_weight, value_weight, output_weight, norm2_gain, router_weight,
    expert_gate, expert_up, expert_down, routes, cotangent,
):
    ylo, core = lax.axis_index("ylo"), lax.axis_index("core")
    z = lax.axis_index("z").astype(jnp.int32).reshape(1)
    place = jnp.stack([ylo, core]).astype(jnp.int32)

    own = tokens.reshape(TOK, D)
    across = swap(own, "ylo")
    gy_own = with_codes(routes.reshape(TOK, TOPK), cotangent.reshape(TOK, D))
    gy_blocks = gather_z(gy_own)

    packed, keep, send = pack(
        place, query_weight, key_weight, value_weight, router_weight, norm1_gain.reshape(1, 8), norm2_gain.reshape(1, 8),
        expert_gate.reshape(TOK, FF), expert_up.reshape(TOK, FF),
    )

    arrived = lax.all_to_all(packed, AXES, split_axis=0, concat_axis=0, tiled=True).reshape(D, 640)
    beside = swap(own, "core")

    expert_w = assemble(place, keep, swap(send, "core"), expert_down.reshape(128, D))
    expert_w, arrived, across, beside = fence(expert_w, arrived, across, beside)
    expert_w = lax.all_gather(expert_w, PLANE, axis=0).reshape(16, 1536, 256)

    lane = jnp.arange(128) % 32
    angles = jnp.arange(LENGTH).astype(f32)[:, None] * (rope_base ** (-2.0 * lane.astype(f32) / HEAD))[None, :]
    cos, sin = fence(jnp.cos(angles), jnp.sin(angles))
    blocks = [own, across, beside, swap(across, "core")]
    q, k, v, *mixed, lse, hidden_all, gains = front(place, blocks, arrived, cos, sin)

    output_rows = jnp.concatenate([output_weight, swap(output_weight, "ylo")], axis=1)
    output_rows, _ = fence(output_rows, arrived)
    output_own = lax.all_to_all(
        jnp.broadcast_to(output_rows[None], (32, 8, 2 * D)), FSDP, split_axis=0, concat_axis=0, tiled=True
    ).reshape(TOK, 2 * D)

    mixed = exchange_seq(*mixed)
    output_own, *rest = fence(output_own, *mixed, *gy_blocks)
    mixed, gy_blocks = rest[:4], rest[4:]
    output_other = swap(output_own, "core")
    gy_blocks = [block for pair in with_core(gy_blocks) for block in pair]
    residual, hidden_two = mid(own, mixed, output_own, output_other, gains)

    h_blocks = gather_z(hidden_two)
    turn, _ = fence(jnp.zeros((8, 128), f32), hidden_two)
    gy_rows, turn = rows_of(z, 0, gy_blocks, None, None, None, turn)
    rows, turn = rows_of(z, 0, (hidden_two, swap(hidden_two, "core")), gy_blocks[:2], arrived, None, turn)
    *h_blocks, turn = fence(*h_blocks, turn)
    h_blocks = [block for pair in with_core(h_blocks[1:]) for block in pair]
    rows, turn = rows_of(z, 2, h_blocks, gy_blocks[2:], arrived, rows, turn)
    (gy_rows,), (rows, gate_rows) = gy_rows, rows

    act, expert_grads, back_own, back_other = main(z, rows, gy_rows, gate_rows, expert_w, gy_blocks)
    sums = core_sums(back_own, back_other)
    parts = scatter_z(sums)
    moe_act, *_ = fence(act, *sums)
    moe_own, moe_other = outs(z, moe_act, expert_w, gy_blocks)
    expert_grads = lax.psum_scatter(expert_grads.reshape(16 * 768, 512), PLANE, scatter_dimension=0, tiled=True)

    moe_sums = core_sums(moe_own, moe_other)
    *do, grad_residual, keep, send, small = turn_back(
        place, parts, gy_own, residual, arrived, gains, mixed, output_own, output_other
    )

    do = exchange_seq(*do)
    grad_output_sum = (keep.astype(f32) + swap(send, "core").astype(f32)).astype(bf16).reshape(64, 8, D)
    grad_output_sum, *rest = fence(grad_output_sum, *moe_sums, *do)
    moe_sums, do = rest[:4], rest[4:]
    moe_near = [shift(moe_sums[1], "z", -1), shift(moe_sums[2], "z", 1)]
    grad_output = lax.all_to_all(grad_output_sum, ("ylo",) + FSDP, split_axis=0, concat_axis=0, tiled=True)
    dqkv, keep, send, gain = back(place, q, k, v, do, lse, cos, sin, arrived, blocks)
    dqkv, keep, send, own, grad_output, *moe_near = fence(dqkv, keep, send, own, grad_output, *moe_near)
    first = projections(hidden_all, dqkv, small, gain)

    away = jnp.where(core == 0, expert_grads[:512, 256:], expert_grads[:512, :256])
    finished = finish(place, expert_grads, swap(away, "core"))

    pair = (keep.astype(f32) + swap(send, "core").astype(f32)).astype(bf16)
    kept = jnp.where(ylo == 0, pair[0], pair[1])
    got = swap(jnp.where(ylo == 0, pair[1], pair[0]), "ylo")
    got, moe_far, grad_gate, grad_up, grad_down = fence(got, shift(moe_sums[3], "z", 2), *finished)
    grad_hidden_one = kept.astype(f32) + got.astype(f32)
    first = lax.all_to_all(first.reshape(128, 8, 640), AXES, split_axis=0, concat_axis=0, tiled=True)
    grad_output = jnp.sum(grad_output.astype(f32), axis=0)
    layer_out = sum(part.astype(f32) for part in (moe_sums[0], *moe_near, moe_far))
    layer_out = (residual + layer_out).astype(bf16).reshape(1, TOK, D)
    first = jnp.sum(first.astype(f32).reshape(4, 32, 8, 640), axis=1)
    grad_query = first[:, :, :256].transpose(1, 0, 2).reshape(8, D)
    grad_key = first[:, :, 256:384].transpose(1, 0, 2).reshape(8, 512)
    grad_value = first[:, :, 384:512].transpose(1, 0, 2).reshape(8, 512)
    small = jnp.sum(first[:, :, 512:], axis=0)

    inputs = own.astype(f32)
    factor_one = lax.rsqrt(jnp.mean(inputs * inputs, axis=-1, keepdims=True) + epsilon)
    normed_one = inputs * factor_one
    scaled = grad_hidden_one * gains[0:1]
    grad_inputs = grad_residual + factor_one * (
        scaled - normed_one * jnp.mean(scaled * normed_one, axis=-1, keepdims=True)
    )

    return (
        layer_out, grad_inputs.reshape(1, TOK, D), small[:, 32], grad_query, grad_key, grad_value, grad_output,
        small[:, 33], small[:, :EXPERTS], grad_gate.reshape(1, TOK, FF), grad_up.reshape(1, TOK, FF),
        grad_down.reshape(1, 128, D),
    )


def solution(mesh):
    fine = Mesh(mesh.devices.reshape(2, 2, 2, 4, 4), AXES)
    tok = P(FSDP, SEQ, None)
    row = P(AXES, None)
    vec = P(AXES)
    in_specs = (tok, vec, row, row, row, row, vec, row, tok, tok, tok, tok, tok)
    out_specs = (tok, tok, vec, row, row, row, row, vec, row, tok, tok, tok)
    return jax.shard_map(on_device, mesh=fine, in_specs=in_specs, out_specs=out_specs, check_vma=False)
```

```python
import functools

import jax
import jax.numpy as jnp
from jax import lax
from jax.experimental import pallas as pl
from jax.experimental.pallas import tpu as pltpu
from jax.sharding import Mesh
from jax.sharding import PartitionSpec as P

HEADS = 16
KV_HEADS = 8
HEAD = 64
TOPK = 8
CAP = 80
TOK = 256
D = 1024
FF = 512
EXPERTS = 32
SHARE = 8
SLOTS = SHARE * CAP
BLOCKS = 8
HALF = FF // 2
GROUP = 4
LENGTH = 1024

epsilon = 1e-06
rope_base = 10000.0

AXES = ("ylo", "core", "yhi", "x", "z")
SEQ = ("ylo", "core")
FSDP = ("yhi", "x", "z")
PLANE = ("x", "yhi", "ylo")

f32 = jnp.float32
bf16 = jnp.bfloat16

NT = (((1,), (1,)), ((), ()))
TN = (((0,), (0,)), ((), ()))
VMEM_LIMIT = 56 * 1024 * 1024


def dot(a, b, dims=(((1,), (0,)), ((), ()))):
    return lax.dot_general(a, b, dims, preferred_element_type=f32)


def iota(shape, axis):
    return lax.broadcasted_iota(jnp.int32, shape, axis)


def as_bf16(cond):
    return jnp.where(cond, 1.0, 0.0).astype(bf16)


def call(kernel, name, flops, moved, **kwargs):
    return pl.pallas_call(
        kernel,
        compiler_params=pltpu.CompilerParams(vmem_limit_bytes=VMEM_LIMIT),
        cost_estimate=pl.CostEstimate(flops=flops, bytes_accessed=moved, transcendentals=0),
        name=name,
        **kwargs,
    )


def shape(*dims, dtype=bf16):
    return jax.ShapeDtypeStruct(dims, dtype)


SCALAR = pl.BlockSpec(memory_space=pltpu.SMEM)
ANYWHERE = pl.BlockSpec(memory_space=pl.ANY)
VECTOR = pl.BlockSpec(memory_space=pltpu.VMEM)


def column_of(row):
    n = row.shape[1]
    step = min(n, 128)
    same = iota((step, step), 0) == iota((step, step), 1)
    parts = [jnp.sum(jnp.where(same, row[:, i : i + step], 0.0), axis=1, keepdims=True) for i in range(0, n, step)]
    return jnp.concatenate(parts, axis=0) if len(parts) > 1 else parts[0]


def row_of(column):
    n = column.shape[0]
    same = iota((128, 128), 0) == iota((128, 128), 1)
    parts = [jnp.sum(jnp.where(same, column[i : i + 128], 0.0), axis=0, keepdims=True) for i in range(0, n, 128)]
    return jnp.concatenate(parts, axis=1)


def codes_kernel(routes_ref, gy_ref, gy_out_ref):
    routes = routes_ref[...]
    expert = iota((TOK, EXPERTS), 1)
    chosen = jnp.zeros((TOK, EXPERTS), jnp.bool_)
    for i in range(TOPK):
        chosen = chosen | (routes[:, i : i + 1] == expert)
    earlier = as_bf16(iota((TOK, TOK), 1) < iota((TOK, TOK), 0))
    codes = jnp.where(chosen, dot(earlier, as_bf16(chosen)), -1.0)
    gy_out_ref[:, :D] = gy_ref[...]
    gy_out_ref[:, D:] = jnp.concatenate([codes, jnp.zeros((TOK, 128 - EXPERTS), f32)], axis=1).astype(bf16)


def with_codes(routes, gy):
    return call(
        codes_kernel, "codes", 50_000_000, 1_500_000, in_specs=[VECTOR] * 2, out_shape=shape(TOK, D + 128)
    )(routes, gy)


def pack_kernel(
    place_ref, query_ref, key_ref, value_ref, router_ref, one_ref, two_ref, gate_ref, up_ref,
    packed_ref, keep_ref, send_ref,
):
    core = place_ref[1]
    lane = iota((8, 128), 1)
    small = jnp.concatenate([router_ref[...].astype(f32), jnp.zeros((8, 96), f32)], axis=1)
    small = jnp.where(lane == 32, column_of(one_ref[...].astype(f32)), small)
    small = jnp.where(lane == 33, column_of(two_ref[...].astype(f32)), small).astype(bf16)
    for s in range(4):
        part = jnp.concatenate(
            [
                query_ref[:, 256 * s : 256 * s + 256],
                key_ref[:, 128 * s : 128 * s + 128],
                value_ref[:, 128 * s : 128 * s + 128],
                small,
            ],
            axis=1,
        )
        for f in range(32):
            packed_ref[32 * s + f] = part
    for i, ref in enumerate((gate_ref, up_ref)):
        for j in range(2):
            keep_ref[i, :, 128 * j : 128 * j + 128] = ref[:, pl.ds(256 * j + 128 * core, 128)]
            send_ref[i, :, 128 * j : 128 * j + 128] = ref[:, pl.ds(256 * j + 128 * (1 - core), 128)]


def pack(place, *args):
    return call(
        pack_kernel, "pack", 100_000_000, 4_000_000,
        in_specs=[SCALAR] + [VECTOR] * len(args),
        out_shape=(shape(128, 8, 640), shape(2, TOK, HALF), shape(2, TOK, HALF)),
    )(place, *args)


def assemble_kernel(place_ref, keep_ref, got_ref, down_ref, out_ref):
    core = place_ref[1]
    for i in range(2):
        out_ref[pl.ds(512 * i + 256 * core, 256)] = keep_ref[i]
        out_ref[pl.ds(512 * i + 256 * (1 - core), 256)] = got_ref[i]
    for j in range(4):
        out_ref[1024 + 128 * j : 1152 + 128 * j] = down_ref[:, 256 * j : 256 * j + 256]


def assemble(place, keep, got, down):
    return call(
        assemble_kernel, "assemble", 1_000_000, 2_000_000,
        in_specs=[SCALAR] + [VECTOR] * 3, out_shape=shape(1536, 256),
    )(place, keep, got, down)


def head_lanes_rope(head):
    lane = iota((1, 256), 1) % 128
    return (lane >= 32 * head) & (lane < 32 * head + 32)


def head_lanes(head):
    lane = iota((1, 256), 1)
    return (lane >= 64 * head) & (lane < 64 * head + 64)


def spread_queries():
    row, col = iota((256, 256), 0), iota((256, 256), 1)
    return row == ((col % 128) // 32) * 64 + (col // 128) * 32 + col % 32


def spread_keys():
    row, col = iota((128, 256), 0), iota((128, 256), 1)
    return row == ((col % 128) // 64) * 64 + (col // 128) * 32 + col % 32, (col % 64) < 32


def spread_values():
    row, col = iota((128, 256), 0), iota((128, 256), 1)
    return row == (col // 128) * 64 + col % 64, (col % 128) < 64


def positions(place_ref):
    ylo, core = place_ref[0], place_ref[1]
    return [(y, c, 2 * y + c) for c in (core, 1 - core) for y in (ylo, 1 - ylo)]


def normed(x):
    return x * lax.rsqrt(jnp.mean(x * x, axis=-1, keepdims=True) + epsilon)


def front_kernel(
    place_ref, x0_ref, x1_ref, x2_ref, x3_ref, w_ref, cos_ref, sin_ref,
    q_ref, k_ref, v_ref, o0_ref, o1_ref, o2_ref, o3_ref, lse_ref, h_ref, gains_ref, o_ref,
):
    gain = row_of(w_ref[:, 512:640].astype(f32)[:, 32:33])
    gains_ref[0:1] = gain
    gains_ref[1:2] = row_of(w_ref[:, 512:640].astype(f32)[:, 33:34])
    wq = dot(w_ref[:, :256], as_bf16(spread_queries())).astype(bf16)
    wk = dot(w_ref[:, 256:384], as_bf16(spread_keys()[0])).astype(bf16)
    wv = dot(w_ref[:, 384:512], as_bf16(spread_values()[0])).astype(bf16)
    for (_, _, at), x_ref in zip(positions(place_ref), (x0_ref, x1_ref, x2_ref, x3_ref)):
        rows = pl.ds(pl.multiple_of(256 * at, 256), 256)
        h = (normed(x_ref[...].astype(f32)) * gain).astype(bf16)
        h_ref[rows] = h
        c, s = cos_ref[rows], sin_ref[rows]
        for w, out in ((wq, q_ref), (wk, k_ref)):
            pre = dot(h, w)
            a, b = pre[:, :128], pre[:, 128:]
            out[rows] = jnp.concatenate([a * c - b * s, b * c + a * s], axis=1).astype(bf16)
        v_ref[rows] = dot(h, wv).astype(bf16)
    for i in range(4):
        rows = slice(256 * i, 256 * i + 256)
        n = 256 * (i + 1)
        seen = iota((256, n), 1) <= iota((256, n), 0) + 256 * i
        mixed = jnp.zeros((256, 256), f32)
        logs = jnp.zeros((256, 128), f32)
        for head in range(GROUP):
            q = q_ref[rows] * as_bf16(head_lanes_rope(head))
            scores = jnp.where(seen, dot(q, k_ref[:n], NT) * HEAD**-0.5, -1e30)
            peak = jnp.max(scores, axis=-1, keepdims=True)
            e = jnp.exp(scores - peak)
            total = jnp.sum(e, axis=-1, keepdims=True)
            probs = (e * (1.0 / total)).astype(bf16)
            mixed = mixed + dot(probs, v_ref[:n] * as_bf16(head_lanes(head)))
            logs = jnp.where(iota((256, 128), 1) == head, peak + jnp.log(total), logs)
        o_ref[i] = mixed.astype(bf16)
        lse_ref[rows] = logs
    for (_, _, at), out in zip(positions(place_ref), (o0_ref, o1_ref, o2_ref, o3_ref)):
        out[...] = o_ref[at]


def front(place, blocks, w, cos, sin):
    return call(
        front_kernel, "front", 8_000_000_000, 10_000_000,
        in_specs=[SCALAR] + [VECTOR] * 7,
        out_shape=(
            shape(LENGTH, 256), shape(LENGTH, 256), shape(LENGTH, 256), *[shape(TOK, 256)] * 4,
            shape(LENGTH, 128, dtype=f32), shape(LENGTH, D), shape(8, D, dtype=f32),
        ),
        scratch_shapes=[pltpu.VMEM((4, TOK, 256), bf16)],
    )(place, *blocks, w, cos, sin)


def output_blocks(own_ref, other_ref):
    return [ref[:, D * i : D * i + D] for ref in (own_ref, other_ref) for i in range(2)]


def mid_kernel(x_ref, m0_ref, m1_ref, m2_ref, m3_ref, own_ref, other_ref, gains_ref, residual_ref, h_ref):
    total = x_ref[...].astype(f32)
    for mixed_ref, w in zip((m0_ref, m1_ref, m2_ref, m3_ref), output_blocks(own_ref, other_ref)):
        total = total + dot(mixed_ref[...], w)
    residual_ref[...] = total
    h_ref[...] = (normed(total) * gains_ref[1:2]).astype(bf16)


def mid(x, mixed, own, other, gains):
    return call(
        mid_kernel, "mid", 1_000_000_000, 5_000_000,
        in_specs=[VECTOR] * 8,
        out_shape=(shape(TOK, D, dtype=f32), shape(TOK, D)),
    )(x, *mixed, own, other, gains)


def turn_kernel(
    place_ref, part0_ref, part1_ref, part2_ref, part3_ref, gy_ref, residual_ref, small_ref, gains_ref,
    m0_ref, m1_ref, m2_ref, m3_ref, own_ref, other_ref,
    do0_ref, do1_ref, do2_ref, do3_ref, grad_ref, keep_ref, send_ref, sums_ref,
):
    parts = (part0_ref, part1_ref, part2_ref, part3_ref)
    summed = sum(part[...].astype(f32) for part in parts)
    residual = residual_ref[...]
    factor = lax.rsqrt(jnp.mean(residual * residual, axis=-1, keepdims=True) + epsilon)
    normal = residual * factor
    gain = gains_ref[1:2]
    h = (normal * gain).astype(bf16)
    router = small_ref[:, 512 : 512 + EXPERTS]
    table = gate_table(dot(h, router), gy_ref[:, D:].astype(f32)[:, :EXPERTS])
    dgates = summed[:, D : D + EXPERTS]
    dlogits = (table * (dgates - jnp.sum(table * dgates, axis=-1, keepdims=True))).astype(bf16)
    dh = summed[:, :D] + dot(dlogits, router, NT)
    grad_gain = column_of(jnp.sum(dh * normal, axis=0, keepdims=True))
    grad_router = dot(h, dlogits, TN)
    sums = jnp.concatenate([grad_router, jnp.zeros((D, 128 - EXPERTS), f32)], axis=1)
    sums_ref[...] = jnp.where(iota((D, 128), 1) == 33, grad_gain, sums)
    scaled = dh * gain
    grad = gy_ref[:, :D].astype(f32) + factor * (scaled - normal * jnp.mean(scaled * normal, axis=-1, keepdims=True))
    grad_ref[...] = grad
    dz = grad.astype(bf16)
    mixed_refs, do_refs = (m0_ref, m1_ref, m2_ref, m3_ref), (do0_ref, do1_ref, do2_ref, do3_ref)
    for i, ((y, _, _), w) in enumerate(zip(positions(place_ref), output_blocks(own_ref, other_ref))):
        do_refs[i][...] = dot(dz, w, NT).astype(bf16)
        out = keep_ref if i < 2 else send_ref
        out[y] = dot(mixed_refs[i][...], dz, TN).astype(bf16)


def turn_back(place, parts, gy, residual, small, gains, mixed, own, other):
    pair = shape(2, TOK, D)
    return call(
        turn_kernel, "turn", 2_000_000_000, 10_000_000,
        in_specs=[SCALAR] + [VECTOR] * 14,
        out_shape=(*[shape(TOK, 256)] * 4, shape(TOK, D, dtype=f32), pair, pair, shape(D, 128, dtype=f32)),
    )(place, *parts, gy, residual, small, gains, *mixed, own, other)


def back_kernel(
    place_ref, q_ref, k_ref, v_ref, do0_ref, do1_ref, do2_ref, do3_ref, lse_ref, cos_ref, sin_ref, w_ref,
    x0_ref, x1_ref, x2_ref, x3_ref, out_ref, keep_ref, send_ref, gain_ref, do_ref, dk_ref, dv_ref,
):
    for (_, _, at), ref in zip(positions(place_ref), (do0_ref, do1_ref, do2_ref, do3_ref)):
        do_ref[at] = ref[...]
    dk_ref[...] = jnp.zeros_like(dk_ref)
    dv_ref[...] = jnp.zeros_like(dv_ref)
    scale = HEAD**-0.5
    place_queries = as_bf16(spread_queries())
    for i in range(4):
        rows = slice(256 * i, 256 * i + 256)
        n = 256 * (i + 1)
        seen = iota((256, n), 1) <= iota((256, n), 0) + 256 * i
        dq = jnp.zeros((256, 256), f32)
        for head in range(GROUP):
            lanes = head_lanes_rope(head)
            q = q_ref[rows] * as_bf16(lanes)
            do = do_ref[i] * as_bf16(head_lanes(head))
            scores = dot(q, k_ref[:n], NT) * scale - lse_ref[rows, head : head + 1]
            probs = jnp.where(seen, jnp.exp(jnp.where(seen, scores, 0.0)), 0.0)
            dprobs = dot(do, v_ref[:n], NT)
            row_dot = jnp.sum(probs * dprobs, axis=-1, keepdims=True)
            ds = (probs * (dprobs - row_dot)).astype(bf16)
            dq = dq + jnp.where(lanes, dot(ds, k_ref[:n]), 0.0)
            dk_ref[:n] += dot(ds, q, TN)
            dv_ref[:n] += dot(probs.astype(bf16), do, TN)
        c, s = cos_ref[rows], sin_ref[rows]
        a, b = dq[:, :128] * scale, dq[:, 128:] * scale
        dq = jnp.concatenate([a * c + b * s, b * c - a * s], axis=1).astype(bf16)
        out_ref[rows, :256] = dot(dq, place_queries, NT).astype(bf16)
    keep_keys, first_key = spread_keys()
    keep_values, first_value = spread_values()
    pick_keys = as_bf16(keep_keys & first_key)
    pick_values = as_bf16(keep_values & first_value)
    for i in range(4):
        rows = slice(256 * i, 256 * i + 256)
        c, s = cos_ref[rows], sin_ref[rows]
        a, b = dk_ref[rows, :128] * scale, dk_ref[rows, 128:] * scale
        a, b = a * c + b * s, b * c - a * s
        a, b = a + pltpu.roll(a, 96, 1), b + pltpu.roll(b, 96, 1)
        out_ref[rows, 256:384] = dot(jnp.concatenate([a, b], axis=1).astype(bf16), pick_keys, NT).astype(bf16)
        a, b = dv_ref[rows, :128], dv_ref[rows, 128:]
        a, b = a + pltpu.roll(a, 64, 1), b + pltpu.roll(b, 64, 1)
        out_ref[rows, 384:512] = dot(jnp.concatenate([a, b], axis=1).astype(bf16), pick_values, NT).astype(bf16)
    w = w_ref[:, :512]
    grad_gain = jnp.zeros((1, D), f32)
    for i, ((y, _, at), x_ref) in enumerate(zip(positions(place_ref), (x0_ref, x1_ref, x2_ref, x3_ref))):
        partial = dot(out_ref[pl.ds(pl.multiple_of(256 * at, 256), 256)], w, NT)
        grad_gain = grad_gain + jnp.sum(partial * normed(x_ref[...].astype(f32)), axis=0, keepdims=True)
        out = keep_ref if i < 2 else send_ref
        out[y] = partial.astype(bf16)
    gain_ref[...] = jnp.broadcast_to(grad_gain, (8, D))


def back(place, q, k, v, do, lse, cos, sin, w, blocks):
    pair = shape(2, TOK, D)
    return call(
        back_kernel, "back", 20_000_000_000, 16_000_000,
        in_specs=[SCALAR] + [VECTOR] * 15,
        out_shape=(shape(LENGTH, 512), pair, pair, shape(8, D, dtype=f32)),
        scratch_shapes=[
            pltpu.VMEM((4, TOK, 256), bf16), pltpu.VMEM((LENGTH, 256), f32), pltpu.VMEM((LENGTH, 256), f32),
        ],
    )(place, q, k, v, *do, lse, cos, sin, w, *blocks)


def projections_kernel(h_ref, dqkv_ref, sums_ref, gain_ref, first_ref):
    first_ref[:, :512] = dot(h_ref[...], dqkv_ref[...], TN).astype(bf16)
    small = jnp.where(iota((D, 128), 1) == 32, column_of(gain_ref[0:1]), sums_ref[...])
    first_ref[:, 512:] = small.astype(bf16)


def projections(h, dqkv, sums, gain):
    return call(
        projections_kernel, "projections", 1_500_000_000, 5_000_000, in_specs=[VECTOR] * 4, out_shape=shape(D, 640)
    )(h, dqkv, sums, gain)


def own_slots(expert, slot, z):
    start = ((expert % 16) // 4 * 2 + expert // 16) * CAP
    own = (expert % 4 == z) & (slot >= start) & (slot < start + CAP)
    return own, jnp.where(own, slot - start, 0)


def slot_tables(z, spread, start):
    own, place = own_slots(iota((EXPERTS, SLOTS), 0), iota((EXPERTS, SLOTS), 1), z)
    spread[...] = as_bf16(own)
    start[...] = jnp.sum(place, axis=0, keepdims=True).astype(f32)


SLOT_TABLES = [pltpu.VMEM((EXPERTS, SLOTS), bf16), pltpu.VMEM((1, SLOTS), f32)]


def gate_table(logits, codes):
    routed = codes >= 0
    logits = jnp.where(routed, logits, -1e30)
    e = jnp.where(routed, jnp.exp(logits - jnp.max(logits, axis=-1, keepdims=True)), 0.0)
    return e / jnp.sum(e, axis=-1, keepdims=True)


def split(values):
    high = values.astype(bf16)
    return high, (values - high.astype(f32)).astype(bf16)


def whole(*shape):
    return pl.BlockSpec(shape, lambda e: (0,) * len(shape))


def per_expert(*shape):
    return pl.BlockSpec((1,) + shape, lambda e: (e,) + (0,) * len(shape))


def rows_kernel(n, with_gates, z_ref, *refs):
    i = pl.program_id(0)
    z = z_ref[0]
    values_refs, refs = refs[:n], refs[n:]
    if with_gates:
        codes_refs, router_ref, refs = refs[:n], refs[n], refs[n + 1 :]
        rows_ref, gates_ref, turn_ref, values, codes, own, start = refs[-7:]
    else:
        rows_ref, turn_ref, values, codes, own, start = refs[-6:]
    for b in range(n):

        @pl.when(i == b)
        def _():
            values[...] = values_refs[b][:, :D]
            codes[...] = codes_refs[b][...] if with_gates else values_refs[b][:, D:]

    @pl.when(i == 0)
    def _():
        turn_ref[...] = jnp.zeros_like(turn_ref)
        mine, offset = own_slots(iota((SLOTS, EXPERTS), 1), iota((SLOTS, EXPERTS), 0), z)
        own[...] = as_bf16(mine)
        start[...] = jnp.sum(offset, axis=1, keepdims=True).astype(f32)

    slots = codes[:, :EXPERTS]
    place = as_bf16(dot(own[...], slots, NT) == start[...])
    rows_ref[:, 0] = dot(place, values[...]).astype(bf16).reshape(SHARE, CAP, D)
    if with_gates:
        table = gate_table(dot(values[...], router_ref[:, :EXPERTS]), slots.astype(f32))
        high, low = split(table)
        both = dot(place, high) + dot(place, low)
        gate = jnp.sum(both * own[...].astype(f32), axis=1, keepdims=True)
        gates_ref[:, 0] = gate.reshape(SHARE, CAP, 1)


def rows_of(z, first, blocks, codes, router, kept, turn):
    n, with_gates = len(blocks), router is not None
    args, specs = [z, *blocks], [SCALAR] + [whole(TOK, blocks[0].shape[1])] * n
    if with_gates:
        args += [*codes, router]
        specs += [pl.BlockSpec((TOK, 128), lambda e: (0, D // 128))] * n + [pl.BlockSpec((D, 128), lambda e: (0, 4))]
    args.append(turn)
    specs.append(ANYWHERE)
    widths = [(D, bf16)] + ([(1, f32)] if with_gates else [])
    out_specs = [pl.BlockSpec((SHARE, 1, CAP, w), lambda e: (0, first + e, 0, 0)) for w, _ in widths]
    out_shape = [shape(SHARE, BLOCKS, CAP, w, dtype=t) for w, t in widths]
    out_specs.append(whole(8, 128))
    out_shape.append(shape(8, 128, dtype=f32))
    aliases = {}
    if kept is not None:
        aliases = {len(args) + i: i for i in range(len(kept))}
        args += kept
        specs += [ANYWHERE] * len(kept)
    *kept, turn = call(
        functools.partial(rows_kernel, n, with_gates), "rows", n * 750_000_000, n * 2_000_000,
        grid=(n,), in_specs=specs, out_specs=out_specs, out_shape=out_shape, input_output_aliases=aliases,
        scratch_shapes=[
            pltpu.VMEM((TOK, D), bf16), pltpu.VMEM((TOK, 128), bf16), pltpu.VMEM((SLOTS, EXPERTS), bf16),
            pltpu.VMEM((SLOTS, 1), f32),
        ],
    )(*args)
    return kept, turn


def down_of(parts):
    return jnp.concatenate(
        [
            jnp.concatenate([parts[0, 128 * j : 128 * j + 128], parts[1, 128 * j : 128 * j + 128]], axis=0)
            for j in range(4)
        ],
        axis=1,
    )


def codes_specs():
    return [pl.BlockSpec((TOK, 128), lambda e: (0, D // 128))] * BLOCKS


PARTS = 2


def main_kernel(z_ref, x_ref, gy_ref, gate_ref, w_ref, *refs):
    codes_refs = refs[:8]
    act_ref, out_ref, own_ref, other_ref, kept, dgates, hidden, codes_kept, spread, start, mine = refs[8:]
    e = pl.program_id(0)

    @pl.when(e == 0)
    def _():
        for b in range(BLOCKS):
            codes_kept[b] = codes_refs[b][...]
        slot_tables(z_ref[0], spread, start)
        own, _ = own_slots(iota((SLOTS, EXPERTS), 1), iota((SLOTS, EXPERTS), 0), z_ref[0])
        mine[...] = own.astype(f32)

    down_w = down_of(w_ref[:, 1024:])
    gate_w = w_ref[:, :512].reshape(D, HALF)
    up_w = w_ref[:, 512:1024].reshape(D, HALF)
    both_w = jnp.concatenate([gate_w, up_w], axis=1)
    step = BLOCKS // PARTS
    for i in range(PARTS):
        blocks, rows = slice(step * i, step * i + step), slice(step * i * CAP, step * (i + 1) * CAP)
        x = x_ref[0, blocks].reshape(step * CAP, D)
        gate = gate_ref[0, blocks].reshape(step * CAP, 1)
        da = dot(gy_ref[0, blocks].reshape(step * CAP, D), down_w, NT)
        g = dot(x, gate_w)
        u = dot(x, up_w)
        s = jax.nn.sigmoid(g)
        silu = g * s
        act = silu * u
        dgates[blocks, e] = jnp.sum(act * da, axis=1, keepdims=True).reshape(step, CAP, 1)
        act_ref[0, rows] = (act * gate).astype(bf16)
        da = da * gate
        hidden[rows, :HALF] = (da * u * (s + silu * (1.0 - s))).astype(bf16)
        hidden[rows, HALF:] = (da * silu).astype(bf16)
        kept[blocks, e] = dot(hidden[rows], both_w, NT).astype(bf16).reshape(step, CAP, D)
    made = dot(hidden[...], x_ref[0].reshape(SLOTS, D), TN).astype(bf16)
    for i in range(2):
        out_ref[0, i, :512] = made[:, 512 * i : 512 * i + 512]
    made = dot(act_ref[0], gy_ref[0].reshape(SLOTS, D), TN).astype(bf16)
    for i in range(2):
        out_ref[0, i, 512:640] = made[128 * i : 128 * i + 128, :512]
        out_ref[0, i, 640:768] = made[128 * i : 128 * i + 128, 512:]

    @pl.when(e == SHARE - 1)
    def _():
        def pair(j, carry):
            for c, out in ((0, own_ref), (1, other_ref)):
                b = 2 * j + c
                place = as_bf16(dot(codes_kept[b][:, :EXPERTS], spread[...]) == start[...])
                out[j, :, :D] = dot(place, kept[b].reshape(SLOTS, D)).astype(bf16)
                high, low = split(mine[...] * dgates[b].reshape(SLOTS, 1))
                scattered = dot(place, high) + dot(place, low)
                out[j, :, D:] = jnp.concatenate([scattered, jnp.zeros((TOK, 128 - EXPERTS), f32)], axis=1).astype(bf16)
            return carry

        lax.fori_loop(0, 4, pair, 0)


def main(z, x, gy, gates, weights, codes):
    back = shape(4, TOK, D + 128)
    return call(
        main_kernel, "experts", 25_000_000_000, 60_000_000,
        grid=(SHARE,),
        in_specs=[
            SCALAR, per_expert(BLOCKS, CAP, D), per_expert(BLOCKS, CAP, D), per_expert(BLOCKS, CAP, 1),
            pl.BlockSpec((2, 1536, 256), lambda e: (e, 0, 0)), *codes_specs(),
        ],
        out_specs=[
            per_expert(SLOTS, HALF), per_expert(2, 768, 512), whole(4, TOK, D + 128), whole(4, TOK, D + 128),
        ],
        out_shape=[shape(SHARE, SLOTS, HALF), shape(SHARE, 2, 768, 512), back, back],
        scratch_shapes=[
            pltpu.VMEM((BLOCKS, SHARE, CAP, D), bf16),
            pltpu.VMEM((BLOCKS, SHARE, CAP, 1), f32),
            pltpu.VMEM((SLOTS, 2 * HALF), bf16),
            pltpu.VMEM((BLOCKS, TOK, 128), bf16),
            *SLOT_TABLES,
            pltpu.VMEM((SLOTS, EXPERTS), f32),
        ],
    )(z, x, gy, gates, weights, *codes)


def outs_kernel(z_ref, act_ref, w_ref, *refs):
    codes_refs = refs[:8]
    own_ref, other_ref, kept, codes_kept, spread, start = refs[8:]
    e = pl.program_id(0)
    kept[:, e] = dot(act_ref[0], down_of(w_ref[...])).astype(bf16).reshape(BLOCKS, CAP, D)

    @pl.when(e == 0)
    def _():
        for b in range(BLOCKS):
            codes_kept[b] = codes_refs[b][...]
        slot_tables(z_ref[0], spread, start)

    @pl.when(e == SHARE - 1)
    def _():
        def pair(j, carry):
            for c, out in ((0, own_ref), (1, other_ref)):
                b = 2 * j + c
                place = as_bf16(dot(codes_kept[b][:, :EXPERTS], spread[...]) == start[...])
                out[j] = dot(place, kept[b].reshape(SLOTS, D)).astype(bf16)
            return carry

        lax.fori_loop(0, 4, pair, 0)


def outs(z, act, weights, codes):
    back = jax.ShapeDtypeStruct((4, TOK, D), bf16)
    return call(
        outs_kernel, "expert_outs", 6_000_000_000, 12_000_000,
        grid=(SHARE,),
        in_specs=[
            SCALAR, per_expert(SLOTS, HALF), pl.BlockSpec((2, 512, 256), lambda e: (e, 2, 0)), *codes_specs(),
        ],
        out_specs=[whole(4, TOK, D)] * 2,
        out_shape=[back, back],
        scratch_shapes=[
            pltpu.VMEM((BLOCKS, SHARE, CAP, D), bf16), pltpu.VMEM((BLOCKS, TOK, 128), bf16), *SLOT_TABLES,
        ],
    )(z, act, weights, *codes)


def finish_kernel(place_ref, mine_ref, got_ref, gate_ref, up_ref, down_ref):
    core = place_ref[1]
    for i, out in enumerate((gate_ref, up_ref)):
        for j in range(2):
            rows = slice(256 * i + 128 * j, 256 * i + 128 * j + 128)
            keep = mine_ref[rows, pl.ds(pl.multiple_of(256 * core, 256), 256)].astype(f32)
            out[:, pl.ds(pl.multiple_of(256 * j + 128 * core, 128), 128)] = keep.T
            got = got_ref[rows].astype(f32)
            out[:, pl.ds(pl.multiple_of(256 * j + 128 * (1 - core), 128), 128)] = got.T
    for j in range(2):
        down_ref[:, 512 * j : 512 * j + 512] = mine_ref[512 + 128 * j : 640 + 128 * j].astype(f32)


def finish(place, mine, got):
    return call(
        finish_kernel, "finish", 1_000_000, 4_000_000,
        in_specs=[SCALAR, VECTOR, VECTOR],
        out_shape=(shape(TOK, FF, dtype=f32), shape(TOK, FF, dtype=f32), shape(128, D, dtype=f32)),
    )(place, mine, got)


def shift(values, axis, by):
    n = 4 if axis in ("x", "z") else 2
    return lax.ppermute(values, axis, [(i, (i + by) % n) for i in range(n)])


def swap(values, axis):
    return shift(values, axis, 1)


def gather_z(values):
    return [values, shift(values, "z", 1), shift(values, "z", -1), shift(values, "z", 2)]


def with_core(blocks):
    return [(block, swap(block, "core")) for block in blocks]


def exchange_seq(own, across, beside, both):
    return [own, swap(across, "ylo"), swap(beside, "core"), swap(swap(both, "ylo"), "core")]


def core_sums(own, other):
    got = swap(other, "core")
    return [(own[j].astype(f32) + got[j].astype(f32)).astype(bf16) for j in range(4)]


def scatter_z(sums):
    return [sums[0], shift(sums[1], "z", -1), shift(sums[2], "z", 1), shift(sums[3], "z", 2)]


def fence(*values):
    return lax.optimization_barrier(values)


def on_device(
    tokens, norm1_gain, query_weight, key_weight, value_weight, output_weight, norm2_gain, router_weight,
    expert_gate, expert_up, expert_down, routes, cotangent,
):
    ylo, core = lax.axis_index("ylo"), lax.axis_index("core")
    z = lax.axis_index("z").astype(jnp.int32).reshape(1)
    place = jnp.stack([ylo, core]).astype(jnp.int32)

    own = tokens.reshape(TOK, D)
    across = swap(own, "ylo")
    gy_own = with_codes(routes.reshape(TOK, TOPK), cotangent.reshape(TOK, D))
    gy_blocks = gather_z(gy_own)

    packed, keep, send = pack(
        place, query_weight, key_weight, value_weight, router_weight, norm1_gain.reshape(1, 8), norm2_gain.reshape(1, 8),
        expert_gate.reshape(TOK, FF), expert_up.reshape(TOK, FF),
    )

    expert_w = assemble(place, keep, swap(send, "core"), expert_down.reshape(128, D))
    expert_w, packed, across = fence(expert_w, packed, across)
    expert_w = lax.all_gather(expert_w, PLANE, axis=0).reshape(16, 1536, 256)

    arrived = lax.all_to_all(packed, AXES, split_axis=0, concat_axis=0, tiled=True).reshape(D, 640)
    beside = swap(own, "core")

    lane = jnp.arange(128) % 32
    angles = jnp.arange(LENGTH).astype(f32)[:, None] * (rope_base ** (-2.0 * lane.astype(f32) / HEAD))[None, :]
    cos, sin = fence(jnp.cos(angles), jnp.sin(angles))
    blocks = [own, across, beside, swap(across, "core")]
    q, k, v, *mixed, lse, hidden_all, gains = front(place, blocks, arrived, cos, sin)

    output_rows = jnp.concatenate([output_weight, swap(output_weight, "ylo")], axis=1)
    output_rows, _ = fence(output_rows, arrived)
    output_own = lax.all_to_all(
        jnp.broadcast_to(output_rows[None], (32, 8, 2 * D)), FSDP, split_axis=0, concat_axis=0, tiled=True
    ).reshape(TOK, 2 * D)

    mixed = exchange_seq(*mixed)
    output_own, *rest = fence(output_own, *mixed, *gy_blocks)
    mixed, gy_blocks = rest[:4], rest[4:]
    output_other = swap(output_own, "core")
    gy_blocks = [block for pair in with_core(gy_blocks) for block in pair]
    residual, hidden_two = mid(own, mixed, output_own, output_other, gains)

    h_blocks = gather_z(hidden_two)
    turn, _ = fence(jnp.zeros((8, 128), f32), hidden_two)
    gy_rows, turn = rows_of(z, 0, gy_blocks, None, None, None, turn)
    rows, turn = rows_of(z, 0, (hidden_two, swap(hidden_two, "core")), gy_blocks[:2], arrived, None, turn)
    *h_blocks, turn = fence(*h_blocks, turn)
    h_blocks = [block for pair in with_core(h_blocks[1:]) for block in pair]
    rows, turn = rows_of(z, 2, h_blocks, gy_blocks[2:], arrived, rows, turn)
    (gy_rows,), (rows, gate_rows) = gy_rows, rows

    act, expert_grads, back_own, back_other = main(z, rows, gy_rows, gate_rows, expert_w, gy_blocks)
    sums = core_sums(back_own, back_other)
    parts = scatter_z(sums)
    moe_act, *_ = fence(act, *sums)
    moe_own, moe_other = outs(z, moe_act, expert_w, gy_blocks)
    expert_grads = lax.psum_scatter(expert_grads.reshape(16 * 768, 512), PLANE, scatter_dimension=0, tiled=True)

    moe_sums = core_sums(moe_own, moe_other)
    *do, grad_residual, keep, send, small = turn_back(
        place, parts, gy_own, residual, arrived, gains, mixed, output_own, output_other
    )

    do = exchange_seq(*do)
    grad_output_sum = (keep.astype(f32) + swap(send, "core").astype(f32)).astype(bf16).reshape(64, 8, D)
    grad_output_sum, *moe_sums = fence(grad_output_sum, *moe_sums)
    moe_near = [shift(moe_sums[1], "z", -1), shift(moe_sums[2], "z", 1)]
    grad_output = lax.all_to_all(grad_output_sum, ("ylo",) + FSDP, split_axis=0, concat_axis=0, tiled=True)
    dqkv, keep, send, gain = back(place, q, k, v, do, lse, cos, sin, arrived, blocks)
    dqkv, keep, send, own, grad_output, *moe_near = fence(dqkv, keep, send, own, grad_output, *moe_near)
    first = projections(hidden_all, dqkv, small, gain)

    away = jnp.where(core == 0, expert_grads[:512, 256:], expert_grads[:512, :256])
    finished = finish(place, expert_grads, swap(away, "core"))

    pair = (keep.astype(f32) + swap(send, "core").astype(f32)).astype(bf16)
    kept = jnp.where(ylo == 0, pair[0], pair[1])
    got = swap(jnp.where(ylo == 0, pair[1], pair[0]), "ylo")
    got, moe_far = fence(got, shift(moe_sums[3], "z", 2))
    grad_hidden_one = kept.astype(f32) + got.astype(f32)
    first = lax.all_to_all(first.reshape(128, 8, 640), AXES, split_axis=0, concat_axis=0, tiled=True)
    grad_output = jnp.sum(grad_output.astype(f32), axis=0)
    layer_out = sum(part.astype(f32) for part in (moe_sums[0], *moe_near, moe_far))
    layer_out = (residual + layer_out).astype(bf16).reshape(1, TOK, D)
    inputs = own.astype(f32)
    factor_one = lax.rsqrt(jnp.mean(inputs * inputs, axis=-1, keepdims=True) + epsilon)
    normed_one = inputs * factor_one
    scaled = grad_hidden_one * gains[0:1]
    grad_inputs = grad_residual + factor_one * (
        scaled - normed_one * jnp.mean(scaled * normed_one, axis=-1, keepdims=True)
    )

    first, layer_out, grad_inputs, grad_output, grad_gate, grad_up, grad_down = fence(
        first, layer_out, grad_inputs, grad_output, *finished
    )
    first = jnp.sum(first.astype(f32).reshape(4, 32, 8, 640), axis=1)
    grad_query = first[:, :, :256].transpose(1, 0, 2).reshape(8, D)
    grad_key = first[:, :, 256:384].transpose(1, 0, 2).reshape(8, 512)
    grad_value = first[:, :, 384:512].transpose(1, 0, 2).reshape(8, 512)
    small = jnp.sum(first[:, :, 512:], axis=0)
    return (
        layer_out, grad_inputs.reshape(1, TOK, D), small[:, 32], grad_query, grad_key, grad_value, grad_output,
        small[:, 33], small[:, :EXPERTS], grad_gate.reshape(1, TOK, FF), grad_up.reshape(1, TOK, FF),
        grad_down.reshape(1, 128, D),
    )


def solution(mesh):
    fine = Mesh(mesh.devices.reshape(2, 2, 2, 4, 4), AXES)
    tok = P(FSDP, SEQ, None)
    row = P(AXES, None)
    vec = P(AXES)
    in_specs = (tok, vec, row, row, row, row, vec, row, tok, tok, tok, tok, tok)
    out_specs = (tok, tok, vec, row, row, row, row, vec, row, tok, tok, tok)
    return jax.shard_map(on_device, mesh=fine, in_specs=in_specs, out_specs=out_specs, check_vma=False)
```

```python
import functools

import jax
import jax.numpy as jnp
from jax import lax
from jax.experimental import pallas as pl
from jax.experimental.pallas import tpu as pltpu
from jax.sharding import Mesh
from jax.sharding import PartitionSpec as P

HEADS = 16
KV_HEADS = 8
HEAD = 64
TOPK = 8
CAP = 80
TOK = 256
D = 1024
FF = 512
EXPERTS = 32
SHARE = 8
SLOTS = SHARE * CAP
BLOCKS = 8
HALF = FF // 2
GROUP = 4
LENGTH = 1024

epsilon = 1e-06
rope_base = 10000.0

AXES = ("ylo", "core", "yhi", "x", "z")
SEQ = ("ylo", "core")
FSDP = ("yhi", "x", "z")
PLANE = ("x", "yhi", "ylo")

f32 = jnp.float32
bf16 = jnp.bfloat16

NT = (((1,), (1,)), ((), ()))
TN = (((0,), (0,)), ((), ()))
VMEM_LIMIT = 56 * 1024 * 1024


def dot(a, b, dims=(((1,), (0,)), ((), ()))):
    return lax.dot_general(a, b, dims, preferred_element_type=f32)


def iota(shape, axis):
    return lax.broadcasted_iota(jnp.int32, shape, axis)


def as_bf16(cond):
    return jnp.where(cond, 1.0, 0.0).astype(bf16)


def call(kernel, name, flops, moved, **kwargs):
    return pl.pallas_call(
        kernel,
        compiler_params=pltpu.CompilerParams(vmem_limit_bytes=VMEM_LIMIT),
        cost_estimate=pl.CostEstimate(flops=flops, bytes_accessed=moved, transcendentals=0),
        name=name,
        **kwargs,
    )


def shape(*dims, dtype=bf16):
    return jax.ShapeDtypeStruct(dims, dtype)


SCALAR = pl.BlockSpec(memory_space=pltpu.SMEM)
ANYWHERE = pl.BlockSpec(memory_space=pl.ANY)
VECTOR = pl.BlockSpec(memory_space=pltpu.VMEM)


def column_of(row):
    n = row.shape[1]
    step = min(n, 128)
    same = iota((step, step), 0) == iota((step, step), 1)
    parts = [jnp.sum(jnp.where(same, row[:, i : i + step], 0.0), axis=1, keepdims=True) for i in range(0, n, step)]
    return jnp.concatenate(parts, axis=0) if len(parts) > 1 else parts[0]


def row_of(column):
    n = column.shape[0]
    same = iota((128, 128), 0) == iota((128, 128), 1)
    parts = [jnp.sum(jnp.where(same, column[i : i + 128], 0.0), axis=0, keepdims=True) for i in range(0, n, 128)]
    return jnp.concatenate(parts, axis=1)


def codes_kernel(routes_ref, gy_ref, gy_out_ref):
    routes = routes_ref[...]
    expert = iota((TOK, EXPERTS), 1)
    chosen = jnp.zeros((TOK, EXPERTS), jnp.bool_)
    for i in range(TOPK):
        chosen = chosen | (routes[:, i : i + 1] == expert)
    earlier = as_bf16(iota((TOK, TOK), 1) < iota((TOK, TOK), 0))
    codes = jnp.where(chosen, dot(earlier, as_bf16(chosen)), -1.0)
    gy_out_ref[:, :D] = gy_ref[...]
    gy_out_ref[:, D:] = jnp.concatenate([codes, jnp.zeros((TOK, 128 - EXPERTS), f32)], axis=1).astype(bf16)


def with_codes(routes, gy):
    return call(
        codes_kernel, "codes", 50_000_000, 1_500_000, in_specs=[VECTOR] * 2, out_shape=shape(TOK, D + 128)
    )(routes, gy)


def pack_kernel(
    place_ref, query_ref, key_ref, value_ref, router_ref, one_ref, two_ref, gate_ref, up_ref,
    packed_ref, keep_ref, send_ref,
):
    core = place_ref[1]
    lane = iota((8, 128), 1)
    small = jnp.concatenate([router_ref[...].astype(f32), jnp.zeros((8, 96), f32)], axis=1)
    small = jnp.where(lane == 32, column_of(one_ref[...].astype(f32)), small)
    small = jnp.where(lane == 33, column_of(two_ref[...].astype(f32)), small).astype(bf16)
    for s in range(4):
        part = jnp.concatenate(
            [
                query_ref[:, 256 * s : 256 * s + 256],
                key_ref[:, 128 * s : 128 * s + 128],
                value_ref[:, 128 * s : 128 * s + 128],
                small,
            ],
            axis=1,
        )
        for f in range(32):
            packed_ref[32 * s + f] = part
    for i, ref in enumerate((gate_ref, up_ref)):
        for j in range(2):
            keep_ref[i, :, 128 * j : 128 * j + 128] = ref[:, pl.ds(256 * j + 128 * core, 128)]
            send_ref[i, :, 128 * j : 128 * j + 128] = ref[:, pl.ds(256 * j + 128 * (1 - core), 128)]


def pack(place, *args):
    return call(
        pack_kernel, "pack", 100_000_000, 4_000_000,
        in_specs=[SCALAR] + [VECTOR] * len(args),
        out_shape=(shape(128, 8, 640), shape(2, TOK, HALF), shape(2, TOK, HALF)),
    )(place, *args)


def assemble_kernel(place_ref, keep_ref, got_ref, down_ref, out_ref):
    core = place_ref[1]
    for i in range(2):
        out_ref[pl.ds(512 * i + 256 * core, 256)] = keep_ref[i]
        out_ref[pl.ds(512 * i + 256 * (1 - core), 256)] = got_ref[i]
    for j in range(4):
        out_ref[1024 + 128 * j : 1152 + 128 * j] = down_ref[:, 256 * j : 256 * j + 256]


def assemble(place, keep, got, down):
    return call(
        assemble_kernel, "assemble", 1_000_000, 2_000_000,
        in_specs=[SCALAR] + [VECTOR] * 3, out_shape=shape(1536, 256),
    )(place, keep, got, down)


def head_lanes_rope(head):
    lane = iota((1, 256), 1) % 128
    return (lane >= 32 * head) & (lane < 32 * head + 32)


def head_lanes(head):
    lane = iota((1, 256), 1)
    return (lane >= 64 * head) & (lane < 64 * head + 64)


def spread_queries():
    row, col = iota((256, 256), 0), iota((256, 256), 1)
    return row == ((col % 128) // 32) * 64 + (col // 128) * 32 + col % 32


def spread_keys():
    row, col = iota((128, 256), 0), iota((128, 256), 1)
    return row == ((col % 128) // 64) * 64 + (col // 128) * 32 + col % 32, (col % 64) < 32


def spread_values():
    row, col = iota((128, 256), 0), iota((128, 256), 1)
    return row == (col // 128) * 64 + col % 64, (col % 128) < 64


def positions(place_ref):
    ylo, core = place_ref[0], place_ref[1]
    return [(y, c, 2 * y + c) for c in (core, 1 - core) for y in (ylo, 1 - ylo)]


def normed(x):
    return x * lax.rsqrt(jnp.mean(x * x, axis=-1, keepdims=True) + epsilon)


def front_kernel(
    place_ref, x0_ref, x1_ref, x2_ref, x3_ref, w_ref, cos_ref, sin_ref,
    q_ref, k_ref, v_ref, o0_ref, o1_ref, o2_ref, o3_ref, lse_ref, h_ref, gains_ref, o_ref,
):
    gain = row_of(w_ref[:, 512:640].astype(f32)[:, 32:33])
    gains_ref[0:1] = gain
    gains_ref[1:2] = row_of(w_ref[:, 512:640].astype(f32)[:, 33:34])
    wq = dot(w_ref[:, :256], as_bf16(spread_queries())).astype(bf16)
    wk = dot(w_ref[:, 256:384], as_bf16(spread_keys()[0])).astype(bf16)
    wv = dot(w_ref[:, 384:512], as_bf16(spread_values()[0])).astype(bf16)
    for (_, _, at), x_ref in zip(positions(place_ref), (x0_ref, x1_ref, x2_ref, x3_ref)):
        rows = pl.ds(pl.multiple_of(256 * at, 256), 256)
        h = (normed(x_ref[...].astype(f32)) * gain).astype(bf16)
        h_ref[rows] = h
        c, s = cos_ref[rows], sin_ref[rows]
        for w, out in ((wq, q_ref), (wk, k_ref)):
            pre = dot(h, w)
            a, b = pre[:, :128], pre[:, 128:]
            out[rows] = jnp.concatenate([a * c - b * s, b * c + a * s], axis=1).astype(bf16)
        v_ref[rows] = dot(h, wv).astype(bf16)
    for i in range(4):
        rows = slice(256 * i, 256 * i + 256)
        n = 256 * (i + 1)
        seen = iota((256, n), 1) <= iota((256, n), 0) + 256 * i
        mixed = jnp.zeros((256, 256), f32)
        logs = jnp.zeros((256, 128), f32)
        for head in range(GROUP):
            q = q_ref[rows] * as_bf16(head_lanes_rope(head))
            scores = jnp.where(seen, dot(q, k_ref[:n], NT) * HEAD**-0.5, -1e30)
            peak = jnp.max(scores, axis=-1, keepdims=True)
            e = jnp.exp(scores - peak)
            total = jnp.sum(e, axis=-1, keepdims=True)
            probs = (e * (1.0 / total)).astype(bf16)
            mixed = mixed + dot(probs, v_ref[:n] * as_bf16(head_lanes(head)))
            logs = jnp.where(iota((256, 128), 1) == head, peak + jnp.log(total), logs)
        o_ref[i] = mixed.astype(bf16)
        lse_ref[rows] = logs
    for (_, _, at), out in zip(positions(place_ref), (o0_ref, o1_ref, o2_ref, o3_ref)):
        out[...] = o_ref[at]


def front(place, blocks, w, cos, sin):
    return call(
        front_kernel, "front", 8_000_000_000, 10_000_000,
        in_specs=[SCALAR] + [VECTOR] * 7,
        out_shape=(
            shape(LENGTH, 256), shape(LENGTH, 256), shape(LENGTH, 256), *[shape(TOK, 256)] * 4,
            shape(LENGTH, 128, dtype=f32), shape(LENGTH, D), shape(8, D, dtype=f32),
        ),
        scratch_shapes=[pltpu.VMEM((4, TOK, 256), bf16)],
    )(place, *blocks, w, cos, sin)


def output_blocks(own_ref, other_ref):
    return [ref[:, D * i : D * i + D] for ref in (own_ref, other_ref) for i in range(2)]


def mid_kernel(x_ref, m0_ref, m1_ref, m2_ref, m3_ref, own_ref, other_ref, gains_ref, residual_ref, h_ref):
    total = x_ref[...].astype(f32)
    for mixed_ref, w in zip((m0_ref, m1_ref, m2_ref, m3_ref), output_blocks(own_ref, other_ref)):
        total = total + dot(mixed_ref[...], w)
    residual_ref[...] = total
    h_ref[...] = (normed(total) * gains_ref[1:2]).astype(bf16)


def mid(x, mixed, own, other, gains):
    return call(
        mid_kernel, "mid", 1_000_000_000, 5_000_000,
        in_specs=[VECTOR] * 8,
        out_shape=(shape(TOK, D, dtype=f32), shape(TOK, D)),
    )(x, *mixed, own, other, gains)


def turn_kernel(
    place_ref, part0_ref, part1_ref, part2_ref, part3_ref, gy_ref, residual_ref, small_ref, gains_ref,
    m0_ref, m1_ref, m2_ref, m3_ref, own_ref, other_ref,
    do0_ref, do1_ref, do2_ref, do3_ref, grad_ref, keep_ref, send_ref, sums_ref,
):
    parts = (part0_ref, part1_ref, part2_ref, part3_ref)
    summed = sum(part[...].astype(f32) for part in parts)
    residual = residual_ref[...]
    factor = lax.rsqrt(jnp.mean(residual * residual, axis=-1, keepdims=True) + epsilon)
    normal = residual * factor
    gain = gains_ref[1:2]
    h = (normal * gain).astype(bf16)
    router = small_ref[:, 512 : 512 + EXPERTS]
    table = gate_table(dot(h, router), gy_ref[:, D:].astype(f32)[:, :EXPERTS])
    dgates = summed[:, D : D + EXPERTS]
    dlogits = (table * (dgates - jnp.sum(table * dgates, axis=-1, keepdims=True))).astype(bf16)
    dh = summed[:, :D] + dot(dlogits, router, NT)
    grad_gain = column_of(jnp.sum(dh * normal, axis=0, keepdims=True))
    grad_router = dot(h, dlogits, TN)
    sums = jnp.concatenate([grad_router, jnp.zeros((D, 128 - EXPERTS), f32)], axis=1)
    sums_ref[...] = jnp.where(iota((D, 128), 1) == 33, grad_gain, sums)
    scaled = dh * gain
    grad = gy_ref[:, :D].astype(f32) + factor * (scaled - normal * jnp.mean(scaled * normal, axis=-1, keepdims=True))
    grad_ref[...] = grad
    dz = grad.astype(bf16)
    mixed_refs, do_refs = (m0_ref, m1_ref, m2_ref, m3_ref), (do0_ref, do1_ref, do2_ref, do3_ref)
    for i, ((y, _, _), w) in enumerate(zip(positions(place_ref), output_blocks(own_ref, other_ref))):
        do_refs[i][...] = dot(dz, w, NT).astype(bf16)
        out = keep_ref if i < 2 else send_ref
        out[y] = dot(mixed_refs[i][...], dz, TN).astype(bf16)


def turn_back(place, parts, gy, residual, small, gains, mixed, own, other):
    pair = shape(2, TOK, D)
    return call(
        turn_kernel, "turn", 2_000_000_000, 10_000_000,
        in_specs=[SCALAR] + [VECTOR] * 14,
        out_shape=(*[shape(TOK, 256)] * 4, shape(TOK, D, dtype=f32), pair, pair, shape(D, 128, dtype=f32)),
    )(place, *parts, gy, residual, small, gains, *mixed, own, other)


def back_kernel(
    place_ref, q_ref, k_ref, v_ref, do0_ref, do1_ref, do2_ref, do3_ref, lse_ref, cos_ref, sin_ref, w_ref,
    x0_ref, x1_ref, x2_ref, x3_ref, out_ref, keep_ref, send_ref, gain_ref, do_ref, dk_ref, dv_ref,
):
    for (_, _, at), ref in zip(positions(place_ref), (do0_ref, do1_ref, do2_ref, do3_ref)):
        do_ref[at] = ref[...]
    dk_ref[...] = jnp.zeros_like(dk_ref)
    dv_ref[...] = jnp.zeros_like(dv_ref)
    scale = HEAD**-0.5
    place_queries = as_bf16(spread_queries())
    for i in range(4):
        rows = slice(256 * i, 256 * i + 256)
        n = 256 * (i + 1)
        seen = iota((256, n), 1) <= iota((256, n), 0) + 256 * i
        dq = jnp.zeros((256, 256), f32)
        for head in range(GROUP):
            lanes = head_lanes_rope(head)
            q = q_ref[rows] * as_bf16(lanes)
            do = do_ref[i] * as_bf16(head_lanes(head))
            scores = dot(q, k_ref[:n], NT) * scale - lse_ref[rows, head : head + 1]
            probs = jnp.where(seen, jnp.exp(jnp.where(seen, scores, 0.0)), 0.0)
            dprobs = dot(do, v_ref[:n], NT)
            row_dot = jnp.sum(probs * dprobs, axis=-1, keepdims=True)
            ds = (probs * (dprobs - row_dot)).astype(bf16)
            dq = dq + jnp.where(lanes, dot(ds, k_ref[:n]), 0.0)
            dk_ref[:n] += dot(ds, q, TN)
            dv_ref[:n] += dot(probs.astype(bf16), do, TN)
        c, s = cos_ref[rows], sin_ref[rows]
        a, b = dq[:, :128] * scale, dq[:, 128:] * scale
        dq = jnp.concatenate([a * c + b * s, b * c - a * s], axis=1).astype(bf16)
        out_ref[rows, :256] = dot(dq, place_queries, NT).astype(bf16)
    keep_keys, first_key = spread_keys()
    keep_values, first_value = spread_values()
    pick_keys = as_bf16(keep_keys & first_key)
    pick_values = as_bf16(keep_values & first_value)
    for i in range(4):
        rows = slice(256 * i, 256 * i + 256)
        c, s = cos_ref[rows], sin_ref[rows]
        a, b = dk_ref[rows, :128] * scale, dk_ref[rows, 128:] * scale
        a, b = a * c + b * s, b * c - a * s
        a, b = a + pltpu.roll(a, 96, 1), b + pltpu.roll(b, 96, 1)
        out_ref[rows, 256:384] = dot(jnp.concatenate([a, b], axis=1).astype(bf16), pick_keys, NT).astype(bf16)
        a, b = dv_ref[rows, :128], dv_ref[rows, 128:]
        a, b = a + pltpu.roll(a, 64, 1), b + pltpu.roll(b, 64, 1)
        out_ref[rows, 384:512] = dot(jnp.concatenate([a, b], axis=1).astype(bf16), pick_values, NT).astype(bf16)
    w = w_ref[:, :512]
    grad_gain = jnp.zeros((1, D), f32)
    for i, ((y, _, at), x_ref) in enumerate(zip(positions(place_ref), (x0_ref, x1_ref, x2_ref, x3_ref))):
        partial = dot(out_ref[pl.ds(pl.multiple_of(256 * at, 256), 256)], w, NT)
        grad_gain = grad_gain + jnp.sum(partial * normed(x_ref[...].astype(f32)), axis=0, keepdims=True)
        out = keep_ref if i < 2 else send_ref
        out[y] = partial.astype(bf16)
    gain_ref[...] = jnp.broadcast_to(grad_gain, (8, D))


def back(place, q, k, v, do, lse, cos, sin, w, blocks):
    pair = shape(2, TOK, D)
    return call(
        back_kernel, "back", 20_000_000_000, 16_000_000,
        in_specs=[SCALAR] + [VECTOR] * 15,
        out_shape=(shape(LENGTH, 512), pair, pair, shape(8, D, dtype=f32)),
        scratch_shapes=[
            pltpu.VMEM((4, TOK, 256), bf16), pltpu.VMEM((LENGTH, 256), f32), pltpu.VMEM((LENGTH, 256), f32),
        ],
    )(place, q, k, v, *do, lse, cos, sin, w, *blocks)


def projections_kernel(h_ref, dqkv_ref, sums_ref, gain_ref, first_ref):
    first_ref[:, :512] = dot(h_ref[...], dqkv_ref[...], TN).astype(bf16)
    small = jnp.where(iota((D, 128), 1) == 32, column_of(gain_ref[0:1]), sums_ref[...])
    first_ref[:, 512:] = small.astype(bf16)


def projections(h, dqkv, sums, gain):
    return call(
        projections_kernel, "projections", 1_500_000_000, 5_000_000, in_specs=[VECTOR] * 4, out_shape=shape(D, 640)
    )(h, dqkv, sums, gain)


def own_slots(expert, slot, z):
    start = ((expert % 16) // 4 * 2 + expert // 16) * CAP
    own = (expert % 4 == z) & (slot >= start) & (slot < start + CAP)
    return own, jnp.where(own, slot - start, 0)


def slot_tables(z, spread, start):
    own, place = own_slots(iota((EXPERTS, SLOTS), 0), iota((EXPERTS, SLOTS), 1), z)
    spread[...] = as_bf16(own)
    start[...] = jnp.sum(place, axis=0, keepdims=True).astype(f32)


SLOT_TABLES = [pltpu.VMEM((EXPERTS, SLOTS), bf16), pltpu.VMEM((1, SLOTS), f32)]


def gate_table(logits, codes):
    routed = codes >= 0
    logits = jnp.where(routed, logits, -1e30)
    e = jnp.where(routed, jnp.exp(logits - jnp.max(logits, axis=-1, keepdims=True)), 0.0)
    return e / jnp.sum(e, axis=-1, keepdims=True)


def whole(*shape):
    return pl.BlockSpec(shape, lambda e: (0,) * len(shape))


def per_expert(*shape):
    return pl.BlockSpec((1,) + shape, lambda e: (e,) + (0,) * len(shape))


def rows_kernel(n, with_gates, z_ref, *refs):
    i = pl.program_id(0)
    z = z_ref[0]
    values_refs, refs = refs[:n], refs[n:]
    if with_gates:
        codes_refs, router_ref, refs = refs[:n], refs[n], refs[n + 1 :]
        rows_ref, gates_ref, turn_ref, values, codes, own, start = refs[-7:]
    else:
        rows_ref, turn_ref, values, codes, own, start = refs[-6:]
    for b in range(n):

        @pl.when(i == b)
        def _():
            values[...] = values_refs[b][:, :D]
            codes[...] = codes_refs[b][...] if with_gates else values_refs[b][:, D:]

    @pl.when(i == 0)
    def _():
        turn_ref[...] = jnp.zeros_like(turn_ref)
        mine, offset = own_slots(iota((SLOTS, EXPERTS), 1), iota((SLOTS, EXPERTS), 0), z)
        own[...] = as_bf16(mine)
        start[...] = jnp.sum(offset, axis=1, keepdims=True).astype(f32)

    slots = codes[:, :EXPERTS]
    place = as_bf16(dot(own[...], slots, NT) == start[...])
    rows_ref[:, 0] = dot(place, values[...]).astype(bf16).reshape(SHARE, CAP, D)
    if with_gates:
        table = gate_table(dot(values[...], router_ref[:, :EXPERTS]), slots.astype(f32))
        gate = jnp.sum(dot(place, table.astype(bf16)) * own[...].astype(f32), axis=1, keepdims=True)
        gates_ref[:, 0] = gate.reshape(SHARE, CAP, 1)


def rows_of(z, first, blocks, codes, router, kept, turn):
    n, with_gates = len(blocks), router is not None
    args, specs = [z, *blocks], [SCALAR] + [whole(TOK, blocks[0].shape[1])] * n
    if with_gates:
        args += [*codes, router]
        specs += [pl.BlockSpec((TOK, 128), lambda e: (0, D // 128))] * n + [pl.BlockSpec((D, 128), lambda e: (0, 4))]
    args.append(turn)
    specs.append(ANYWHERE)
    widths = [(D, bf16)] + ([(1, f32)] if with_gates else [])
    out_specs = [pl.BlockSpec((SHARE, 1, CAP, w), lambda e: (0, first + e, 0, 0)) for w, _ in widths]
    out_shape = [shape(SHARE, BLOCKS, CAP, w, dtype=t) for w, t in widths]
    out_specs.append(whole(8, 128))
    out_shape.append(shape(8, 128, dtype=f32))
    aliases = {}
    if kept is not None:
        aliases = {len(args) + i: i for i in range(len(kept))}
        args += kept
        specs += [ANYWHERE] * len(kept)
    *kept, turn = call(
        functools.partial(rows_kernel, n, with_gates), "rows", n * 750_000_000, n * 2_000_000,
        grid=(n,), in_specs=specs, out_specs=out_specs, out_shape=out_shape, input_output_aliases=aliases,
        scratch_shapes=[
            pltpu.VMEM((TOK, D), bf16), pltpu.VMEM((TOK, 128), bf16), pltpu.VMEM((SLOTS, EXPERTS), bf16),
            pltpu.VMEM((SLOTS, 1), f32),
        ],
    )(*args)
    return kept, turn


def down_of(parts):
    return jnp.concatenate(
        [
            jnp.concatenate([parts[0, 128 * j : 128 * j + 128], parts[1, 128 * j : 128 * j + 128]], axis=0)
            for j in range(4)
        ],
        axis=1,
    )


def codes_specs():
    return [pl.BlockSpec((TOK, 128), lambda e: (0, D // 128))] * BLOCKS


PARTS = 2


def main_kernel(z_ref, x_ref, gy_ref, gate_ref, w_ref, *refs):
    codes_refs = refs[:8]
    act_ref, out_ref, own_ref, other_ref, kept, dgates, hidden, codes_kept, spread, start, mine = refs[8:]
    e = pl.program_id(0)

    @pl.when(e == 0)
    def _():
        for b in range(BLOCKS):
            codes_kept[b] = codes_refs[b][...]
        slot_tables(z_ref[0], spread, start)
        own, _ = own_slots(iota((SLOTS, EXPERTS), 1), iota((SLOTS, EXPERTS), 0), z_ref[0])
        mine[...] = own.astype(f32)

    down_w = down_of(w_ref[:, 1024:])
    gate_w = w_ref[:, :512].reshape(D, HALF)
    up_w = w_ref[:, 512:1024].reshape(D, HALF)
    both_w = jnp.concatenate([gate_w, up_w], axis=1)
    step = BLOCKS // PARTS
    for i in range(PARTS):
        blocks, rows = slice(step * i, step * i + step), slice(step * i * CAP, step * (i + 1) * CAP)
        x = x_ref[0, blocks].reshape(step * CAP, D)
        gate = gate_ref[0, blocks].reshape(step * CAP, 1)
        da = dot(gy_ref[0, blocks].reshape(step * CAP, D), down_w, NT)
        g = dot(x, gate_w)
        u = dot(x, up_w)
        s = jax.nn.sigmoid(g)
        silu = g * s
        act = silu * u
        dgates[blocks, e] = jnp.sum(act * da, axis=1, keepdims=True).reshape(step, CAP, 1)
        act_ref[0, rows] = (act * gate).astype(bf16)
        da = da * gate
        hidden[rows, :HALF] = (da * u * (s + silu * (1.0 - s))).astype(bf16)
        hidden[rows, HALF:] = (da * silu).astype(bf16)
        kept[blocks, e] = dot(hidden[rows], both_w, NT).astype(bf16).reshape(step, CAP, D)
    made = dot(hidden[...], x_ref[0].reshape(SLOTS, D), TN).astype(bf16)
    for i in range(2):
        out_ref[0, i, :512] = made[:, 512 * i : 512 * i + 512]
    made = dot(act_ref[0], gy_ref[0].reshape(SLOTS, D), TN).astype(bf16)
    for i in range(2):
        out_ref[0, i, 512:640] = made[128 * i : 128 * i + 128, :512]
        out_ref[0, i, 640:768] = made[128 * i : 128 * i + 128, 512:]

    @pl.when(e == SHARE - 1)
    def _():
        def pair(j, carry):
            for c, out in ((0, own_ref), (1, other_ref)):
                b = 2 * j + c
                place = as_bf16(dot(codes_kept[b][:, :EXPERTS], spread[...]) == start[...])
                out[j, :, :D] = dot(place, kept[b].reshape(SLOTS, D)).astype(bf16)
                scattered = dot(place, (mine[...] * dgates[b].reshape(SLOTS, 1)).astype(bf16))
                out[j, :, D:] = jnp.concatenate([scattered, jnp.zeros((TOK, 128 - EXPERTS), f32)], axis=1).astype(bf16)
            return carry

        lax.fori_loop(0, 4, pair, 0)


def main(z, x, gy, gates, weights, codes):
    back = shape(4, TOK, D + 128)
    return call(
        main_kernel, "experts", 25_000_000_000, 60_000_000,
        grid=(SHARE,),
        in_specs=[
            SCALAR, per_expert(BLOCKS, CAP, D), per_expert(BLOCKS, CAP, D), per_expert(BLOCKS, CAP, 1),
            pl.BlockSpec((2, 1536, 256), lambda e: (e, 0, 0)), *codes_specs(),
        ],
        out_specs=[
            per_expert(SLOTS, HALF), per_expert(2, 768, 512), whole(4, TOK, D + 128), whole(4, TOK, D + 128),
        ],
        out_shape=[shape(SHARE, SLOTS, HALF), shape(SHARE, 2, 768, 512), back, back],
        scratch_shapes=[
            pltpu.VMEM((BLOCKS, SHARE, CAP, D), bf16),
            pltpu.VMEM((BLOCKS, SHARE, CAP, 1), f32),
            pltpu.VMEM((SLOTS, 2 * HALF), bf16),
            pltpu.VMEM((BLOCKS, TOK, 128), bf16),
            *SLOT_TABLES,
            pltpu.VMEM((SLOTS, EXPERTS), f32),
        ],
    )(z, x, gy, gates, weights, *codes)


def outs_kernel(z_ref, act_ref, w_ref, *refs):
    codes_refs = refs[:8]
    own_ref, other_ref, kept, codes_kept, spread, start = refs[8:]
    e = pl.program_id(0)
    kept[:, e] = dot(act_ref[0], down_of(w_ref[...])).astype(bf16).reshape(BLOCKS, CAP, D)

    @pl.when(e == 0)
    def _():
        for b in range(BLOCKS):
            codes_kept[b] = codes_refs[b][...]
        slot_tables(z_ref[0], spread, start)

    @pl.when(e == SHARE - 1)
    def _():
        def pair(j, carry):
            for c, out in ((0, own_ref), (1, other_ref)):
                b = 2 * j + c
                place = as_bf16(dot(codes_kept[b][:, :EXPERTS], spread[...]) == start[...])
                out[j] = dot(place, kept[b].reshape(SLOTS, D)).astype(bf16)
            return carry

        lax.fori_loop(0, 4, pair, 0)


def outs(z, act, weights, codes):
    back = jax.ShapeDtypeStruct((4, TOK, D), bf16)
    return call(
        outs_kernel, "expert_outs", 6_000_000_000, 12_000_000,
        grid=(SHARE,),
        in_specs=[
            SCALAR, per_expert(SLOTS, HALF), pl.BlockSpec((2, 512, 256), lambda e: (e, 2, 0)), *codes_specs(),
        ],
        out_specs=[whole(4, TOK, D)] * 2,
        out_shape=[back, back],
        scratch_shapes=[
            pltpu.VMEM((BLOCKS, SHARE, CAP, D), bf16), pltpu.VMEM((BLOCKS, TOK, 128), bf16), *SLOT_TABLES,
        ],
    )(z, act, weights, *codes)


def finish_kernel(place_ref, mine_ref, got_ref, gate_ref, up_ref, down_ref):
    core = place_ref[1]
    for i, out in enumerate((gate_ref, up_ref)):
        for j in range(2):
            rows = slice(256 * i + 128 * j, 256 * i + 128 * j + 128)
            keep = mine_ref[rows, pl.ds(pl.multiple_of(256 * core, 256), 256)].astype(f32)
            out[:, pl.ds(pl.multiple_of(256 * j + 128 * core, 128), 128)] = keep.T
            got = got_ref[rows].astype(f32)
            out[:, pl.ds(pl.multiple_of(256 * j + 128 * (1 - core), 128), 128)] = got.T
    for j in range(2):
        down_ref[:, 512 * j : 512 * j + 512] = mine_ref[512 + 128 * j : 640 + 128 * j].astype(f32)


def finish(place, mine, got):
    return call(
        finish_kernel, "finish", 1_000_000, 4_000_000,
        in_specs=[SCALAR, VECTOR, VECTOR],
        out_shape=(shape(TOK, FF, dtype=f32), shape(TOK, FF, dtype=f32), shape(128, D, dtype=f32)),
    )(place, mine, got)


def shift(values, axis, by):
    n = 4 if axis in ("x", "z") else 2
    return lax.ppermute(values, axis, [(i, (i + by) % n) for i in range(n)])


def swap(values, axis):
    return shift(values, axis, 1)


def gather_z(values):
    return [values, shift(values, "z", 1), shift(values, "z", -1), shift(values, "z", 2)]


def with_core(blocks):
    return [(block, swap(block, "core")) for block in blocks]


def exchange_seq(own, across, beside, both):
    return [own, swap(across, "ylo"), swap(beside, "core"), swap(swap(both, "ylo"), "core")]


def core_sums(own, other):
    got = swap(other, "core")
    return [(own[j].astype(f32) + got[j].astype(f32)).astype(bf16) for j in range(4)]


def scatter_z(sums):
    return [sums[0], shift(sums[1], "z", -1), shift(sums[2], "z", 1), shift(sums[3], "z", 2)]


def fence(*values):
    return lax.optimization_barrier(values)


def on_device(
    tokens, norm1_gain, query_weight, key_weight, value_weight, output_weight, norm2_gain, router_weight,
    expert_gate, expert_up, expert_down, routes, cotangent,
):
    ylo, core = lax.axis_index("ylo"), lax.axis_index("core")
    z = lax.axis_index("z").astype(jnp.int32).reshape(1)
    place = jnp.stack([ylo, core]).astype(jnp.int32)

    own = tokens.reshape(TOK, D)
    across = swap(own, "ylo")
    gy_own = with_codes(routes.reshape(TOK, TOPK), cotangent.reshape(TOK, D))
    packed, keep, send = pack(
        place, query_weight, key_weight, value_weight, router_weight, norm1_gain.reshape(1, 8), norm2_gain.reshape(1, 8),
        expert_gate.reshape(TOK, FF), expert_up.reshape(TOK, FF),
    )

    lane = jnp.arange(128) % 32
    angles = jnp.arange(LENGTH).astype(f32)[:, None] * (rope_base ** (-2.0 * lane.astype(f32) / HEAD))[None, :]
    output_rows = jnp.concatenate([output_weight, swap(output_weight, "ylo")], axis=1)
    expert_w = assemble(place, keep, swap(send, "core"), expert_down.reshape(128, D))
    packed, across, cos, sin, gy_own, output_rows, expert_w = fence(
        packed, across, jnp.cos(angles), jnp.sin(angles), gy_own, output_rows, expert_w
    )
    arrived = lax.all_to_all(packed, AXES, split_axis=0, concat_axis=0, tiled=True).reshape(D, 640)
    gy_blocks = gather_z(gy_own)
    beside = swap(own, "core")

    expert_w, arrived, beside = fence(expert_w, arrived, beside)
    expert_w = lax.all_gather(expert_w, PLANE, axis=0).reshape(16, 1536, 256)

    blocks = [own, across, beside, swap(across, "core")]
    q, k, v, *mixed, lse, hidden_all, gains = front(place, blocks, arrived, cos, sin)

    output_own = lax.all_to_all(
        jnp.broadcast_to(output_rows[None], (32, 8, 2 * D)), FSDP, split_axis=0, concat_axis=0, tiled=True
    ).reshape(TOK, 2 * D)

    mixed = exchange_seq(*mixed)
    output_own, *rest = fence(output_own, *mixed, *gy_blocks)
    mixed, gy_blocks = rest[:4], rest[4:]
    output_other = swap(output_own, "core")
    gy_blocks = [block for pair in with_core(gy_blocks) for block in pair]
    residual, hidden_two = mid(own, mixed, output_own, output_other, gains)

    h_blocks = gather_z(hidden_two)
    turn, _ = fence(jnp.zeros((8, 128), f32), hidden_two)
    gy_rows, turn = rows_of(z, 0, gy_blocks, None, None, None, turn)
    rows, turn = rows_of(z, 0, (hidden_two, swap(hidden_two, "core")), gy_blocks[:2], arrived, None, turn)
    *h_blocks, turn = fence(*h_blocks, turn)
    h_blocks = [block for pair in with_core(h_blocks[1:]) for block in pair]
    rows, turn = rows_of(z, 2, h_blocks, gy_blocks[2:], arrived, rows, turn)
    (gy_rows,), (rows, gate_rows) = gy_rows, rows

    act, expert_grads, back_own, back_other = main(z, rows, gy_rows, gate_rows, expert_w, gy_blocks)
    sums = core_sums(back_own, back_other)
    parts = scatter_z(sums)
    moe_act, *_ = fence(act, *sums)
    moe_own, moe_other = outs(z, moe_act, expert_w, gy_blocks)
    expert_grads = lax.psum_scatter(expert_grads.reshape(16 * 768, 512), PLANE, scatter_dimension=0, tiled=True)

    moe_sums = core_sums(moe_own, moe_other)
    *do, grad_residual, keep, send, small = turn_back(
        place, parts, gy_own, residual, arrived, gains, mixed, output_own, output_other
    )

    do = exchange_seq(*do)
    grad_output_sum = (keep.astype(f32) + swap(send, "core").astype(f32)).astype(bf16).reshape(64, 8, D)
    grad_output_sum, *moe_sums = fence(grad_output_sum, *moe_sums)
    moe_near = [shift(moe_sums[1], "z", -1), shift(moe_sums[2], "z", 1)]
    grad_output = lax.all_to_all(grad_output_sum, ("ylo",) + FSDP, split_axis=0, concat_axis=0, tiled=True)
    dqkv, keep, send, gain = back(place, q, k, v, do, lse, cos, sin, arrived, blocks)
    dqkv, keep, send, own, grad_output, *moe_near = fence(dqkv, keep, send, own, grad_output, *moe_near)
    first = projections(hidden_all, dqkv, small, gain)

    away = jnp.where(core == 0, expert_grads[:512, 256:], expert_grads[:512, :256])
    finished = finish(place, expert_grads, swap(away, "core"))

    pair = (keep.astype(f32) + swap(send, "core").astype(f32)).astype(bf16)
    kept = jnp.where(ylo == 0, pair[0], pair[1])
    got = swap(jnp.where(ylo == 0, pair[1], pair[0]), "ylo")
    first = lax.all_to_all(first.reshape(128, 8, 640), AXES, split_axis=0, concat_axis=0, tiled=True)
    first, got, moe_far, grad_gate, grad_up, grad_down = fence(first, got, shift(moe_sums[3], "z", 2), *finished)
    grad_hidden_one = kept.astype(f32) + got.astype(f32)
    grad_output = jnp.sum(grad_output.astype(f32), axis=0)
    layer_out = sum(part.astype(f32) for part in (moe_sums[0], *moe_near, moe_far))
    layer_out = (residual + layer_out).astype(bf16).reshape(1, TOK, D)
    inputs = own.astype(f32)
    factor_one = lax.rsqrt(jnp.mean(inputs * inputs, axis=-1, keepdims=True) + epsilon)
    normed_one = inputs * factor_one
    scaled = grad_hidden_one * gains[0:1]
    grad_inputs = grad_residual + factor_one * (
        scaled - normed_one * jnp.mean(scaled * normed_one, axis=-1, keepdims=True)
    )

    first = jnp.sum(first.astype(f32).reshape(4, 32, 8, 640), axis=1)
    grad_query = first[:, :, :256].transpose(1, 0, 2).reshape(8, D)
    grad_key = first[:, :, 256:384].transpose(1, 0, 2).reshape(8, 512)
    grad_value = first[:, :, 384:512].transpose(1, 0, 2).reshape(8, 512)
    small = jnp.sum(first[:, :, 512:], axis=0)
    return (
        layer_out, grad_inputs.reshape(1, TOK, D), small[:, 32], grad_query, grad_key, grad_value, grad_output,
        small[:, 33], small[:, :EXPERTS], grad_gate.reshape(1, TOK, FF), grad_up.reshape(1, TOK, FF),
        grad_down.reshape(1, 128, D),
    )


def solution(mesh):
    fine = Mesh(mesh.devices.reshape(2, 2, 2, 4, 4), AXES)
    tok = P(FSDP, SEQ, None)
    row = P(AXES, None)
    vec = P(AXES)
    in_specs = (tok, vec, row, row, row, row, vec, row, tok, tok, tok, tok, tok)
    out_specs = (tok, tok, vec, row, row, row, row, vec, row, tok, tok, tok)
    return jax.shard_map(on_device, mesh=fine, in_specs=in_specs, out_specs=out_specs, check_vma=False)
```

```python
import functools

import jax
import jax.numpy as jnp
from jax import lax
from jax.experimental import pallas as pl
from jax.experimental.pallas import tpu as pltpu
from jax.sharding import Mesh
from jax.sharding import PartitionSpec as P

HEADS = 16
KV_HEADS = 8
HEAD = 64
TOPK = 8
CAP = 80
TOK = 256
D = 1024
FF = 512
EXPERTS = 32
SHARE = 8
SLOTS = SHARE * CAP
BLOCKS = 8
HALF = FF // 2
GROUP = 4
LENGTH = 1024

epsilon = 1e-06
rope_base = 10000.0

AXES = ("ylo", "core", "yhi", "x", "z")
SEQ = ("ylo", "core")
FSDP = ("yhi", "x", "z")
PLANE = ("x", "yhi", "ylo")

f32 = jnp.float32
bf16 = jnp.bfloat16

NT = (((1,), (1,)), ((), ()))
TN = (((0,), (0,)), ((), ()))
VMEM_LIMIT = 56 * 1024 * 1024


def dot(a, b, dims=(((1,), (0,)), ((), ()))):
    return lax.dot_general(a, b, dims, preferred_element_type=f32)


def iota(shape, axis):
    return lax.broadcasted_iota(jnp.int32, shape, axis)


def as_bf16(cond):
    return jnp.where(cond, 1.0, 0.0).astype(bf16)


def call(kernel, name, flops, moved, **kwargs):
    return pl.pallas_call(
        kernel,
        compiler_params=pltpu.CompilerParams(vmem_limit_bytes=VMEM_LIMIT),
        cost_estimate=pl.CostEstimate(flops=flops, bytes_accessed=moved, transcendentals=0),
        name=name,
        **kwargs,
    )


def shape(*dims, dtype=bf16):
    return jax.ShapeDtypeStruct(dims, dtype)


SCALAR = pl.BlockSpec(memory_space=pltpu.SMEM)
ANYWHERE = pl.BlockSpec(memory_space=pl.ANY)
VECTOR = pl.BlockSpec(memory_space=pltpu.VMEM)


def column_of(row):
    n = row.shape[1]
    step = min(n, 128)
    same = iota((step, step), 0) == iota((step, step), 1)
    parts = [jnp.sum(jnp.where(same, row[:, i : i + step], 0.0), axis=1, keepdims=True) for i in range(0, n, step)]
    return jnp.concatenate(parts, axis=0) if len(parts) > 1 else parts[0]


def row_of(column):
    n = column.shape[0]
    same = iota((128, 128), 0) == iota((128, 128), 1)
    parts = [jnp.sum(jnp.where(same, column[i : i + 128], 0.0), axis=0, keepdims=True) for i in range(0, n, 128)]
    return jnp.concatenate(parts, axis=1)


def codes_kernel(routes_ref, gy_ref, gy_out_ref):
    routes = routes_ref[...]
    expert = iota((TOK, EXPERTS), 1)
    chosen = jnp.zeros((TOK, EXPERTS), jnp.bool_)
    for i in range(TOPK):
        chosen = chosen | (routes[:, i : i + 1] == expert)
    earlier = as_bf16(iota((TOK, TOK), 1) < iota((TOK, TOK), 0))
    codes = jnp.where(chosen, dot(earlier, as_bf16(chosen)), -1.0)
    gy_out_ref[:, :D] = gy_ref[...]
    gy_out_ref[:, D:] = jnp.concatenate([codes, jnp.zeros((TOK, 128 - EXPERTS), f32)], axis=1).astype(bf16)


def with_codes(routes, gy):
    return call(
        codes_kernel, "codes", 50_000_000, 1_500_000, in_specs=[VECTOR] * 2, out_shape=shape(TOK, D + 128)
    )(routes, gy)


def pack_kernel(
    place_ref, query_ref, key_ref, value_ref, router_ref, one_ref, two_ref, gate_ref, up_ref,
    packed_ref, keep_ref, send_ref,
):
    core = place_ref[1]
    lane = iota((8, 128), 1)
    small = jnp.concatenate([router_ref[...].astype(f32), jnp.zeros((8, 96), f32)], axis=1)
    small = jnp.where(lane == 32, column_of(one_ref[...].astype(f32)), small)
    small = jnp.where(lane == 33, column_of(two_ref[...].astype(f32)), small).astype(bf16)
    for s in range(4):
        part = jnp.concatenate(
            [
                query_ref[:, 256 * s : 256 * s + 256],
                key_ref[:, 128 * s : 128 * s + 128],
                value_ref[:, 128 * s : 128 * s + 128],
                small,
            ],
            axis=1,
        )
        for f in range(32):
            packed_ref[32 * s + f] = part
    for i, ref in enumerate((gate_ref, up_ref)):
        for j in range(2):
            keep_ref[i, :, 128 * j : 128 * j + 128] = ref[:, pl.ds(256 * j + 128 * core, 128)]
            send_ref[i, :, 128 * j : 128 * j + 128] = ref[:, pl.ds(256 * j + 128 * (1 - core), 128)]


def pack(place, *args):
    return call(
        pack_kernel, "pack", 100_000_000, 4_000_000,
        in_specs=[SCALAR] + [VECTOR] * len(args),
        out_shape=(shape(128, 8, 640), shape(2, TOK, HALF), shape(2, TOK, HALF)),
    )(place, *args)


def assemble_kernel(place_ref, keep_ref, got_ref, down_ref, out_ref):
    core = place_ref[1]
    for i in range(2):
        out_ref[pl.ds(512 * i + 256 * core, 256)] = keep_ref[i]
        out_ref[pl.ds(512 * i + 256 * (1 - core), 256)] = got_ref[i]
    for j in range(4):
        out_ref[1024 + 128 * j : 1152 + 128 * j] = down_ref[:, 256 * j : 256 * j + 256]


def assemble(place, keep, got, down):
    return call(
        assemble_kernel, "assemble", 1_000_000, 2_000_000,
        in_specs=[SCALAR] + [VECTOR] * 3, out_shape=shape(1536, 256),
    )(place, keep, got, down)


def head_lanes_rope(head):
    lane = iota((1, 256), 1) % 128
    return (lane >= 32 * head) & (lane < 32 * head + 32)


def head_lanes(head):
    lane = iota((1, 256), 1)
    return (lane >= 64 * head) & (lane < 64 * head + 64)


def spread_queries():
    row, col = iota((256, 256), 0), iota((256, 256), 1)
    return row == ((col % 128) // 32) * 64 + (col // 128) * 32 + col % 32


def spread_keys():
    row, col = iota((128, 256), 0), iota((128, 256), 1)
    return row == ((col % 128) // 64) * 64 + (col // 128) * 32 + col % 32, (col % 64) < 32


def spread_values():
    row, col = iota((128, 256), 0), iota((128, 256), 1)
    return row == (col // 128) * 64 + col % 64, (col % 128) < 64


def positions(place_ref):
    ylo, core = place_ref[0], place_ref[1]
    return [(y, c, 2 * y + c) for c in (core, 1 - core) for y in (ylo, 1 - ylo)]


def normed(x):
    return x * lax.rsqrt(jnp.mean(x * x, axis=-1, keepdims=True) + epsilon)


def front_kernel(
    place_ref, x0_ref, x1_ref, x2_ref, x3_ref, w_ref, cos_ref, sin_ref,
    q_ref, k_ref, v_ref, o0_ref, o1_ref, o2_ref, o3_ref, lse_ref, h_ref, gains_ref, o_ref,
):
    gain = row_of(w_ref[:, 512:640].astype(f32)[:, 32:33])
    gains_ref[0:1] = gain
    gains_ref[1:2] = row_of(w_ref[:, 512:640].astype(f32)[:, 33:34])
    wq = dot(w_ref[:, :256], as_bf16(spread_queries())).astype(bf16)
    wk = dot(w_ref[:, 256:384], as_bf16(spread_keys()[0])).astype(bf16)
    wv = dot(w_ref[:, 384:512], as_bf16(spread_values()[0])).astype(bf16)
    for (_, _, at), x_ref in zip(positions(place_ref), (x0_ref, x1_ref, x2_ref, x3_ref)):
        rows = pl.ds(pl.multiple_of(256 * at, 256), 256)
        h = (normed(x_ref[...].astype(f32)) * gain).astype(bf16)
        h_ref[rows] = h
        c, s = cos_ref[rows], sin_ref[rows]
        for w, out in ((wq, q_ref), (wk, k_ref)):
            pre = dot(h, w)
            a, b = pre[:, :128], pre[:, 128:]
            out[rows] = jnp.concatenate([a * c - b * s, b * c + a * s], axis=1).astype(bf16)
        v_ref[rows] = dot(h, wv).astype(bf16)
    for i in range(4):
        rows = slice(256 * i, 256 * i + 256)
        n = 256 * (i + 1)
        seen = iota((256, n), 1) <= iota((256, n), 0) + 256 * i
        mixed = jnp.zeros((256, 256), f32)
        logs = jnp.zeros((256, 128), f32)
        for head in range(GROUP):
            q = q_ref[rows] * as_bf16(head_lanes_rope(head))
            scores = jnp.where(seen, dot(q, k_ref[:n], NT) * HEAD**-0.5, -1e30)
            peak = jnp.max(scores, axis=-1, keepdims=True)
            e = jnp.exp(scores - peak)
            total = jnp.sum(e, axis=-1, keepdims=True)
            probs = (e * (1.0 / total)).astype(bf16)
            mixed = mixed + dot(probs, v_ref[:n] * as_bf16(head_lanes(head)))
            logs = jnp.where(iota((256, 128), 1) == head, peak + jnp.log(total), logs)
        o_ref[i] = mixed.astype(bf16)
        lse_ref[rows] = logs
    for (_, _, at), out in zip(positions(place_ref), (o0_ref, o1_ref, o2_ref, o3_ref)):
        out[...] = o_ref[at]


def front(place, blocks, w, cos, sin):
    return call(
        front_kernel, "front", 8_000_000_000, 10_000_000,
        in_specs=[SCALAR] + [VECTOR] * 7,
        out_shape=(
            shape(LENGTH, 256), shape(LENGTH, 256), shape(LENGTH, 256), *[shape(TOK, 256)] * 4,
            shape(LENGTH, 128, dtype=f32), shape(LENGTH, D), shape(8, D, dtype=f32),
        ),
        scratch_shapes=[pltpu.VMEM((4, TOK, 256), bf16)],
    )(place, *blocks, w, cos, sin)


def output_blocks(own_ref, other_ref):
    return [ref[:, D * i : D * i + D] for ref in (own_ref, other_ref) for i in range(2)]


def mid_kernel(x_ref, m0_ref, m1_ref, m2_ref, m3_ref, own_ref, other_ref, gains_ref, residual_ref, h_ref):
    total = x_ref[...].astype(f32)
    for mixed_ref, w in zip((m0_ref, m1_ref, m2_ref, m3_ref), output_blocks(own_ref, other_ref)):
        total = total + dot(mixed_ref[...], w)
    residual_ref[...] = total
    h_ref[...] = (normed(total) * gains_ref[1:2]).astype(bf16)


def mid(x, mixed, own, other, gains):
    return call(
        mid_kernel, "mid", 1_000_000_000, 5_000_000,
        in_specs=[VECTOR] * 8,
        out_shape=(shape(TOK, D, dtype=f32), shape(TOK, D)),
    )(x, *mixed, own, other, gains)


def turn_kernel(
    place_ref, part0_ref, part1_ref, part2_ref, part3_ref, gy_ref, residual_ref, small_ref, gains_ref,
    m0_ref, m1_ref, m2_ref, m3_ref, own_ref, other_ref,
    do0_ref, do1_ref, do2_ref, do3_ref, grad_ref, keep_ref, send_ref, sums_ref,
):
    parts = (part0_ref, part1_ref, part2_ref, part3_ref)
    summed = sum(part[...].astype(f32) for part in parts)
    residual = residual_ref[...]
    factor = lax.rsqrt(jnp.mean(residual * residual, axis=-1, keepdims=True) + epsilon)
    normal = residual * factor
    gain = gains_ref[1:2]
    h = (normal * gain).astype(bf16)
    router = small_ref[:, 512 : 512 + EXPERTS]
    table = gate_table(dot(h, router), gy_ref[:, D:].astype(f32)[:, :EXPERTS])
    dgates = summed[:, D : D + EXPERTS]
    dlogits = (table * (dgates - jnp.sum(table * dgates, axis=-1, keepdims=True))).astype(bf16)
    dh = summed[:, :D] + dot(dlogits, router, NT)
    grad_gain = column_of(jnp.sum(dh * normal, axis=0, keepdims=True))
    grad_router = dot(h, dlogits, TN)
    sums = jnp.concatenate([grad_router, jnp.zeros((D, 128 - EXPERTS), f32)], axis=1)
    sums_ref[...] = jnp.where(iota((D, 128), 1) == 33, grad_gain, sums)
    scaled = dh * gain
    grad = gy_ref[:, :D].astype(f32) + factor * (scaled - normal * jnp.mean(scaled * normal, axis=-1, keepdims=True))
    grad_ref[...] = grad
    dz = grad.astype(bf16)
    mixed_refs, do_refs = (m0_ref, m1_ref, m2_ref, m3_ref), (do0_ref, do1_ref, do2_ref, do3_ref)
    for i, ((y, _, _), w) in enumerate(zip(positions(place_ref), output_blocks(own_ref, other_ref))):
        do_refs[i][...] = dot(dz, w, NT).astype(bf16)
        out = keep_ref if i < 2 else send_ref
        out[y] = dot(mixed_refs[i][...], dz, TN).astype(bf16)


def turn_back(place, parts, gy, residual, small, gains, mixed, own, other):
    pair = shape(2, TOK, D)
    return call(
        turn_kernel, "turn", 2_000_000_000, 10_000_000,
        in_specs=[SCALAR] + [VECTOR] * 14,
        out_shape=(*[shape(TOK, 256)] * 4, shape(TOK, D, dtype=f32), pair, pair, shape(D, 128, dtype=f32)),
    )(place, *parts, gy, residual, small, gains, *mixed, own, other)


def back_kernel(
    place_ref, q_ref, k_ref, v_ref, do0_ref, do1_ref, do2_ref, do3_ref, lse_ref, cos_ref, sin_ref, w_ref,
    x0_ref, x1_ref, x2_ref, x3_ref, out_ref, keep_ref, send_ref, gain_ref, do_ref, dk_ref, dv_ref,
):
    for (_, _, at), ref in zip(positions(place_ref), (do0_ref, do1_ref, do2_ref, do3_ref)):
        do_ref[at] = ref[...]
    dk_ref[...] = jnp.zeros_like(dk_ref)
    dv_ref[...] = jnp.zeros_like(dv_ref)
    scale = HEAD**-0.5
    place_queries = as_bf16(spread_queries())
    for i in range(4):
        rows = slice(256 * i, 256 * i + 256)
        n = 256 * (i + 1)
        seen = iota((256, n), 1) <= iota((256, n), 0) + 256 * i
        dq = jnp.zeros((256, 256), f32)
        for head in range(GROUP):
            lanes = head_lanes_rope(head)
            q = q_ref[rows] * as_bf16(lanes)
            do = do_ref[i] * as_bf16(head_lanes(head))
            scores = dot(q, k_ref[:n], NT) * scale - lse_ref[rows, head : head + 1]
            probs = jnp.where(seen, jnp.exp(jnp.where(seen, scores, 0.0)), 0.0)
            dprobs = dot(do, v_ref[:n], NT)
            row_dot = jnp.sum(probs * dprobs, axis=-1, keepdims=True)
            ds = (probs * (dprobs - row_dot)).astype(bf16)
            dq = dq + jnp.where(lanes, dot(ds, k_ref[:n]), 0.0)
            dk_ref[:n] += dot(ds, q, TN)
            dv_ref[:n] += dot(probs.astype(bf16), do, TN)
        c, s = cos_ref[rows], sin_ref[rows]
        a, b = dq[:, :128] * scale, dq[:, 128:] * scale
        dq = jnp.concatenate([a * c + b * s, b * c - a * s], axis=1).astype(bf16)
        out_ref[rows, :256] = dot(dq, place_queries, NT).astype(bf16)
    keep_keys, first_key = spread_keys()
    keep_values, first_value = spread_values()
    pick_keys = as_bf16(keep_keys & first_key)
    pick_values = as_bf16(keep_values & first_value)
    for i in range(4):
        rows = slice(256 * i, 256 * i + 256)
        c, s = cos_ref[rows], sin_ref[rows]
        a, b = dk_ref[rows, :128] * scale, dk_ref[rows, 128:] * scale
        a, b = a * c + b * s, b * c - a * s
        a, b = a + pltpu.roll(a, 96, 1), b + pltpu.roll(b, 96, 1)
        out_ref[rows, 256:384] = dot(jnp.concatenate([a, b], axis=1).astype(bf16), pick_keys, NT).astype(bf16)
        a, b = dv_ref[rows, :128], dv_ref[rows, 128:]
        a, b = a + pltpu.roll(a, 64, 1), b + pltpu.roll(b, 64, 1)
        out_ref[rows, 384:512] = dot(jnp.concatenate([a, b], axis=1).astype(bf16), pick_values, NT).astype(bf16)
    w = w_ref[:, :512]
    grad_gain = jnp.zeros((1, D), f32)
    for i, ((y, _, at), x_ref) in enumerate(zip(positions(place_ref), (x0_ref, x1_ref, x2_ref, x3_ref))):
        partial = dot(out_ref[pl.ds(pl.multiple_of(256 * at, 256), 256)], w, NT)
        grad_gain = grad_gain + jnp.sum(partial * normed(x_ref[...].astype(f32)), axis=0, keepdims=True)
        out = keep_ref if i < 2 else send_ref
        out[y] = partial.astype(bf16)
    gain_ref[...] = jnp.broadcast_to(grad_gain, (8, D))


def back(place, q, k, v, do, lse, cos, sin, w, blocks):
    pair = shape(2, TOK, D)
    return call(
        back_kernel, "back", 20_000_000_000, 16_000_000,
        in_specs=[SCALAR] + [VECTOR] * 15,
        out_shape=(shape(LENGTH, 512), pair, pair, shape(8, D, dtype=f32)),
        scratch_shapes=[
            pltpu.VMEM((4, TOK, 256), bf16), pltpu.VMEM((LENGTH, 256), f32), pltpu.VMEM((LENGTH, 256), f32),
        ],
    )(place, q, k, v, *do, lse, cos, sin, w, *blocks)


def projections_kernel(h_ref, dqkv_ref, sums_ref, gain_ref, first_ref):
    first_ref[:, :512] = dot(h_ref[...], dqkv_ref[...], TN).astype(bf16)
    small = jnp.where(iota((D, 128), 1) == 32, column_of(gain_ref[0:1]), sums_ref[...])
    first_ref[:, 512:] = small.astype(bf16)


def projections(h, dqkv, sums, gain):
    return call(
        projections_kernel, "projections", 1_500_000_000, 5_000_000, in_specs=[VECTOR] * 4, out_shape=shape(D, 640)
    )(h, dqkv, sums, gain)


def own_slots(expert, slot, z):
    start = ((expert % 16) // 4 * 2 + expert // 16) * CAP
    own = (expert % 4 == z) & (slot >= start) & (slot < start + CAP)
    return own, jnp.where(own, slot - start, 0)


def slot_tables(z, spread, start):
    own, place = own_slots(iota((EXPERTS, SLOTS), 0), iota((EXPERTS, SLOTS), 1), z)
    spread[...] = as_bf16(own)
    start[...] = jnp.sum(place, axis=0, keepdims=True).astype(f32)


SLOT_TABLES = [pltpu.VMEM((EXPERTS, SLOTS), bf16), pltpu.VMEM((1, SLOTS), f32)]


def gate_table(logits, codes):
    routed = codes >= 0
    logits = jnp.where(routed, logits, -1e30)
    e = jnp.where(routed, jnp.exp(logits - jnp.max(logits, axis=-1, keepdims=True)), 0.0)
    return e / jnp.sum(e, axis=-1, keepdims=True)


def whole(*shape):
    return pl.BlockSpec(shape, lambda e: (0,) * len(shape))


def per_expert(*shape):
    return pl.BlockSpec((1,) + shape, lambda e: (e,) + (0,) * len(shape))


def rows_kernel(n, with_gates, z_ref, *refs):
    i = pl.program_id(0)
    z = z_ref[0]
    values_refs, refs = refs[:n], refs[n:]
    if with_gates:
        codes_refs, router_ref, refs = refs[:n], refs[n], refs[n + 1 :]
        rows_ref, gates_ref, turn_ref, values, codes, own, start = refs[-7:]
    else:
        rows_ref, turn_ref, values, codes, own, start = refs[-6:]
    for b in range(n):

        @pl.when(i == b)
        def _():
            values[...] = values_refs[b][:, :D]
            codes[...] = codes_refs[b][...] if with_gates else values_refs[b][:, D:]

    @pl.when(i == 0)
    def _():
        turn_ref[...] = jnp.zeros_like(turn_ref)
        mine, offset = own_slots(iota((SLOTS, EXPERTS), 1), iota((SLOTS, EXPERTS), 0), z)
        own[...] = as_bf16(mine)
        start[...] = jnp.sum(offset, axis=1, keepdims=True).astype(f32)

    slots = codes[:, :EXPERTS]
    place = as_bf16(dot(own[...], slots, NT) == start[...])
    rows_ref[:, 0] = dot(place, values[...]).astype(bf16).reshape(SHARE, CAP, D)
    if with_gates:
        table = gate_table(dot(values[...], router_ref[:, :EXPERTS]), slots.astype(f32))
        gate = jnp.sum(dot(place, table.astype(bf16)) * own[...].astype(f32), axis=1, keepdims=True)
        gates_ref[:, 0] = gate.reshape(SHARE, CAP, 1)


def rows_of(z, first, blocks, codes, router, kept, turn):
    n, with_gates = len(blocks), router is not None
    args, specs = [z, *blocks], [SCALAR] + [whole(TOK, blocks[0].shape[1])] * n
    if with_gates:
        args += [*codes, router]
        specs += [pl.BlockSpec((TOK, 128), lambda e: (0, D // 128))] * n + [pl.BlockSpec((D, 128), lambda e: (0, 4))]
    args.append(turn)
    specs.append(ANYWHERE)
    widths = [(D, bf16)] + ([(1, f32)] if with_gates else [])
    out_specs = [pl.BlockSpec((SHARE, 1, CAP, w), lambda e: (0, first + e, 0, 0)) for w, _ in widths]
    out_shape = [shape(SHARE, BLOCKS, CAP, w, dtype=t) for w, t in widths]
    out_specs.append(whole(8, 128))
    out_shape.append(shape(8, 128, dtype=f32))
    aliases = {}
    if kept is not None:
        aliases = {len(args) + i: i for i in range(len(kept))}
        args += kept
        specs += [ANYWHERE] * len(kept)
    *kept, turn = call(
        functools.partial(rows_kernel, n, with_gates), "rows", n * 750_000_000, n * 2_000_000,
        grid=(n,), in_specs=specs, out_specs=out_specs, out_shape=out_shape, input_output_aliases=aliases,
        scratch_shapes=[
            pltpu.VMEM((TOK, D), bf16), pltpu.VMEM((TOK, 128), bf16), pltpu.VMEM((SLOTS, EXPERTS), bf16),
            pltpu.VMEM((SLOTS, 1), f32),
        ],
    )(*args)
    return kept, turn


def down_of(parts):
    return jnp.concatenate(
        [
            jnp.concatenate([parts[0, 128 * j : 128 * j + 128], parts[1, 128 * j : 128 * j + 128]], axis=0)
            for j in range(4)
        ],
        axis=1,
    )


def codes_specs():
    return [pl.BlockSpec((TOK, 128), lambda e: (0, D // 128))] * BLOCKS


PARTS = 2


def main_kernel(z_ref, x_ref, gy_ref, gate_ref, w_ref, *refs):
    codes_refs = refs[:8]
    act_ref, out_ref, own_ref, other_ref, kept, dgates, hidden, codes_kept, spread, start, mine = refs[8:]
    e = pl.program_id(0)

    @pl.when(e == 0)
    def _():
        for b in range(BLOCKS):
            codes_kept[b] = codes_refs[b][...]
        slot_tables(z_ref[0], spread, start)
        own, _ = own_slots(iota((SLOTS, EXPERTS), 1), iota((SLOTS, EXPERTS), 0), z_ref[0])
        mine[...] = own.astype(f32)

    down_w = down_of(w_ref[:, 1024:])
    gate_w = w_ref[:, :512].reshape(D, HALF)
    up_w = w_ref[:, 512:1024].reshape(D, HALF)
    both_w = jnp.concatenate([gate_w, up_w], axis=1)
    step = BLOCKS // PARTS
    for i in range(PARTS):
        blocks, rows = slice(step * i, step * i + step), slice(step * i * CAP, step * (i + 1) * CAP)
        x = x_ref[0, blocks].reshape(step * CAP, D)
        gate = gate_ref[0, blocks].reshape(step * CAP, 1)
        da = dot(gy_ref[0, blocks].reshape(step * CAP, D), down_w, NT)
        g = dot(x, gate_w)
        u = dot(x, up_w)
        s = jax.nn.sigmoid(g)
        silu = g * s
        act = silu * u
        dgates[blocks, e] = jnp.sum(act * da, axis=1, keepdims=True).reshape(step, CAP, 1)
        act_ref[0, rows] = (act * gate).astype(bf16)
        da = da * gate
        hidden[rows, :HALF] = (da * u * (s + silu * (1.0 - s))).astype(bf16)
        hidden[rows, HALF:] = (da * silu).astype(bf16)
        kept[blocks, e] = dot(hidden[rows], both_w, NT).astype(bf16).reshape(step, CAP, D)
    made = dot(hidden[...], x_ref[0].reshape(SLOTS, D), TN).astype(bf16)
    for i in range(2):
        out_ref[0, i, :512] = made[:, 512 * i : 512 * i + 512]
    made = dot(act_ref[0], gy_ref[0].reshape(SLOTS, D), TN).astype(bf16)
    for i in range(2):
        out_ref[0, i, 512:640] = made[128 * i : 128 * i + 128, :512]
        out_ref[0, i, 640:768] = made[128 * i : 128 * i + 128, 512:]

    @pl.when(e == SHARE - 1)
    def _():
        def pair(j, carry):
            for c, out in ((0, own_ref), (1, other_ref)):
                b = 2 * j + c
                place = as_bf16(dot(codes_kept[b][:, :EXPERTS], spread[...]) == start[...])
                out[j, :, :D] = dot(place, kept[b].reshape(SLOTS, D)).astype(bf16)
                scattered = dot(place, (mine[...] * dgates[b].reshape(SLOTS, 1)).astype(bf16))
                out[j, :, D:] = jnp.concatenate([scattered, jnp.zeros((TOK, 128 - EXPERTS), f32)], axis=1).astype(bf16)
            return carry

        lax.fori_loop(0, 4, pair, 0)


def main(z, x, gy, gates, weights, codes):
    back = shape(4, TOK, D + 128)
    return call(
        main_kernel, "experts", 25_000_000_000, 60_000_000,
        grid=(SHARE,),
        in_specs=[
            SCALAR, per_expert(BLOCKS, CAP, D), per_expert(BLOCKS, CAP, D), per_expert(BLOCKS, CAP, 1),
            pl.BlockSpec((2, 1536, 256), lambda e: (e, 0, 0)), *codes_specs(),
        ],
        out_specs=[
            per_expert(SLOTS, HALF), per_expert(2, 768, 512), whole(4, TOK, D + 128), whole(4, TOK, D + 128),
        ],
        out_shape=[shape(SHARE, SLOTS, HALF), shape(SHARE, 2, 768, 512), back, back],
        scratch_shapes=[
            pltpu.VMEM((BLOCKS, SHARE, CAP, D), bf16),
            pltpu.VMEM((BLOCKS, SHARE, CAP, 1), f32),
            pltpu.VMEM((SLOTS, 2 * HALF), bf16),
            pltpu.VMEM((BLOCKS, TOK, 128), bf16),
            *SLOT_TABLES,
            pltpu.VMEM((SLOTS, EXPERTS), f32),
        ],
    )(z, x, gy, gates, weights, *codes)


def outs_kernel(z_ref, act_ref, w_ref, *refs):
    codes_refs = refs[:8]
    own_ref, other_ref, kept, codes_kept, spread, start = refs[8:]
    e = pl.program_id(0)
    kept[:, e] = dot(act_ref[0], down_of(w_ref[...])).astype(bf16).reshape(BLOCKS, CAP, D)

    @pl.when(e == 0)
    def _():
        for b in range(BLOCKS):
            codes_kept[b] = codes_refs[b][...]
        slot_tables(z_ref[0], spread, start)

    @pl.when(e == SHARE - 1)
    def _():
        def pair(j, carry):
            for c, out in ((0, own_ref), (1, other_ref)):
                b = 2 * j + c
                place = as_bf16(dot(codes_kept[b][:, :EXPERTS], spread[...]) == start[...])
                out[j] = dot(place, kept[b].reshape(SLOTS, D)).astype(bf16)
            return carry

        lax.fori_loop(0, 4, pair, 0)


def outs(z, act, weights, codes):
    back = jax.ShapeDtypeStruct((4, TOK, D), bf16)
    return call(
        outs_kernel, "expert_outs", 6_000_000_000, 12_000_000,
        grid=(SHARE,),
        in_specs=[
            SCALAR, per_expert(SLOTS, HALF), pl.BlockSpec((2, 512, 256), lambda e: (e, 2, 0)), *codes_specs(),
        ],
        out_specs=[whole(4, TOK, D)] * 2,
        out_shape=[back, back],
        scratch_shapes=[
            pltpu.VMEM((BLOCKS, SHARE, CAP, D), bf16), pltpu.VMEM((BLOCKS, TOK, 128), bf16), *SLOT_TABLES,
        ],
    )(z, act, weights, *codes)


def finish_kernel(place_ref, mine_ref, got_ref, gate_ref, up_ref, down_ref):
    core = place_ref[1]
    for i, out in enumerate((gate_ref, up_ref)):
        for j in range(2):
            rows = slice(256 * i + 128 * j, 256 * i + 128 * j + 128)
            keep = mine_ref[rows, pl.ds(pl.multiple_of(256 * core, 256), 256)].astype(f32)
            out[:, pl.ds(pl.multiple_of(256 * j + 128 * core, 128), 128)] = keep.T
            got = got_ref[rows].astype(f32)
            out[:, pl.ds(pl.multiple_of(256 * j + 128 * (1 - core), 128), 128)] = got.T
    for j in range(2):
        down_ref[:, 512 * j : 512 * j + 512] = mine_ref[512 + 128 * j : 640 + 128 * j].astype(f32)


def finish(place, mine, got):
    return call(
        finish_kernel, "finish", 1_000_000, 4_000_000,
        in_specs=[SCALAR, VECTOR, VECTOR],
        out_shape=(shape(TOK, FF, dtype=f32), shape(TOK, FF, dtype=f32), shape(128, D, dtype=f32)),
    )(place, mine, got)


def shift(values, axis, by):
    n = 4 if axis in ("x", "z") else 2
    return lax.ppermute(values, axis, [(i, (i + by) % n) for i in range(n)])


def swap(values, axis):
    return shift(values, axis, 1)


def gather_z(values):
    return [values, shift(values, "z", 1), shift(values, "z", -1), shift(values, "z", 2)]


def with_core(blocks):
    return [(block, swap(block, "core")) for block in blocks]


def exchange_seq(own, across, beside, both):
    return [own, swap(across, "ylo"), swap(beside, "core"), swap(swap(both, "ylo"), "core")]


def core_sums(own, other):
    got = swap(other, "core")
    return [(own[j].astype(f32) + got[j].astype(f32)).astype(bf16) for j in range(4)]


def scatter_z(sums):
    return [sums[0], shift(sums[1], "z", -1), shift(sums[2], "z", 1), shift(sums[3], "z", 2)]


def fence(*values):
    return lax.optimization_barrier(values)


def on_device(
    tokens, norm1_gain, query_weight, key_weight, value_weight, output_weight, norm2_gain, router_weight,
    expert_gate, expert_up, expert_down, routes, cotangent,
):
    ylo, core = lax.axis_index("ylo"), lax.axis_index("core")
    z = lax.axis_index("z").astype(jnp.int32).reshape(1)
    place = jnp.stack([ylo, core]).astype(jnp.int32)

    own = tokens.reshape(TOK, D)
    across = swap(own, "ylo")
    gy_own = with_codes(routes.reshape(TOK, TOPK), cotangent.reshape(TOK, D))
    packed, keep, send = pack(
        place, query_weight, key_weight, value_weight, router_weight, norm1_gain.reshape(1, 8), norm2_gain.reshape(1, 8),
        expert_gate.reshape(TOK, FF), expert_up.reshape(TOK, FF),
    )

    expert_w = assemble(place, keep, swap(send, "core"), expert_down.reshape(128, D))
    lane = jnp.arange(128) % 32
    angles = jnp.arange(LENGTH).astype(f32)[:, None] * (rope_base ** (-2.0 * lane.astype(f32) / HEAD))[None, :]
    expert_w, packed, across, cos, sin = fence(expert_w, packed, across, jnp.cos(angles), jnp.sin(angles))
    expert_w = lax.all_gather(expert_w, PLANE, axis=0).reshape(16, 1536, 256)

    arrived = lax.all_to_all(packed, AXES, split_axis=0, concat_axis=0, tiled=True).reshape(D, 640)
    output_rows = jnp.concatenate([output_weight, swap(output_weight, "ylo")], axis=1)
    gy_blocks = gather_z(gy_own)
    arrived, output_rows, *near = fence(arrived, output_rows, *gy_blocks[1:3])
    gy_blocks[1:3] = near
    beside = swap(own, "core")

    blocks = [own, across, beside, swap(across, "core")]
    q, k, v, *mixed, lse, hidden_all, gains = front(place, blocks, arrived, cos, sin)

    output_own = lax.all_to_all(
        jnp.broadcast_to(output_rows[None], (32, 8, 2 * D)), FSDP, split_axis=0, concat_axis=0, tiled=True
    ).reshape(TOK, 2 * D)

    mixed = exchange_seq(*mixed)
    output_own, *rest = fence(output_own, *mixed, *gy_blocks)
    mixed, gy_blocks = rest[:4], rest[4:]
    output_other = swap(output_own, "core")
    gy_blocks = [block for pair in with_core(gy_blocks) for block in pair]
    residual, hidden_two = mid(own, mixed, output_own, output_other, gains)

    near = [shift(hidden_two, "z", 1), shift(hidden_two, "z", -1)]
    turn, _ = fence(jnp.zeros((8, 128), f32), hidden_two)
    gy_rows, turn = rows_of(z, 0, gy_blocks, None, None, None, turn)
    *near, far, turn = fence(*near, hidden_two, turn)
    far = shift(far, "z", 2)
    rows, turn = rows_of(z, 0, (hidden_two, swap(hidden_two, "core")), gy_blocks[:2], arrived, None, turn)
    near = [block for pair in with_core(near) for block in pair]
    rows, turn = rows_of(z, 2, near, gy_blocks[2:6], arrived, rows, turn)
    far, turn = fence(far, turn)
    rows, turn = rows_of(z, 6, (far, swap(far, "core")), gy_blocks[6:], arrived, rows, turn)
    (gy_rows,), (rows, gate_rows) = gy_rows, rows

    act, expert_grads, back_own, back_other = main(z, rows, gy_rows, gate_rows, expert_w, gy_blocks)
    sums = core_sums(back_own, back_other)
    parts = scatter_z(sums)
    moe_act, *_ = fence(act, *sums)
    moe_own, moe_other = outs(z, moe_act, expert_w, gy_blocks)
    expert_grads = lax.psum_scatter(expert_grads.reshape(16 * 768, 512), PLANE, scatter_dimension=0, tiled=True)

    moe_sums = core_sums(moe_own, moe_other)
    *do, grad_residual, keep, send, small = turn_back(
        place, parts, gy_own, residual, arrived, gains, mixed, output_own, output_other
    )

    do = exchange_seq(*do)
    grad_output_sum = (keep.astype(f32) + swap(send, "core").astype(f32)).astype(bf16).reshape(64, 8, D)
    grad_output_sum, *moe_sums = fence(grad_output_sum, *moe_sums)
    moe_near = [shift(moe_sums[1], "z", -1), shift(moe_sums[2], "z", 1)]
    grad_output = lax.all_to_all(grad_output_sum, ("ylo",) + FSDP, split_axis=0, concat_axis=0, tiled=True)
    dqkv, keep, send, gain = back(place, q, k, v, do, lse, cos, sin, arrived, blocks)
    dqkv, keep, send, own, grad_output, *moe_near = fence(dqkv, keep, send, own, grad_output, *moe_near)
    first = projections(hidden_all, dqkv, small, gain)

    away = jnp.where(core == 0, expert_grads[:512, 256:], expert_grads[:512, :256])
    finished = finish(place, expert_grads, swap(away, "core"))

    pair = (keep.astype(f32) + swap(send, "core").astype(f32)).astype(bf16)
    kept = jnp.where(ylo == 0, pair[0], pair[1])
    got = swap(jnp.where(ylo == 0, pair[1], pair[0]), "ylo")
    first = lax.all_to_all(first.reshape(128, 8, 640), AXES, split_axis=0, concat_axis=0, tiled=True)
    first, got, moe_far, grad_gate, grad_up, grad_down = fence(first, got, shift(moe_sums[3], "z", 2), *finished)
    grad_hidden_one = kept.astype(f32) + got.astype(f32)
    grad_output = jnp.sum(grad_output.astype(f32), axis=0)
    layer_out = sum(part.astype(f32) for part in (moe_sums[0], *moe_near, moe_far))
    layer_out = (residual + layer_out).astype(bf16).reshape(1, TOK, D)
    inputs = own.astype(f32)
    factor_one = lax.rsqrt(jnp.mean(inputs * inputs, axis=-1, keepdims=True) + epsilon)
    normed_one = inputs * factor_one
    scaled = grad_hidden_one * gains[0:1]
    grad_inputs = grad_residual + factor_one * (
        scaled - normed_one * jnp.mean(scaled * normed_one, axis=-1, keepdims=True)
    )

    first = jnp.sum(first.astype(f32).reshape(4, 32, 8, 640), axis=1)
    grad_query = first[:, :, :256].transpose(1, 0, 2).reshape(8, D)
    grad_key = first[:, :, 256:384].transpose(1, 0, 2).reshape(8, 512)
    grad_value = first[:, :, 384:512].transpose(1, 0, 2).reshape(8, 512)
    small = jnp.sum(first[:, :, 512:], axis=0)
    return (
        layer_out, grad_inputs.reshape(1, TOK, D), small[:, 32], grad_query, grad_key, grad_value, grad_output,
        small[:, 33], small[:, :EXPERTS], grad_gate.reshape(1, TOK, FF), grad_up.reshape(1, TOK, FF),
        grad_down.reshape(1, 128, D),
    )


def solution(mesh):
    fine = Mesh(mesh.devices.reshape(2, 2, 2, 4, 4), AXES)
    tok = P(FSDP, SEQ, None)
    row = P(AXES, None)
    vec = P(AXES)
    in_specs = (tok, vec, row, row, row, row, vec, row, tok, tok, tok, tok, tok)
    out_specs = (tok, tok, vec, row, row, row, row, vec, row, tok, tok, tok)
    return jax.shard_map(on_device, mesh=fine, in_specs=in_specs, out_specs=out_specs, check_vma=False)
```

```python
import functools

import jax
import jax.numpy as jnp
from jax import lax
from jax.experimental import pallas as pl
from jax.experimental.pallas import tpu as pltpu
from jax.sharding import Mesh
from jax.sharding import PartitionSpec as P

HEADS = 16
KV_HEADS = 8
HEAD = 64
TOPK = 8
CAP = 80
TOK = 256
D = 1024
FF = 512
EXPERTS = 32
SHARE = 8
SLOTS = SHARE * CAP
BLOCKS = 8
HALF = FF // 2
GROUP = 4
LENGTH = 1024

epsilon = 1e-06
rope_base = 10000.0

AXES = ("ylo", "core", "yhi", "x", "z")
SEQ = ("ylo", "core")
FSDP = ("yhi", "x", "z")
PLANE = ("x", "yhi", "ylo")

f32 = jnp.float32
bf16 = jnp.bfloat16

NT = (((1,), (1,)), ((), ()))
TN = (((0,), (0,)), ((), ()))
VMEM_LIMIT = 56 * 1024 * 1024


def dot(a, b, dims=(((1,), (0,)), ((), ()))):
    return lax.dot_general(a, b, dims, preferred_element_type=f32)


def iota(shape, axis):
    return lax.broadcasted_iota(jnp.int32, shape, axis)


def as_bf16(cond):
    return jnp.where(cond, 1.0, 0.0).astype(bf16)


def call(kernel, name, flops, moved, **kwargs):
    return pl.pallas_call(
        kernel,
        compiler_params=pltpu.CompilerParams(vmem_limit_bytes=VMEM_LIMIT),
        cost_estimate=pl.CostEstimate(flops=flops, bytes_accessed=moved, transcendentals=0),
        name=name,
        **kwargs,
    )


def shape(*dims, dtype=bf16):
    return jax.ShapeDtypeStruct(dims, dtype)


SCALAR = pl.BlockSpec(memory_space=pltpu.SMEM)
ANYWHERE = pl.BlockSpec(memory_space=pl.ANY)
VECTOR = pl.BlockSpec(memory_space=pltpu.VMEM)


def column_of(row):
    n = row.shape[1]
    step = min(n, 128)
    same = iota((step, step), 0) == iota((step, step), 1)
    parts = [jnp.sum(jnp.where(same, row[:, i : i + step], 0.0), axis=1, keepdims=True) for i in range(0, n, step)]
    return jnp.concatenate(parts, axis=0) if len(parts) > 1 else parts[0]


def row_of(column):
    n = column.shape[0]
    same = iota((128, 128), 0) == iota((128, 128), 1)
    parts = [jnp.sum(jnp.where(same, column[i : i + 128], 0.0), axis=0, keepdims=True) for i in range(0, n, 128)]
    return jnp.concatenate(parts, axis=1)


def codes_kernel(routes_ref, gy_ref, gy_out_ref):
    routes = routes_ref[...]
    expert = iota((TOK, EXPERTS), 1)
    chosen = jnp.zeros((TOK, EXPERTS), jnp.bool_)
    for i in range(TOPK):
        chosen = chosen | (routes[:, i : i + 1] == expert)
    earlier = as_bf16(iota((TOK, TOK), 1) < iota((TOK, TOK), 0))
    codes = jnp.where(chosen, dot(earlier, as_bf16(chosen)), -1.0)
    gy_out_ref[:, :D] = gy_ref[...]
    gy_out_ref[:, D:] = jnp.concatenate([codes, jnp.zeros((TOK, 128 - EXPERTS), f32)], axis=1).astype(bf16)


def with_codes(routes, gy):
    return call(
        codes_kernel, "codes", 50_000_000, 1_500_000, in_specs=[VECTOR] * 2, out_shape=shape(TOK, D + 128)
    )(routes, gy)


def pack_kernel(
    place_ref, query_ref, key_ref, value_ref, router_ref, one_ref, two_ref, gate_ref, up_ref,
    packed_ref, keep_ref, send_ref,
):
    core = place_ref[1]
    lane = iota((8, 128), 1)
    small = jnp.concatenate([router_ref[...].astype(f32), jnp.zeros((8, 96), f32)], axis=1)
    small = jnp.where(lane == 32, column_of(one_ref[...].astype(f32)), small)
    small = jnp.where(lane == 33, column_of(two_ref[...].astype(f32)), small).astype(bf16)
    for s in range(4):
        part = jnp.concatenate(
            [
                query_ref[:, 256 * s : 256 * s + 256],
                key_ref[:, 128 * s : 128 * s + 128],
                value_ref[:, 128 * s : 128 * s + 128],
                small,
            ],
            axis=1,
        )
        for f in range(32):
            packed_ref[32 * s + f] = part
    for i, ref in enumerate((gate_ref, up_ref)):
        for j in range(2):
            keep_ref[i, :, 128 * j : 128 * j + 128] = ref[:, pl.ds(256 * j + 128 * core, 128)]
            send_ref[i, :, 128 * j : 128 * j + 128] = ref[:, pl.ds(256 * j + 128 * (1 - core), 128)]


def pack(place, *args):
    return call(
        pack_kernel, "pack", 100_000_000, 4_000_000,
        in_specs=[SCALAR] + [VECTOR] * len(args),
        out_shape=(shape(128, 8, 640), shape(2, TOK, HALF), shape(2, TOK, HALF)),
    )(place, *args)


def assemble_kernel(place_ref, keep_ref, got_ref, down_ref, out_ref):
    core = place_ref[1]
    for i in range(2):
        out_ref[pl.ds(512 * i + 256 * core, 256)] = keep_ref[i]
        out_ref[pl.ds(512 * i + 256 * (1 - core), 256)] = got_ref[i]
    for j in range(4):
        out_ref[1024 + 128 * j : 1152 + 128 * j] = down_ref[:, 256 * j : 256 * j + 256]


def assemble(place, keep, got, down):
    return call(
        assemble_kernel, "assemble", 1_000_000, 2_000_000,
        in_specs=[SCALAR] + [VECTOR] * 3, out_shape=shape(1536, 256),
    )(place, keep, got, down)


def head_lanes_rope(head):
    lane = iota((1, 256), 1) % 128
    return (lane >= 32 * head) & (lane < 32 * head + 32)


def head_lanes(head):
    lane = iota((1, 256), 1)
    return (lane >= 64 * head) & (lane < 64 * head + 64)


def spread_queries():
    row, col = iota((256, 256), 0), iota((256, 256), 1)
    return row == ((col % 128) // 32) * 64 + (col // 128) * 32 + col % 32


def spread_keys():
    row, col = iota((128, 256), 0), iota((128, 256), 1)
    return row == ((col % 128) // 64) * 64 + (col // 128) * 32 + col % 32, (col % 64) < 32


def spread_values():
    row, col = iota((128, 256), 0), iota((128, 256), 1)
    return row == (col // 128) * 64 + col % 64, (col % 128) < 64


def positions(place_ref):
    ylo, core = place_ref[0], place_ref[1]
    return [(y, c, 2 * y + c) for c in (core, 1 - core) for y in (ylo, 1 - ylo)]


def normed(x):
    return x * lax.rsqrt(jnp.mean(x * x, axis=-1, keepdims=True) + epsilon)


def front_kernel(
    place_ref, x0_ref, x1_ref, x2_ref, x3_ref, w_ref, cos_ref, sin_ref,
    q_ref, k_ref, v_ref, o0_ref, o1_ref, o2_ref, o3_ref, lse_ref, h_ref, gains_ref, o_ref,
):
    gain = row_of(w_ref[:, 512:640].astype(f32)[:, 32:33])
    gains_ref[0:1] = gain
    gains_ref[1:2] = row_of(w_ref[:, 512:640].astype(f32)[:, 33:34])
    wq = dot(w_ref[:, :256], as_bf16(spread_queries())).astype(bf16)
    wk = dot(w_ref[:, 256:384], as_bf16(spread_keys()[0])).astype(bf16)
    wv = dot(w_ref[:, 384:512], as_bf16(spread_values()[0])).astype(bf16)
    for (_, _, at), x_ref in zip(positions(place_ref), (x0_ref, x1_ref, x2_ref, x3_ref)):
        rows = pl.ds(pl.multiple_of(256 * at, 256), 256)
        h = (normed(x_ref[...].astype(f32)) * gain).astype(bf16)
        h_ref[rows] = h
        c, s = cos_ref[rows], sin_ref[rows]
        for w, out in ((wq, q_ref), (wk, k_ref)):
            pre = dot(h, w)
            a, b = pre[:, :128], pre[:, 128:]
            out[rows] = jnp.concatenate([a * c - b * s, b * c + a * s], axis=1).astype(bf16)
        v_ref[rows] = dot(h, wv).astype(bf16)
    for i in range(4):
        rows = slice(256 * i, 256 * i + 256)
        n = 256 * (i + 1)
        seen = iota((256, n), 1) <= iota((256, n), 0) + 256 * i
        mixed = jnp.zeros((256, 256), f32)
        logs = jnp.zeros((256, 128), f32)
        for head in range(GROUP):
            q = q_ref[rows] * as_bf16(head_lanes_rope(head))
            scores = jnp.where(seen, dot(q, k_ref[:n], NT) * HEAD**-0.5, -1e30)
            peak = jnp.max(scores, axis=-1, keepdims=True)
            e = jnp.exp(scores - peak)
            total = jnp.sum(e, axis=-1, keepdims=True)
            probs = (e * (1.0 / total)).astype(bf16)
            mixed = mixed + dot(probs, v_ref[:n] * as_bf16(head_lanes(head)))
            logs = jnp.where(iota((256, 128), 1) == head, peak + jnp.log(total), logs)
        o_ref[i] = mixed.astype(bf16)
        lse_ref[rows] = logs
    for (_, _, at), out in zip(positions(place_ref), (o0_ref, o1_ref, o2_ref, o3_ref)):
        out[...] = o_ref[at]


def front(place, blocks, w, cos, sin):
    return call(
        front_kernel, "front", 8_000_000_000, 10_000_000,
        in_specs=[SCALAR] + [VECTOR] * 7,
        out_shape=(
            shape(LENGTH, 256), shape(LENGTH, 256), shape(LENGTH, 256), *[shape(TOK, 256)] * 4,
            shape(LENGTH, 128, dtype=f32), shape(LENGTH, D), shape(8, D, dtype=f32),
        ),
        scratch_shapes=[pltpu.VMEM((4, TOK, 256), bf16)],
    )(place, *blocks, w, cos, sin)


def output_blocks(own_ref, other_ref):
    return [ref[:, D * i : D * i + D] for ref in (own_ref, other_ref) for i in range(2)]


def mid_kernel(x_ref, m0_ref, m1_ref, m2_ref, m3_ref, own_ref, other_ref, gains_ref, residual_ref, h_ref):
    total = x_ref[...].astype(f32)
    for mixed_ref, w in zip((m0_ref, m1_ref, m2_ref, m3_ref), output_blocks(own_ref, other_ref)):
        total = total + dot(mixed_ref[...], w)
    residual_ref[...] = total
    h_ref[...] = (normed(total) * gains_ref[1:2]).astype(bf16)


def mid(x, mixed, own, other, gains):
    return call(
        mid_kernel, "mid", 1_000_000_000, 5_000_000,
        in_specs=[VECTOR] * 8,
        out_shape=(shape(TOK, D, dtype=f32), shape(TOK, D)),
    )(x, *mixed, own, other, gains)


def turn_kernel(
    place_ref, part0_ref, part1_ref, part2_ref, part3_ref, gy_ref, residual_ref, small_ref, gains_ref,
    m0_ref, m1_ref, m2_ref, m3_ref, own_ref, other_ref,
    do0_ref, do1_ref, do2_ref, do3_ref, grad_ref, keep_ref, send_ref, sums_ref,
):
    parts = (part0_ref, part1_ref, part2_ref, part3_ref)
    summed = sum(part[...].astype(f32) for part in parts)
    residual = residual_ref[...]
    factor = lax.rsqrt(jnp.mean(residual * residual, axis=-1, keepdims=True) + epsilon)
    normal = residual * factor
    gain = gains_ref[1:2]
    h = (normal * gain).astype(bf16)
    router = small_ref[:, 512 : 512 + EXPERTS]
    table = gate_table(dot(h, router), gy_ref[:, D:].astype(f32)[:, :EXPERTS])
    dgates = summed[:, D : D + EXPERTS]
    dlogits = (table * (dgates - jnp.sum(table * dgates, axis=-1, keepdims=True))).astype(bf16)
    dh = summed[:, :D] + dot(dlogits, router, NT)
    grad_gain = column_of(jnp.sum(dh * normal, axis=0, keepdims=True))
    grad_router = dot(h, dlogits, TN)
    sums = jnp.concatenate([grad_router, jnp.zeros((D, 128 - EXPERTS), f32)], axis=1)
    sums_ref[...] = jnp.where(iota((D, 128), 1) == 33, grad_gain, sums)
    scaled = dh * gain
    grad = gy_ref[:, :D].astype(f32) + factor * (scaled - normal * jnp.mean(scaled * normal, axis=-1, keepdims=True))
    grad_ref[...] = grad
    dz = grad.astype(bf16)
    mixed_refs, do_refs = (m0_ref, m1_ref, m2_ref, m3_ref), (do0_ref, do1_ref, do2_ref, do3_ref)
    for i, ((y, _, _), w) in enumerate(zip(positions(place_ref), output_blocks(own_ref, other_ref))):
        do_refs[i][...] = dot(dz, w, NT).astype(bf16)
        out = keep_ref if i < 2 else send_ref
        out[y] = dot(mixed_refs[i][...], dz, TN).astype(bf16)


def turn_back(place, parts, gy, residual, small, gains, mixed, own, other):
    pair = shape(2, TOK, D)
    return call(
        turn_kernel, "turn", 2_000_000_000, 10_000_000,
        in_specs=[SCALAR] + [VECTOR] * 14,
        out_shape=(*[shape(TOK, 256)] * 4, shape(TOK, D, dtype=f32), pair, pair, shape(D, 128, dtype=f32)),
    )(place, *parts, gy, residual, small, gains, *mixed, own, other)


def back_kernel(
    place_ref, q_ref, k_ref, v_ref, do0_ref, do1_ref, do2_ref, do3_ref, lse_ref, cos_ref, sin_ref, w_ref,
    x0_ref, x1_ref, x2_ref, x3_ref, out_ref, keep_ref, send_ref, gain_ref, do_ref, dk_ref, dv_ref,
):
    for (_, _, at), ref in zip(positions(place_ref), (do0_ref, do1_ref, do2_ref, do3_ref)):
        do_ref[at] = ref[...]
    dk_ref[...] = jnp.zeros_like(dk_ref)
    dv_ref[...] = jnp.zeros_like(dv_ref)
    scale = HEAD**-0.5
    place_queries = as_bf16(spread_queries())
    for i in range(4):
        rows = slice(256 * i, 256 * i + 256)
        n = 256 * (i + 1)
        seen = iota((256, n), 1) <= iota((256, n), 0) + 256 * i
        dq = jnp.zeros((256, 256), f32)
        for head in range(GROUP):
            lanes = head_lanes_rope(head)
            q = q_ref[rows] * as_bf16(lanes)
            do = do_ref[i] * as_bf16(head_lanes(head))
            scores = dot(q, k_ref[:n], NT) * scale - lse_ref[rows, head : head + 1]
            probs = jnp.where(seen, jnp.exp(jnp.where(seen, scores, 0.0)), 0.0)
            dprobs = dot(do, v_ref[:n], NT)
            row_dot = jnp.sum(probs * dprobs, axis=-1, keepdims=True)
            ds = (probs * (dprobs - row_dot)).astype(bf16)
            dq = dq + jnp.where(lanes, dot(ds, k_ref[:n]), 0.0)
            dk_ref[:n] += dot(ds, q, TN)
            dv_ref[:n] += dot(probs.astype(bf16), do, TN)
        c, s = cos_ref[rows], sin_ref[rows]
        a, b = dq[:, :128] * scale, dq[:, 128:] * scale
        dq = jnp.concatenate([a * c + b * s, b * c - a * s], axis=1).astype(bf16)
        out_ref[rows, :256] = dot(dq, place_queries, NT).astype(bf16)
    keep_keys, first_key = spread_keys()
    keep_values, first_value = spread_values()
    pick_keys = as_bf16(keep_keys & first_key)
    pick_values = as_bf16(keep_values & first_value)
    for i in range(4):
        rows = slice(256 * i, 256 * i + 256)
        c, s = cos_ref[rows], sin_ref[rows]
        a, b = dk_ref[rows, :128] * scale, dk_ref[rows, 128:] * scale
        a, b = a * c + b * s, b * c - a * s
        a, b = a + pltpu.roll(a, 96, 1), b + pltpu.roll(b, 96, 1)
        out_ref[rows, 256:384] = dot(jnp.concatenate([a, b], axis=1).astype(bf16), pick_keys, NT).astype(bf16)
        a, b = dv_ref[rows, :128], dv_ref[rows, 128:]
        a, b = a + pltpu.roll(a, 64, 1), b + pltpu.roll(b, 64, 1)
        out_ref[rows, 384:512] = dot(jnp.concatenate([a, b], axis=1).astype(bf16), pick_values, NT).astype(bf16)
    w = w_ref[:, :512]
    grad_gain = jnp.zeros((1, D), f32)
    for i, ((y, _, at), x_ref) in enumerate(zip(positions(place_ref), (x0_ref, x1_ref, x2_ref, x3_ref))):
        partial = dot(out_ref[pl.ds(pl.multiple_of(256 * at, 256), 256)], w, NT)
        grad_gain = grad_gain + jnp.sum(partial * normed(x_ref[...].astype(f32)), axis=0, keepdims=True)
        out = keep_ref if i < 2 else send_ref
        out[y] = partial.astype(bf16)
    gain_ref[...] = jnp.broadcast_to(grad_gain, (8, D))


def back(place, q, k, v, do, lse, cos, sin, w, blocks):
    pair = shape(2, TOK, D)
    return call(
        back_kernel, "back", 20_000_000_000, 16_000_000,
        in_specs=[SCALAR] + [VECTOR] * 15,
        out_shape=(shape(LENGTH, 512), pair, pair, shape(8, D, dtype=f32)),
        scratch_shapes=[
            pltpu.VMEM((4, TOK, 256), bf16), pltpu.VMEM((LENGTH, 256), f32), pltpu.VMEM((LENGTH, 256), f32),
        ],
    )(place, q, k, v, *do, lse, cos, sin, w, *blocks)


def projections_kernel(h_ref, dqkv_ref, sums_ref, gain_ref, first_ref):
    first_ref[:, :512] = dot(h_ref[...], dqkv_ref[...], TN).astype(bf16)
    small = jnp.where(iota((D, 128), 1) == 32, column_of(gain_ref[0:1]), sums_ref[...])
    first_ref[:, 512:] = small.astype(bf16)


def projections(h, dqkv, sums, gain):
    return call(
        projections_kernel, "projections", 1_500_000_000, 5_000_000, in_specs=[VECTOR] * 4, out_shape=shape(D, 640)
    )(h, dqkv, sums, gain)


def own_slots(expert, slot, z):
    start = ((expert % 16) // 4 * 2 + expert // 16) * CAP
    own = (expert % 4 == z) & (slot >= start) & (slot < start + CAP)
    return own, jnp.where(own, slot - start, 0)


def slot_tables(z, spread, start):
    own, place = own_slots(iota((EXPERTS, SLOTS), 0), iota((EXPERTS, SLOTS), 1), z)
    spread[...] = as_bf16(own)
    start[...] = jnp.sum(place, axis=0, keepdims=True).astype(f32)


SLOT_TABLES = [pltpu.VMEM((EXPERTS, SLOTS), bf16), pltpu.VMEM((1, SLOTS), f32)]


def gate_table(logits, codes):
    routed = codes >= 0
    logits = jnp.where(routed, logits, -1e30)
    e = jnp.where(routed, jnp.exp(logits - jnp.max(logits, axis=-1, keepdims=True)), 0.0)
    return e / jnp.sum(e, axis=-1, keepdims=True)


def whole(*shape):
    return pl.BlockSpec(shape, lambda e: (0,) * len(shape))


def per_expert(*shape):
    return pl.BlockSpec((1,) + shape, lambda e: (e,) + (0,) * len(shape))


def rows_kernel(n, with_gates, z_ref, *refs):
    i = pl.program_id(0)
    z = z_ref[0]
    values_refs, refs = refs[:n], refs[n:]
    if with_gates:
        codes_refs, router_ref, refs = refs[:n], refs[n], refs[n + 1 :]
        rows_ref, gates_ref, turn_ref, values, codes, own, start = refs[-7:]
    else:
        rows_ref, turn_ref, values, codes, own, start = refs[-6:]
    for b in range(n):

        @pl.when(i == b)
        def _():
            values[...] = values_refs[b][:, :D]
            codes[...] = codes_refs[b][...] if with_gates else values_refs[b][:, D:]

    @pl.when(i == 0)
    def _():
        turn_ref[...] = jnp.zeros_like(turn_ref)
        mine, offset = own_slots(iota((SLOTS, EXPERTS), 1), iota((SLOTS, EXPERTS), 0), z)
        own[...] = as_bf16(mine)
        start[...] = jnp.sum(offset, axis=1, keepdims=True).astype(f32)

    slots = codes[:, :EXPERTS]
    place = as_bf16(dot(own[...], slots, NT) == start[...])
    rows_ref[:, 0] = dot(place, values[...]).astype(bf16).reshape(SHARE, CAP, D)
    if with_gates:
        table = gate_table(dot(values[...], router_ref[:, :EXPERTS]), slots.astype(f32))
        gate = jnp.sum(dot(place, table.astype(bf16)) * own[...].astype(f32), axis=1, keepdims=True)
        gates_ref[:, 0] = gate.reshape(SHARE, CAP, 1)


def rows_of(z, first, blocks, codes, router, kept, turn):
    n, with_gates = len(blocks), router is not None
    args, specs = [z, *blocks], [SCALAR] + [whole(TOK, blocks[0].shape[1])] * n
    if with_gates:
        args += [*codes, router]
        specs += [pl.BlockSpec((TOK, 128), lambda e: (0, D // 128))] * n + [pl.BlockSpec((D, 128), lambda e: (0, 4))]
    args.append(turn)
    specs.append(ANYWHERE)
    widths = [(D, bf16)] + ([(1, f32)] if with_gates else [])
    out_specs = [pl.BlockSpec((SHARE, 1, CAP, w), lambda e: (0, first + e, 0, 0)) for w, _ in widths]
    out_shape = [shape(SHARE, BLOCKS, CAP, w, dtype=t) for w, t in widths]
    out_specs.append(whole(8, 128))
    out_shape.append(shape(8, 128, dtype=f32))
    aliases = {}
    if kept is not None:
        aliases = {len(args) + i: i for i in range(len(kept))}
        args += kept
        specs += [ANYWHERE] * len(kept)
    *kept, turn = call(
        functools.partial(rows_kernel, n, with_gates), "rows", n * 750_000_000, n * 2_000_000,
        grid=(n,), in_specs=specs, out_specs=out_specs, out_shape=out_shape, input_output_aliases=aliases,
        scratch_shapes=[
            pltpu.VMEM((TOK, D), bf16), pltpu.VMEM((TOK, 128), bf16), pltpu.VMEM((SLOTS, EXPERTS), bf16),
            pltpu.VMEM((SLOTS, 1), f32),
        ],
    )(*args)
    return kept, turn


def down_of(parts):
    return jnp.concatenate(
        [
            jnp.concatenate([parts[0, 128 * j : 128 * j + 128], parts[1, 128 * j : 128 * j + 128]], axis=0)
            for j in range(4)
        ],
        axis=1,
    )


def codes_specs():
    return [pl.BlockSpec((TOK, 128), lambda e: (0, D // 128))] * BLOCKS


PARTS = 2


def main_kernel(z_ref, x_ref, gy_ref, gate_ref, w_ref, *refs):
    codes_refs = refs[:8]
    act_ref, out_ref, own_ref, other_ref, kept, dgates, hidden, codes_kept, spread, start, mine = refs[8:]
    e = pl.program_id(0)

    @pl.when(e == 0)
    def _():
        for b in range(BLOCKS):
            codes_kept[b] = codes_refs[b][...]
        slot_tables(z_ref[0], spread, start)
        own, _ = own_slots(iota((SLOTS, EXPERTS), 1), iota((SLOTS, EXPERTS), 0), z_ref[0])
        mine[...] = own.astype(f32)

    down_w = down_of(w_ref[:, 1024:])
    gate_w = w_ref[:, :512].reshape(D, HALF)
    up_w = w_ref[:, 512:1024].reshape(D, HALF)
    both_w = jnp.concatenate([gate_w, up_w], axis=1)
    step = BLOCKS // PARTS
    for i in range(PARTS):
        blocks, rows = slice(step * i, step * i + step), slice(step * i * CAP, step * (i + 1) * CAP)
        x = x_ref[0, blocks].reshape(step * CAP, D)
        gate = gate_ref[0, blocks].reshape(step * CAP, 1)
        da = dot(gy_ref[0, blocks].reshape(step * CAP, D), down_w, NT)
        g = dot(x, gate_w)
        u = dot(x, up_w)
        s = jax.nn.sigmoid(g)
        silu = g * s
        act = silu * u
        dgates[blocks, e] = jnp.sum(act * da, axis=1, keepdims=True).reshape(step, CAP, 1)
        act_ref[0, rows] = (act * gate).astype(bf16)
        da = da * gate
        hidden[rows, :HALF] = (da * u * (s + silu * (1.0 - s))).astype(bf16)
        hidden[rows, HALF:] = (da * silu).astype(bf16)
        kept[blocks, e] = dot(hidden[rows], both_w, NT).astype(bf16).reshape(step, CAP, D)
    made = dot(hidden[...], x_ref[0].reshape(SLOTS, D), TN).astype(bf16)
    for i in range(2):
        out_ref[0, i, :512] = made[:, 512 * i : 512 * i + 512]
    made = dot(act_ref[0], gy_ref[0].reshape(SLOTS, D), TN).astype(bf16)
    for i in range(2):
        out_ref[0, i, 512:640] = made[128 * i : 128 * i + 128, :512]
        out_ref[0, i, 640:768] = made[128 * i : 128 * i + 128, 512:]

    @pl.when(e == SHARE - 1)
    def _():
        def pair(j, carry):
            for c, out in ((0, own_ref), (1, other_ref)):
                b = 2 * j + c
                place = as_bf16(dot(codes_kept[b][:, :EXPERTS], spread[...]) == start[...])
                out[j, :, :D] = dot(place, kept[b].reshape(SLOTS, D)).astype(bf16)
                scattered = dot(place, (mine[...] * dgates[b].reshape(SLOTS, 1)).astype(bf16))
                out[j, :, D:] = jnp.concatenate([scattered, jnp.zeros((TOK, 128 - EXPERTS), f32)], axis=1).astype(bf16)
            return carry

        lax.fori_loop(0, 4, pair, 0)


def main(z, x, gy, gates, weights, codes):
    back = shape(4, TOK, D + 128)
    return call(
        main_kernel, "experts", 25_000_000_000, 60_000_000,
        grid=(SHARE,),
        in_specs=[
            SCALAR, per_expert(BLOCKS, CAP, D), per_expert(BLOCKS, CAP, D), per_expert(BLOCKS, CAP, 1),
            pl.BlockSpec((2, 1536, 256), lambda e: (e, 0, 0)), *codes_specs(),
        ],
        out_specs=[
            per_expert(SLOTS, HALF), per_expert(2, 768, 512), whole(4, TOK, D + 128), whole(4, TOK, D + 128),
        ],
        out_shape=[shape(SHARE, SLOTS, HALF), shape(SHARE, 2, 768, 512), back, back],
        scratch_shapes=[
            pltpu.VMEM((BLOCKS, SHARE, CAP, D), bf16),
            pltpu.VMEM((BLOCKS, SHARE, CAP, 1), f32),
            pltpu.VMEM((SLOTS, 2 * HALF), bf16),
            pltpu.VMEM((BLOCKS, TOK, 128), bf16),
            *SLOT_TABLES,
            pltpu.VMEM((SLOTS, EXPERTS), f32),
        ],
    )(z, x, gy, gates, weights, *codes)


def outs_kernel(z_ref, act_ref, w_ref, *refs):
    codes_refs = refs[:8]
    own_ref, other_ref, kept, codes_kept, spread, start = refs[8:]
    e = pl.program_id(0)
    kept[:, e] = dot(act_ref[0], down_of(w_ref[...])).astype(bf16).reshape(BLOCKS, CAP, D)

    @pl.when(e == 0)
    def _():
        for b in range(BLOCKS):
            codes_kept[b] = codes_refs[b][...]
        slot_tables(z_ref[0], spread, start)

    @pl.when(e == SHARE - 1)
    def _():
        def pair(j, carry):
            for c, out in ((0, own_ref), (1, other_ref)):
                b = 2 * j + c
                place = as_bf16(dot(codes_kept[b][:, :EXPERTS], spread[...]) == start[...])
                out[j] = dot(place, kept[b].reshape(SLOTS, D)).astype(bf16)
            return carry

        lax.fori_loop(0, 4, pair, 0)


def outs(z, act, weights, codes):
    back = jax.ShapeDtypeStruct((4, TOK, D), bf16)
    return call(
        outs_kernel, "expert_outs", 6_000_000_000, 12_000_000,
        grid=(SHARE,),
        in_specs=[
            SCALAR, per_expert(SLOTS, HALF), pl.BlockSpec((2, 512, 256), lambda e: (e, 2, 0)), *codes_specs(),
        ],
        out_specs=[whole(4, TOK, D)] * 2,
        out_shape=[back, back],
        scratch_shapes=[
            pltpu.VMEM((BLOCKS, SHARE, CAP, D), bf16), pltpu.VMEM((BLOCKS, TOK, 128), bf16), *SLOT_TABLES,
        ],
    )(z, act, weights, *codes)


def finish_kernel(place_ref, mine_ref, got_ref, gate_ref, up_ref, down_ref):
    core = place_ref[1]
    for i, out in enumerate((gate_ref, up_ref)):
        for j in range(2):
            rows = slice(256 * i + 128 * j, 256 * i + 128 * j + 128)
            keep = mine_ref[rows, pl.ds(pl.multiple_of(256 * core, 256), 256)].astype(f32)
            out[:, pl.ds(pl.multiple_of(256 * j + 128 * core, 128), 128)] = keep.T
            got = got_ref[rows].astype(f32)
            out[:, pl.ds(pl.multiple_of(256 * j + 128 * (1 - core), 128), 128)] = got.T
    for j in range(2):
        down_ref[:, 512 * j : 512 * j + 512] = mine_ref[512 + 128 * j : 640 + 128 * j].astype(f32)


def finish(place, mine, got):
    return call(
        finish_kernel, "finish", 1_000_000, 4_000_000,
        in_specs=[SCALAR, VECTOR, VECTOR],
        out_shape=(shape(TOK, FF, dtype=f32), shape(TOK, FF, dtype=f32), shape(128, D, dtype=f32)),
    )(place, mine, got)


def shift(values, axis, by):
    n = 4 if axis in ("x", "z") else 2
    return lax.ppermute(values, axis, [(i, (i + by) % n) for i in range(n)])


def swap(values, axis):
    return shift(values, axis, 1)


def gather_z(values):
    return [values, shift(values, "z", 1), shift(values, "z", -1), shift(values, "z", 2)]


def with_core(blocks):
    return [(block, swap(block, "core")) for block in blocks]


def exchange_seq(own, across, beside, both):
    return [own, swap(across, "ylo"), swap(beside, "core"), swap(swap(both, "ylo"), "core")]


def core_sums(own, other):
    got = swap(other, "core")
    return [(own[j].astype(f32) + got[j].astype(f32)).astype(bf16) for j in range(4)]


def scatter_z(sums):
    return [sums[0], shift(sums[1], "z", -1), shift(sums[2], "z", 1), shift(sums[3], "z", 2)]


def fence(*values):
    return lax.optimization_barrier(values)


def on_device(
    tokens, norm1_gain, query_weight, key_weight, value_weight, output_weight, norm2_gain, router_weight,
    expert_gate, expert_up, expert_down, routes, cotangent,
):
    ylo, core = lax.axis_index("ylo"), lax.axis_index("core")
    z = lax.axis_index("z").astype(jnp.int32).reshape(1)
    place = jnp.stack([ylo, core]).astype(jnp.int32)

    own = tokens.reshape(TOK, D)
    across = swap(own, "ylo")
    gy_own = with_codes(routes.reshape(TOK, TOPK), cotangent.reshape(TOK, D))
    packed, keep, send = pack(
        place, query_weight, key_weight, value_weight, router_weight, norm1_gain.reshape(1, 8), norm2_gain.reshape(1, 8),
        expert_gate.reshape(TOK, FF), expert_up.reshape(TOK, FF),
    )

    expert_w = assemble(place, keep, swap(send, "core"), expert_down.reshape(128, D))
    lane = jnp.arange(128) % 32
    angles = jnp.arange(LENGTH).astype(f32)[:, None] * (rope_base ** (-2.0 * lane.astype(f32) / HEAD))[None, :]
    expert_w, packed, across, cos, sin = fence(expert_w, packed, across, jnp.cos(angles), jnp.sin(angles))
    expert_w = lax.all_gather(expert_w, PLANE, axis=0).reshape(16, 1536, 256)

    arrived = lax.all_to_all(packed, AXES, split_axis=0, concat_axis=0, tiled=True).reshape(D, 640)
    output_rows = jnp.concatenate([output_weight, swap(output_weight, "ylo")], axis=1)
    gy_blocks = gather_z(gy_own)
    arrived, output_rows, *near = fence(arrived, output_rows, *gy_blocks[1:3])
    gy_near = [block for pair in with_core([gy_own, *near]) for block in pair]
    gy_far = gy_blocks[3]
    beside = swap(own, "core")

    blocks = [own, across, beside, swap(across, "core")]
    q, k, v, *mixed, lse, hidden_all, gains = front(place, blocks, arrived, cos, sin)

    output_own = lax.all_to_all(
        jnp.broadcast_to(output_rows[None], (32, 8, 2 * D)), FSDP, split_axis=0, concat_axis=0, tiled=True
    ).reshape(TOK, 2 * D)

    turn, mixed[0], *gy_near = fence(jnp.zeros((8, 128), f32), mixed[0], *gy_near)
    own_mixed, across_mixed, beside_mixed, both_mixed = mixed
    gy_rows, turn = rows_of(z, 0, gy_near, None, None, None, turn)
    both_mixed, turn = fence(swap(both_mixed, "ylo"), turn)
    mixed = [own_mixed, swap(across_mixed, "ylo"), swap(beside_mixed, "core"), swap(both_mixed, "core")]
    output_own, gy_far, turn, *mixed = fence(output_own, gy_far, turn, *mixed)
    output_other = swap(output_own, "core")
    gy_blocks = [*gy_near, gy_far, swap(gy_far, "core")]
    residual, hidden_two = mid(own, mixed, output_own, output_other, gains)

    near = [shift(hidden_two, "z", 1), shift(hidden_two, "z", -1)]
    turn, _ = fence(turn, hidden_two)
    gy_rows, turn = rows_of(z, 6, gy_blocks[6:], None, None, gy_rows, turn)
    rows, turn = rows_of(z, 0, (hidden_two, swap(hidden_two, "core")), gy_blocks[:2], arrived, None, turn)
    *near, far, turn = fence(*near, hidden_two, turn)
    far = shift(far, "z", 2)
    near = [block for pair in with_core(near) for block in pair]
    rows, turn = rows_of(z, 2, near, gy_blocks[2:6], arrived, rows, turn)
    far, turn = fence(far, turn)
    rows, turn = rows_of(z, 6, (far, swap(far, "core")), gy_blocks[6:], arrived, rows, turn)
    (gy_rows,), (rows, gate_rows) = gy_rows, rows

    act, expert_grads, back_own, back_other = main(z, rows, gy_rows, gate_rows, expert_w, gy_blocks)
    sums = core_sums(back_own, back_other)
    parts = scatter_z(sums)
    moe_act, *_ = fence(act, *sums)
    moe_own, moe_other = outs(z, moe_act, expert_w, gy_blocks)
    expert_grads = lax.psum_scatter(expert_grads.reshape(16 * 768, 512), PLANE, scatter_dimension=0, tiled=True)

    moe_sums = core_sums(moe_own, moe_other)
    *do, grad_residual, keep, send, small = turn_back(
        place, parts, gy_own, residual, arrived, gains, mixed, output_own, output_other
    )

    do = exchange_seq(*do)
    grad_output_sum = (keep.astype(f32) + swap(send, "core").astype(f32)).astype(bf16).reshape(64, 8, D)
    grad_output_sum, *moe_sums = fence(grad_output_sum, *moe_sums)
    moe_near = [shift(moe_sums[1], "z", -1), shift(moe_sums[2], "z", 1)]
    grad_output = lax.all_to_all(grad_output_sum, ("ylo",) + FSDP, split_axis=0, concat_axis=0, tiled=True)
    dqkv, keep, send, gain = back(place, q, k, v, do, lse, cos, sin, arrived, blocks)
    dqkv, keep, send, own, grad_output, *moe_near = fence(dqkv, keep, send, own, grad_output, *moe_near)
    first = projections(hidden_all, dqkv, small, gain)

    away = jnp.where(core == 0, expert_grads[:512, 256:], expert_grads[:512, :256])
    finished = finish(place, expert_grads, swap(away, "core"))

    pair = (keep.astype(f32) + swap(send, "core").astype(f32)).astype(bf16)
    kept = jnp.where(ylo == 0, pair[0], pair[1])
    got = swap(jnp.where(ylo == 0, pair[1], pair[0]), "ylo")
    first = lax.all_to_all(first.reshape(128, 8, 640), AXES, split_axis=0, concat_axis=0, tiled=True)
    first, got, moe_far, grad_gate, grad_up, grad_down = fence(first, got, shift(moe_sums[3], "z", 2), *finished)
    grad_hidden_one = kept.astype(f32) + got.astype(f32)
    grad_output = jnp.sum(grad_output.astype(f32), axis=0)
    layer_out = sum(part.astype(f32) for part in (moe_sums[0], *moe_near, moe_far))
    layer_out = (residual + layer_out).astype(bf16).reshape(1, TOK, D)
    inputs = own.astype(f32)
    factor_one = lax.rsqrt(jnp.mean(inputs * inputs, axis=-1, keepdims=True) + epsilon)
    normed_one = inputs * factor_one
    scaled = grad_hidden_one * gains[0:1]
    grad_inputs = grad_residual + factor_one * (
        scaled - normed_one * jnp.mean(scaled * normed_one, axis=-1, keepdims=True)
    )

    first = jnp.sum(first.astype(f32).reshape(4, 32, 8, 640), axis=1)
    grad_query = first[:, :, :256].transpose(1, 0, 2).reshape(8, D)
    grad_key = first[:, :, 256:384].transpose(1, 0, 2).reshape(8, 512)
    grad_value = first[:, :, 384:512].transpose(1, 0, 2).reshape(8, 512)
    small = jnp.sum(first[:, :, 512:], axis=0)
    return (
        layer_out, grad_inputs.reshape(1, TOK, D), small[:, 32], grad_query, grad_key, grad_value, grad_output,
        small[:, 33], small[:, :EXPERTS], grad_gate.reshape(1, TOK, FF), grad_up.reshape(1, TOK, FF),
        grad_down.reshape(1, 128, D),
    )


def solution(mesh):
    fine = Mesh(mesh.devices.reshape(2, 2, 2, 4, 4), AXES)
    tok = P(FSDP, SEQ, None)
    row = P(AXES, None)
    vec = P(AXES)
    in_specs = (tok, vec, row, row, row, row, vec, row, tok, tok, tok, tok, tok)
    out_specs = (tok, tok, vec, row, row, row, row, vec, row, tok, tok, tok)
    return jax.shard_map(on_device, mesh=fine, in_specs=in_specs, out_specs=out_specs, check_vma=False)
```

```python
import functools

import jax
import jax.numpy as jnp
from jax import lax
from jax.experimental import pallas as pl
from jax.experimental.pallas import tpu as pltpu
from jax.sharding import Mesh
from jax.sharding import PartitionSpec as P

HEADS = 16
KV_HEADS = 8
HEAD = 64
TOPK = 8
CAP = 80
TOK = 256
D = 1024
FF = 512
EXPERTS = 32
SHARE = 8
SLOTS = SHARE * CAP
BLOCKS = 8
HALF = FF // 2
GROUP = 4
LENGTH = 1024

epsilon = 1e-06
rope_base = 10000.0

AXES = ("ylo", "core", "yhi", "x", "z")
SEQ = ("ylo", "core")
FSDP = ("yhi", "x", "z")
PLANE = ("x", "yhi", "ylo")

f32 = jnp.float32
bf16 = jnp.bfloat16

NT = (((1,), (1,)), ((), ()))
TN = (((0,), (0,)), ((), ()))
VMEM_LIMIT = 56 * 1024 * 1024


def dot(a, b, dims=(((1,), (0,)), ((), ()))):
    return lax.dot_general(a, b, dims, preferred_element_type=f32)


def iota(shape, axis):
    return lax.broadcasted_iota(jnp.int32, shape, axis)


def as_bf16(cond):
    return jnp.where(cond, 1.0, 0.0).astype(bf16)


def call(kernel, name, flops, moved, **kwargs):
    return pl.pallas_call(
        kernel,
        compiler_params=pltpu.CompilerParams(vmem_limit_bytes=VMEM_LIMIT),
        cost_estimate=pl.CostEstimate(flops=flops, bytes_accessed=moved, transcendentals=0),
        name=name,
        **kwargs,
    )


def shape(*dims, dtype=bf16):
    return jax.ShapeDtypeStruct(dims, dtype)


SCALAR = pl.BlockSpec(memory_space=pltpu.SMEM)
ANYWHERE = pl.BlockSpec(memory_space=pl.ANY)
VECTOR = pl.BlockSpec(memory_space=pltpu.VMEM)


def column_of(row):
    n = row.shape[1]
    step = min(n, 128)
    same = iota((step, step), 0) == iota((step, step), 1)
    parts = [jnp.sum(jnp.where(same, row[:, i : i + step], 0.0), axis=1, keepdims=True) for i in range(0, n, step)]
    return jnp.concatenate(parts, axis=0) if len(parts) > 1 else parts[0]


def row_of(column):
    n = column.shape[0]
    same = iota((128, 128), 0) == iota((128, 128), 1)
    parts = [jnp.sum(jnp.where(same, column[i : i + 128], 0.0), axis=0, keepdims=True) for i in range(0, n, 128)]
    return jnp.concatenate(parts, axis=1)


def codes_kernel(routes_ref, gy_ref, gy_out_ref):
    routes = routes_ref[...]
    expert = iota((TOK, EXPERTS), 1)
    chosen = jnp.zeros((TOK, EXPERTS), jnp.bool_)
    for i in range(TOPK):
        chosen = chosen | (routes[:, i : i + 1] == expert)
    earlier = as_bf16(iota((TOK, TOK), 1) < iota((TOK, TOK), 0))
    codes = jnp.where(chosen, dot(earlier, as_bf16(chosen)), -1.0)
    gy_out_ref[:, :D] = gy_ref[...]
    gy_out_ref[:, D:] = jnp.concatenate([codes, jnp.zeros((TOK, 128 - EXPERTS), f32)], axis=1).astype(bf16)


def with_codes(routes, gy):
    return call(
        codes_kernel, "codes", 50_000_000, 1_500_000, in_specs=[VECTOR] * 2, out_shape=shape(TOK, D + 128)
    )(routes, gy)


def pack_kernel(
    place_ref, query_ref, key_ref, value_ref, router_ref, one_ref, two_ref, gate_ref, up_ref,
    packed_ref, keep_ref, send_ref,
):
    core = place_ref[1]
    lane = iota((8, 128), 1)
    small = jnp.concatenate([router_ref[...].astype(f32), jnp.zeros((8, 96), f32)], axis=1)
    small = jnp.where(lane == 32, column_of(one_ref[...].astype(f32)), small)
    small = jnp.where(lane == 33, column_of(two_ref[...].astype(f32)), small).astype(bf16)
    for s in range(4):
        part = jnp.concatenate(
            [
                query_ref[:, 256 * s : 256 * s + 256],
                key_ref[:, 128 * s : 128 * s + 128],
                value_ref[:, 128 * s : 128 * s + 128],
                small,
            ],
            axis=1,
        )
        for f in range(32):
            packed_ref[32 * s + f] = part
    for i, ref in enumerate((gate_ref, up_ref)):
        for j in range(2):
            keep_ref[i, :, 128 * j : 128 * j + 128] = ref[:, pl.ds(256 * j + 128 * core, 128)]
            send_ref[i, :, 128 * j : 128 * j + 128] = ref[:, pl.ds(256 * j + 128 * (1 - core), 128)]


def pack(place, *args):
    return call(
        pack_kernel, "pack", 100_000_000, 4_000_000,
        in_specs=[SCALAR] + [VECTOR] * len(args),
        out_shape=(shape(128, 8, 640), shape(2, TOK, HALF), shape(2, TOK, HALF)),
    )(place, *args)


def assemble_kernel(place_ref, keep_ref, got_ref, down_ref, out_ref):
    core = place_ref[1]
    for i in range(2):
        out_ref[pl.ds(512 * i + 256 * core, 256)] = keep_ref[i]
        out_ref[pl.ds(512 * i + 256 * (1 - core), 256)] = got_ref[i]
    for j in range(4):
        out_ref[1024 + 128 * j : 1152 + 128 * j] = down_ref[:, 256 * j : 256 * j + 256]


def assemble(place, keep, got, down):
    return call(
        assemble_kernel, "assemble", 1_000_000, 2_000_000,
        in_specs=[SCALAR] + [VECTOR] * 3, out_shape=shape(1536, 256),
    )(place, keep, got, down)


def head_lanes_rope(head):
    lane = iota((1, 256), 1) % 128
    return (lane >= 32 * head) & (lane < 32 * head + 32)


def head_lanes(head):
    lane = iota((1, 256), 1)
    return (lane >= 64 * head) & (lane < 64 * head + 64)


def spread_queries():
    row, col = iota((256, 256), 0), iota((256, 256), 1)
    return row == ((col % 128) // 32) * 64 + (col // 128) * 32 + col % 32


def spread_keys():
    row, col = iota((128, 256), 0), iota((128, 256), 1)
    return row == ((col % 128) // 64) * 64 + (col // 128) * 32 + col % 32, (col % 64) < 32


def spread_values():
    row, col = iota((128, 256), 0), iota((128, 256), 1)
    return row == (col // 128) * 64 + col % 64, (col % 128) < 64


def positions(place_ref):
    ylo, core = place_ref[0], place_ref[1]
    return [(y, c, 2 * y + c) for c in (core, 1 - core) for y in (ylo, 1 - ylo)]


def normed(x):
    return x * lax.rsqrt(jnp.mean(x * x, axis=-1, keepdims=True) + epsilon)


def front_kernel(
    place_ref, x0_ref, x1_ref, x2_ref, x3_ref, w_ref, cos_ref, sin_ref,
    q_ref, k_ref, v_ref, o0_ref, o1_ref, o2_ref, o3_ref, lse_ref, h_ref, gains_ref, o_ref,
):
    gain = row_of(w_ref[:, 512:640].astype(f32)[:, 32:33])
    gains_ref[0:1] = gain
    gains_ref[1:2] = row_of(w_ref[:, 512:640].astype(f32)[:, 33:34])
    wq = dot(w_ref[:, :256], as_bf16(spread_queries())).astype(bf16)
    wk = dot(w_ref[:, 256:384], as_bf16(spread_keys()[0])).astype(bf16)
    wv = dot(w_ref[:, 384:512], as_bf16(spread_values()[0])).astype(bf16)
    for (_, _, at), x_ref in zip(positions(place_ref), (x0_ref, x1_ref, x2_ref, x3_ref)):
        rows = pl.ds(pl.multiple_of(256 * at, 256), 256)
        h = (normed(x_ref[...].astype(f32)) * gain).astype(bf16)
        h_ref[rows] = h
        c, s = cos_ref[rows], sin_ref[rows]
        for w, out in ((wq, q_ref), (wk, k_ref)):
            pre = dot(h, w)
            a, b = pre[:, :128], pre[:, 128:]
            out[rows] = jnp.concatenate([a * c - b * s, b * c + a * s], axis=1).astype(bf16)
        v_ref[rows] = dot(h, wv).astype(bf16)
    for i in range(4):
        rows = slice(256 * i, 256 * i + 256)
        n = 256 * (i + 1)
        seen = iota((256, n), 1) <= iota((256, n), 0) + 256 * i
        mixed = jnp.zeros((256, 256), f32)
        logs = jnp.zeros((256, 128), f32)
        for head in range(GROUP):
            q = q_ref[rows] * as_bf16(head_lanes_rope(head))
            scores = jnp.where(seen, dot(q, k_ref[:n], NT) * HEAD**-0.5, -1e30)
            peak = jnp.max(scores, axis=-1, keepdims=True)
            e = jnp.exp(scores - peak)
            total = jnp.sum(e, axis=-1, keepdims=True)
            probs = (e * (1.0 / total)).astype(bf16)
            mixed = mixed + dot(probs, v_ref[:n] * as_bf16(head_lanes(head)))
            logs = jnp.where(iota((256, 128), 1) == head, peak + jnp.log(total), logs)
        o_ref[i] = mixed.astype(bf16)
        lse_ref[rows] = logs
    for (_, _, at), out in zip(positions(place_ref), (o0_ref, o1_ref, o2_ref, o3_ref)):
        out[...] = o_ref[at]


def front(place, blocks, w, cos, sin):
    return call(
        front_kernel, "front", 8_000_000_000, 10_000_000,
        in_specs=[SCALAR] + [VECTOR] * 7,
        out_shape=(
            shape(LENGTH, 256), shape(LENGTH, 256), shape(LENGTH, 256), *[shape(TOK, 256)] * 4,
            shape(LENGTH, 128, dtype=f32), shape(LENGTH, D), shape(8, D, dtype=f32),
        ),
        scratch_shapes=[pltpu.VMEM((4, TOK, 256), bf16)],
    )(place, *blocks, w, cos, sin)


def output_blocks(own_ref, other_ref):
    return [ref[:, D * i : D * i + D] for ref in (own_ref, other_ref) for i in range(2)]


def mid_kernel(x_ref, m0_ref, m1_ref, m2_ref, m3_ref, own_ref, other_ref, gains_ref, residual_ref, h_ref):
    total = x_ref[...].astype(f32)
    for mixed_ref, w in zip((m0_ref, m1_ref, m2_ref, m3_ref), output_blocks(own_ref, other_ref)):
        total = total + dot(mixed_ref[...], w)
    residual_ref[...] = total
    h_ref[...] = (normed(total) * gains_ref[1:2]).astype(bf16)


def mid(x, mixed, own, other, gains):
    return call(
        mid_kernel, "mid", 1_000_000_000, 5_000_000,
        in_specs=[VECTOR] * 8,
        out_shape=(shape(TOK, D, dtype=f32), shape(TOK, D)),
    )(x, *mixed, own, other, gains)


def turn_kernel(
    place_ref, part0_ref, part1_ref, part2_ref, part3_ref, gy_ref, residual_ref, small_ref, gains_ref,
    m0_ref, m1_ref, m2_ref, m3_ref, own_ref, other_ref,
    do0_ref, do1_ref, do2_ref, do3_ref, grad_ref, keep_ref, send_ref, sums_ref,
):
    parts = (part0_ref, part1_ref, part2_ref, part3_ref)
    summed = sum(part[...].astype(f32) for part in parts)
    residual = residual_ref[...]
    factor = lax.rsqrt(jnp.mean(residual * residual, axis=-1, keepdims=True) + epsilon)
    normal = residual * factor
    gain = gains_ref[1:2]
    h = (normal * gain).astype(bf16)
    router = small_ref[:, 512 : 512 + EXPERTS]
    table = gate_table(dot(h, router), gy_ref[:, D:].astype(f32)[:, :EXPERTS])
    dgates = summed[:, D : D + EXPERTS]
    dlogits = (table * (dgates - jnp.sum(table * dgates, axis=-1, keepdims=True))).astype(bf16)
    dh = summed[:, :D] + dot(dlogits, router, NT)
    grad_gain = column_of(jnp.sum(dh * normal, axis=0, keepdims=True))
    grad_router = dot(h, dlogits, TN)
    sums = jnp.concatenate([grad_router, jnp.zeros((D, 128 - EXPERTS), f32)], axis=1)
    sums_ref[...] = jnp.where(iota((D, 128), 1) == 33, grad_gain, sums)
    scaled = dh * gain
    grad = gy_ref[:, :D].astype(f32) + factor * (scaled - normal * jnp.mean(scaled * normal, axis=-1, keepdims=True))
    grad_ref[...] = grad
    dz = grad.astype(bf16)
    mixed_refs, do_refs = (m0_ref, m1_ref, m2_ref, m3_ref), (do0_ref, do1_ref, do2_ref, do3_ref)
    for i, ((y, _, _), w) in enumerate(zip(positions(place_ref), output_blocks(own_ref, other_ref))):
        do_refs[i][...] = dot(dz, w, NT).astype(bf16)
        out = keep_ref if i < 2 else send_ref
        out[y] = dot(mixed_refs[i][...], dz, TN).astype(bf16)


def turn_back(place, parts, gy, residual, small, gains, mixed, own, other):
    pair = shape(2, TOK, D)
    return call(
        turn_kernel, "turn", 2_000_000_000, 10_000_000,
        in_specs=[SCALAR] + [VECTOR] * 14,
        out_shape=(*[shape(TOK, 256)] * 4, shape(TOK, D, dtype=f32), pair, pair, shape(D, 128, dtype=f32)),
    )(place, *parts, gy, residual, small, gains, *mixed, own, other)


def back_kernel(
    place_ref, q_ref, k_ref, v_ref, do0_ref, do1_ref, do2_ref, do3_ref, lse_ref, cos_ref, sin_ref, w_ref,
    x0_ref, x1_ref, x2_ref, x3_ref, out_ref, keep_ref, send_ref, gain_ref, do_ref, dk_ref, dv_ref,
):
    for (_, _, at), ref in zip(positions(place_ref), (do0_ref, do1_ref, do2_ref, do3_ref)):
        do_ref[at] = ref[...]
    dk_ref[...] = jnp.zeros_like(dk_ref)
    dv_ref[...] = jnp.zeros_like(dv_ref)
    scale = HEAD**-0.5
    place_queries = as_bf16(spread_queries())
    for i in range(4):
        rows = slice(256 * i, 256 * i + 256)
        n = 256 * (i + 1)
        seen = iota((256, n), 1) <= iota((256, n), 0) + 256 * i
        dq = jnp.zeros((256, 256), f32)
        for head in range(GROUP):
            lanes = head_lanes_rope(head)
            q = q_ref[rows] * as_bf16(lanes)
            do = do_ref[i] * as_bf16(head_lanes(head))
            scores = dot(q, k_ref[:n], NT) * scale - lse_ref[rows, head : head + 1]
            probs = jnp.where(seen, jnp.exp(jnp.where(seen, scores, 0.0)), 0.0)
            dprobs = dot(do, v_ref[:n], NT)
            row_dot = jnp.sum(probs * dprobs, axis=-1, keepdims=True)
            ds = (probs * (dprobs - row_dot)).astype(bf16)
            dq = dq + jnp.where(lanes, dot(ds, k_ref[:n]), 0.0)
            dk_ref[:n] += dot(ds, q, TN)
            dv_ref[:n] += dot(probs.astype(bf16), do, TN)
        c, s = cos_ref[rows], sin_ref[rows]
        a, b = dq[:, :128] * scale, dq[:, 128:] * scale
        dq = jnp.concatenate([a * c + b * s, b * c - a * s], axis=1).astype(bf16)
        out_ref[rows, :256] = dot(dq, place_queries, NT).astype(bf16)
    keep_keys, first_key = spread_keys()
    keep_values, first_value = spread_values()
    pick_keys = as_bf16(keep_keys & first_key)
    pick_values = as_bf16(keep_values & first_value)
    for i in range(4):
        rows = slice(256 * i, 256 * i + 256)
        c, s = cos_ref[rows], sin_ref[rows]
        a, b = dk_ref[rows, :128] * scale, dk_ref[rows, 128:] * scale
        a, b = a * c + b * s, b * c - a * s
        a, b = a + pltpu.roll(a, 96, 1), b + pltpu.roll(b, 96, 1)
        out_ref[rows, 256:384] = dot(jnp.concatenate([a, b], axis=1).astype(bf16), pick_keys, NT).astype(bf16)
        a, b = dv_ref[rows, :128], dv_ref[rows, 128:]
        a, b = a + pltpu.roll(a, 64, 1), b + pltpu.roll(b, 64, 1)
        out_ref[rows, 384:512] = dot(jnp.concatenate([a, b], axis=1).astype(bf16), pick_values, NT).astype(bf16)
    w = w_ref[:, :512]
    grad_gain = jnp.zeros((1, D), f32)
    for i, ((y, _, at), x_ref) in enumerate(zip(positions(place_ref), (x0_ref, x1_ref, x2_ref, x3_ref))):
        partial = dot(out_ref[pl.ds(pl.multiple_of(256 * at, 256), 256)], w, NT)
        grad_gain = grad_gain + jnp.sum(partial * normed(x_ref[...].astype(f32)), axis=0, keepdims=True)
        out = keep_ref if i < 2 else send_ref
        out[y] = partial.astype(bf16)
    gain_ref[...] = jnp.broadcast_to(grad_gain, (8, D))


def back(place, q, k, v, do, lse, cos, sin, w, blocks):
    pair = shape(2, TOK, D)
    return call(
        back_kernel, "back", 20_000_000_000, 16_000_000,
        in_specs=[SCALAR] + [VECTOR] * 15,
        out_shape=(shape(LENGTH, 512), pair, pair, shape(8, D, dtype=f32)),
        scratch_shapes=[
            pltpu.VMEM((4, TOK, 256), bf16), pltpu.VMEM((LENGTH, 256), f32), pltpu.VMEM((LENGTH, 256), f32),
        ],
    )(place, q, k, v, *do, lse, cos, sin, w, *blocks)


def projections_kernel(h_ref, dqkv_ref, sums_ref, gain_ref, first_ref):
    first_ref[:, :512] = dot(h_ref[...], dqkv_ref[...], TN).astype(bf16)
    small = jnp.where(iota((D, 128), 1) == 32, column_of(gain_ref[0:1]), sums_ref[...])
    first_ref[:, 512:] = small.astype(bf16)


def projections(h, dqkv, sums, gain):
    return call(
        projections_kernel, "projections", 1_500_000_000, 5_000_000, in_specs=[VECTOR] * 4, out_shape=shape(D, 640)
    )(h, dqkv, sums, gain)


def own_slots(expert, slot, z):
    start = ((expert % 16) // 4 * 2 + expert // 16) * CAP
    own = (expert % 4 == z) & (slot >= start) & (slot < start + CAP)
    return own, jnp.where(own, slot - start, 0)


def slot_tables(z, spread, start):
    own, place = own_slots(iota((EXPERTS, SLOTS), 0), iota((EXPERTS, SLOTS), 1), z)
    spread[...] = as_bf16(own)
    start[...] = jnp.sum(place, axis=0, keepdims=True).astype(f32)


SLOT_TABLES = [pltpu.VMEM((EXPERTS, SLOTS), bf16), pltpu.VMEM((1, SLOTS), f32)]


def gate_table(logits, codes):
    routed = codes >= 0
    logits = jnp.where(routed, logits, -1e30)
    e = jnp.where(routed, jnp.exp(logits - jnp.max(logits, axis=-1, keepdims=True)), 0.0)
    return e / jnp.sum(e, axis=-1, keepdims=True)


def split(values):
    high = values.astype(bf16)
    return high, (values - high.astype(f32)).astype(bf16)


def whole(*shape):
    return pl.BlockSpec(shape, lambda e: (0,) * len(shape))


def per_expert(*shape):
    return pl.BlockSpec((1,) + shape, lambda e: (e,) + (0,) * len(shape))


def rows_kernel(n, with_gates, z_ref, *refs):
    i = pl.program_id(0)
    z = z_ref[0]
    values_refs, refs = refs[:n], refs[n:]
    if with_gates:
        codes_refs, router_ref, refs = refs[:n], refs[n], refs[n + 1 :]
        rows_ref, gates_ref, turn_ref, values, codes, own, start = refs[-7:]
    else:
        rows_ref, turn_ref, values, codes, own, start = refs[-6:]
    for b in range(n):

        @pl.when(i == b)
        def _():
            values[...] = values_refs[b][:, :D]
            codes[...] = codes_refs[b][...] if with_gates else values_refs[b][:, D:]

    @pl.when(i == 0)
    def _():
        turn_ref[...] = jnp.zeros_like(turn_ref)
        mine, offset = own_slots(iota((SLOTS, EXPERTS), 1), iota((SLOTS, EXPERTS), 0), z)
        own[...] = as_bf16(mine)
        start[...] = jnp.sum(offset, axis=1, keepdims=True).astype(f32)

    slots = codes[:, :EXPERTS]
    place = as_bf16(dot(own[...], slots, NT) == start[...])
    rows_ref[:, 0] = dot(place, values[...]).astype(bf16).reshape(SHARE, CAP, D)
    if with_gates:
        table = gate_table(dot(values[...], router_ref[:, :EXPERTS]), slots.astype(f32))
        high, low = split(table)
        both = dot(place, high) + dot(place, low)
        gate = jnp.sum(both * own[...].astype(f32), axis=1, keepdims=True)
        gates_ref[:, 0] = gate.reshape(SHARE, CAP, 1)


def rows_of(z, first, blocks, codes, router, kept, turn):
    n, with_gates = len(blocks), router is not None
    args, specs = [z, *blocks], [SCALAR] + [whole(TOK, blocks[0].shape[1])] * n
    if with_gates:
        args += [*codes, router]
        specs += [pl.BlockSpec((TOK, 128), lambda e: (0, D // 128))] * n + [pl.BlockSpec((D, 128), lambda e: (0, 4))]
    args.append(turn)
    specs.append(ANYWHERE)
    widths = [(D, bf16)] + ([(1, f32)] if with_gates else [])
    out_specs = [pl.BlockSpec((SHARE, 1, CAP, w), lambda e: (0, first + e, 0, 0)) for w, _ in widths]
    out_shape = [shape(SHARE, BLOCKS, CAP, w, dtype=t) for w, t in widths]
    out_specs.append(whole(8, 128))
    out_shape.append(shape(8, 128, dtype=f32))
    aliases = {}
    if kept is not None:
        aliases = {len(args) + i: i for i in range(len(kept))}
        args += kept
        specs += [ANYWHERE] * len(kept)
    *kept, turn = call(
        functools.partial(rows_kernel, n, with_gates), "rows", n * 750_000_000, n * 2_000_000,
        grid=(n,), in_specs=specs, out_specs=out_specs, out_shape=out_shape, input_output_aliases=aliases,
        scratch_shapes=[
            pltpu.VMEM((TOK, D), bf16), pltpu.VMEM((TOK, 128), bf16), pltpu.VMEM((SLOTS, EXPERTS), bf16),
            pltpu.VMEM((SLOTS, 1), f32),
        ],
    )(*args)
    return kept, turn


def down_of(parts):
    return jnp.concatenate(
        [
            jnp.concatenate([parts[0, 128 * j : 128 * j + 128], parts[1, 128 * j : 128 * j + 128]], axis=0)
            for j in range(4)
        ],
        axis=1,
    )


def codes_specs():
    return [pl.BlockSpec((TOK, 128), lambda e: (0, D // 128))] * BLOCKS


PARTS = 2


def main_kernel(z_ref, x_ref, gy_ref, gate_ref, w_ref, *refs):
    codes_refs = refs[:8]
    act_ref, out_ref, own_ref, other_ref, kept, dgates, hidden, codes_kept, spread, start, mine = refs[8:]
    e = pl.program_id(0)

    @pl.when(e == 0)
    def _():
        for b in range(BLOCKS):
            codes_kept[b] = codes_refs[b][...]
        slot_tables(z_ref[0], spread, start)
        own, _ = own_slots(iota((SLOTS, EXPERTS), 1), iota((SLOTS, EXPERTS), 0), z_ref[0])
        mine[...] = own.astype(f32)

    down_w = down_of(w_ref[:, 1024:])
    gate_w = w_ref[:, :512].reshape(D, HALF)
    up_w = w_ref[:, 512:1024].reshape(D, HALF)
    both_w = jnp.concatenate([gate_w, up_w], axis=1)
    step = BLOCKS // PARTS
    for i in range(PARTS):
        blocks, rows = slice(step * i, step * i + step), slice(step * i * CAP, step * (i + 1) * CAP)
        x = x_ref[0, blocks].reshape(step * CAP, D)
        gate = gate_ref[0, blocks].reshape(step * CAP, 1)
        da = dot(gy_ref[0, blocks].reshape(step * CAP, D), down_w, NT)
        both = dot(x, both_w)
        g, u = both[:, :HALF], both[:, HALF:]
        s = jax.nn.sigmoid(g)
        silu = g * s
        act = silu * u
        dgates[blocks, e] = jnp.sum(act * da, axis=1, keepdims=True).reshape(step, CAP, 1)
        act_ref[0, rows] = (act * gate).astype(bf16)
        da = da * gate
        hidden[rows, :HALF] = (da * u * (s + silu * (1.0 - s))).astype(bf16)
        hidden[rows, HALF:] = (da * silu).astype(bf16)
        kept[blocks, e] = dot(hidden[rows], both_w, NT).astype(bf16).reshape(step, CAP, D)
    made = dot(hidden[...], x_ref[0].reshape(SLOTS, D), TN).astype(bf16)
    for i in range(2):
        out_ref[0, i, :512] = made[:, 512 * i : 512 * i + 512]
    made = dot(act_ref[0], gy_ref[0].reshape(SLOTS, D), TN).astype(bf16)
    for i in range(2):
        out_ref[0, i, 512:640] = made[128 * i : 128 * i + 128, :512]
        out_ref[0, i, 640:768] = made[128 * i : 128 * i + 128, 512:]

    @pl.when(e == SHARE - 1)
    def _():
        def pair(j, carry):
            for c, out in ((0, own_ref), (1, other_ref)):
                b = 2 * j + c
                place = as_bf16(dot(codes_kept[b][:, :EXPERTS], spread[...]) == start[...])
                out[j, :, :D] = dot(place, kept[b].reshape(SLOTS, D)).astype(bf16)
                scattered = dot(place, (mine[...] * dgates[b].reshape(SLOTS, 1)).astype(bf16))
                out[j, :, D:] = jnp.concatenate([scattered, jnp.zeros((TOK, 128 - EXPERTS), f32)], axis=1).astype(bf16)
            return carry

        lax.fori_loop(0, 4, pair, 0)


def main(z, x, gy, gates, weights, codes):
    back = shape(4, TOK, D + 128)
    return call(
        main_kernel, "experts", 25_000_000_000, 60_000_000,
        grid=(SHARE,),
        in_specs=[
            SCALAR, per_expert(BLOCKS, CAP, D), per_expert(BLOCKS, CAP, D), per_expert(BLOCKS, CAP, 1),
            pl.BlockSpec((2, 1536, 256), lambda e: (e, 0, 0)), *codes_specs(),
        ],
        out_specs=[
            per_expert(SLOTS, HALF), per_expert(2, 768, 512), whole(4, TOK, D + 128), whole(4, TOK, D + 128),
        ],
        out_shape=[shape(SHARE, SLOTS, HALF), shape(SHARE, 2, 768, 512), back, back],
        scratch_shapes=[
            pltpu.VMEM((BLOCKS, SHARE, CAP, D), bf16),
            pltpu.VMEM((BLOCKS, SHARE, CAP, 1), f32),
            pltpu.VMEM((SLOTS, 2 * HALF), bf16),
            pltpu.VMEM((BLOCKS, TOK, 128), bf16),
            *SLOT_TABLES,
            pltpu.VMEM((SLOTS, EXPERTS), f32),
        ],
    )(z, x, gy, gates, weights, *codes)


def outs_kernel(z_ref, act_ref, w_ref, *refs):
    codes_refs = refs[:8]
    own_ref, other_ref, kept, codes_kept, spread, start = refs[8:]
    e = pl.program_id(0)
    kept[:, e] = dot(act_ref[0], down_of(w_ref[...])).astype(bf16).reshape(BLOCKS, CAP, D)

    @pl.when(e == 0)
    def _():
        for b in range(BLOCKS):
            codes_kept[b] = codes_refs[b][...]
        slot_tables(z_ref[0], spread, start)

    @pl.when(e == SHARE - 1)
    def _():
        def pair(j, carry):
            for c, out in ((0, own_ref), (1, other_ref)):
                b = 2 * j + c
                place = as_bf16(dot(codes_kept[b][:, :EXPERTS], spread[...]) == start[...])
                out[j] = dot(place, kept[b].reshape(SLOTS, D)).astype(bf16)
            return carry

        lax.fori_loop(0, 4, pair, 0)


def outs(z, act, weights, codes):
    back = jax.ShapeDtypeStruct((4, TOK, D), bf16)
    return call(
        outs_kernel, "expert_outs", 6_000_000_000, 12_000_000,
        grid=(SHARE,),
        in_specs=[
            SCALAR, per_expert(SLOTS, HALF), pl.BlockSpec((2, 512, 256), lambda e: (e, 2, 0)), *codes_specs(),
        ],
        out_specs=[whole(4, TOK, D)] * 2,
        out_shape=[back, back],
        scratch_shapes=[
            pltpu.VMEM((BLOCKS, SHARE, CAP, D), bf16), pltpu.VMEM((BLOCKS, TOK, 128), bf16), *SLOT_TABLES,
        ],
    )(z, act, weights, *codes)


def finish_kernel(place_ref, mine_ref, got_ref, gate_ref, up_ref, down_ref):
    core = place_ref[1]
    for i, out in enumerate((gate_ref, up_ref)):
        for j in range(2):
            rows = slice(256 * i + 128 * j, 256 * i + 128 * j + 128)
            keep = mine_ref[rows, pl.ds(pl.multiple_of(256 * core, 256), 256)].astype(f32)
            out[:, pl.ds(pl.multiple_of(256 * j + 128 * core, 128), 128)] = keep.T
            got = got_ref[rows].astype(f32)
            out[:, pl.ds(pl.multiple_of(256 * j + 128 * (1 - core), 128), 128)] = got.T
    for j in range(2):
        down_ref[:, 512 * j : 512 * j + 512] = mine_ref[512 + 128 * j : 640 + 128 * j].astype(f32)


def finish(place, mine, got):
    return call(
        finish_kernel, "finish", 1_000_000, 4_000_000,
        in_specs=[SCALAR, VECTOR, VECTOR],
        out_shape=(shape(TOK, FF, dtype=f32), shape(TOK, FF, dtype=f32), shape(128, D, dtype=f32)),
    )(place, mine, got)


def shift(values, axis, by):
    n = 4 if axis in ("x", "z") else 2
    return lax.ppermute(values, axis, [(i, (i + by) % n) for i in range(n)])


def swap(values, axis):
    return shift(values, axis, 1)


def gather_z(values):
    return [values, shift(values, "z", 1), shift(values, "z", -1), shift(values, "z", 2)]


def with_core(blocks):
    return [(block, swap(block, "core")) for block in blocks]


def exchange_seq(own, across, beside, both):
    return [own, swap(across, "ylo"), swap(beside, "core"), swap(swap(both, "ylo"), "core")]


def core_sums(own, other):
    got = swap(other, "core")
    return [(own[j].astype(f32) + got[j].astype(f32)).astype(bf16) for j in range(4)]


def scatter_z(sums):
    return [sums[0], shift(sums[1], "z", -1), shift(sums[2], "z", 1), shift(sums[3], "z", 2)]


def fence(*values):
    return lax.optimization_barrier(values)


def on_device(
    tokens, norm1_gain, query_weight, key_weight, value_weight, output_weight, norm2_gain, router_weight,
    expert_gate, expert_up, expert_down, routes, cotangent,
):
    ylo, core = lax.axis_index("ylo"), lax.axis_index("core")
    z = lax.axis_index("z").astype(jnp.int32).reshape(1)
    place = jnp.stack([ylo, core]).astype(jnp.int32)

    own = tokens.reshape(TOK, D)
    across = swap(own, "ylo")
    gy_own = with_codes(routes.reshape(TOK, TOPK), cotangent.reshape(TOK, D))
    gy_blocks = gather_z(gy_own)

    packed, keep, send = pack(
        place, query_weight, key_weight, value_weight, router_weight, norm1_gain.reshape(1, 8), norm2_gain.reshape(1, 8),
        expert_gate.reshape(TOK, FF), expert_up.reshape(TOK, FF),
    )

    arrived = lax.all_to_all(packed, AXES, split_axis=0, concat_axis=0, tiled=True).reshape(D, 640)
    beside = swap(own, "core")

    expert_w = assemble(place, keep, swap(send, "core"), expert_down.reshape(128, D))
    expert_w, arrived, across, beside = fence(expert_w, arrived, across, beside)
    expert_w = lax.all_gather(expert_w, PLANE, axis=0).reshape(16, 1536, 256)

    lane = jnp.arange(128) % 32
    angles = jnp.arange(LENGTH).astype(f32)[:, None] * (rope_base ** (-2.0 * lane.astype(f32) / HEAD))[None, :]
    cos, sin = fence(jnp.cos(angles), jnp.sin(angles))
    blocks = [own, across, beside, swap(across, "core")]
    q, k, v, *mixed, lse, hidden_all, gains = front(place, blocks, arrived, cos, sin)

    output_rows = jnp.concatenate([output_weight, swap(output_weight, "ylo")], axis=1)
    output_rows, _ = fence(output_rows, arrived)
    output_own = lax.all_to_all(
        jnp.broadcast_to(output_rows[None], (32, 8, 2 * D)), FSDP, split_axis=0, concat_axis=0, tiled=True
    ).reshape(TOK, 2 * D)

    mixed = exchange_seq(*mixed)
    output_own, *rest = fence(output_own, *mixed, *gy_blocks)
    mixed, gy_blocks = rest[:4], rest[4:]
    output_other = swap(output_own, "core")
    gy_blocks = [block for pair in with_core(gy_blocks) for block in pair]
    residual, hidden_two = mid(own, mixed, output_own, output_other, gains)

    h_blocks = gather_z(hidden_two)
    turn, _ = fence(jnp.zeros((8, 128), f32), hidden_two)
    gy_rows, turn = rows_of(z, 0, gy_blocks, None, None, None, turn)
    rows, turn = rows_of(z, 0, (hidden_two, swap(hidden_two, "core")), gy_blocks[:2], arrived, None, turn)
    *h_blocks, turn = fence(*h_blocks, turn)
    h_blocks = [block for pair in with_core(h_blocks[1:]) for block in pair]
    rows, turn = rows_of(z, 2, h_blocks, gy_blocks[2:], arrived, rows, turn)
    (gy_rows,), (rows, gate_rows) = gy_rows, rows

    act, expert_grads, back_own, back_other = main(z, rows, gy_rows, gate_rows, expert_w, gy_blocks)
    sums = core_sums(back_own, back_other)
    parts = scatter_z(sums)
    moe_act, *_ = fence(act, *sums)
    moe_own, moe_other = outs(z, moe_act, expert_w, gy_blocks)
    expert_grads = lax.psum_scatter(expert_grads.reshape(16 * 768, 512), PLANE, scatter_dimension=0, tiled=True)

    moe_sums = core_sums(moe_own, moe_other)
    *do, grad_residual, keep, send, small = turn_back(
        place, parts, gy_own, residual, arrived, gains, mixed, output_own, output_other
    )

    do = exchange_seq(*do)
    grad_output_sum = (keep.astype(f32) + swap(send, "core").astype(f32)).astype(bf16).reshape(64, 8, D)
    grad_output_sum, *rest = fence(grad_output_sum, *moe_sums, *do)
    moe_sums, do = rest[:4], rest[4:]
    moe_near = [shift(moe_sums[1], "z", -1), shift(moe_sums[2], "z", 1)]
    grad_output = lax.all_to_all(grad_output_sum, ("ylo",) + FSDP, split_axis=0, concat_axis=0, tiled=True)
    dqkv, keep, send, gain = back(place, q, k, v, do, lse, cos, sin, arrived, blocks)
    dqkv, keep, send, own, grad_output, *moe_near = fence(dqkv, keep, send, own, grad_output, *moe_near)
    first = projections(hidden_all, dqkv, small, gain)

    away = jnp.where(core == 0, expert_grads[:512, 256:], expert_grads[:512, :256])
    finished = finish(place, expert_grads, swap(away, "core"))

    pair = (keep.astype(f32) + swap(send, "core").astype(f32)).astype(bf16)
    kept = jnp.where(ylo == 0, pair[0], pair[1])
    got = swap(jnp.where(ylo == 0, pair[1], pair[0]), "ylo")
    got, moe_far, grad_gate, grad_up, grad_down = fence(got, shift(moe_sums[3], "z", 2), *finished)
    grad_hidden_one = kept.astype(f32) + got.astype(f32)
    first = lax.all_to_all(first.reshape(128, 8, 640), AXES, split_axis=0, concat_axis=0, tiled=True)
    grad_output = jnp.sum(grad_output.astype(f32), axis=0)
    layer_out = sum(part.astype(f32) for part in (moe_sums[0], *moe_near, moe_far))
    layer_out = (residual + layer_out).astype(bf16).reshape(1, TOK, D)
    first = jnp.sum(first.astype(f32).reshape(4, 32, 8, 640), axis=1)
    grad_query = first[:, :, :256].transpose(1, 0, 2).reshape(8, D)
    grad_key = first[:, :, 256:384].transpose(1, 0, 2).reshape(8, 512)
    grad_value = first[:, :, 384:512].transpose(1, 0, 2).reshape(8, 512)
    small = jnp.sum(first[:, :, 512:], axis=0)

    inputs = own.astype(f32)
    factor_one = lax.rsqrt(jnp.mean(inputs * inputs, axis=-1, keepdims=True) + epsilon)
    normed_one = inputs * factor_one
    scaled = grad_hidden_one * gains[0:1]
    grad_inputs = grad_residual + factor_one * (
        scaled - normed_one * jnp.mean(scaled * normed_one, axis=-1, keepdims=True)
    )

    return (
        layer_out, grad_inputs.reshape(1, TOK, D), small[:, 32], grad_query, grad_key, grad_value, grad_output,
        small[:, 33], small[:, :EXPERTS], grad_gate.reshape(1, TOK, FF), grad_up.reshape(1, TOK, FF),
        grad_down.reshape(1, 128, D),
    )


def solution(mesh):
    fine = Mesh(mesh.devices.reshape(2, 2, 2, 4, 4), AXES)
    tok = P(FSDP, SEQ, None)
    row = P(AXES, None)
    vec = P(AXES)
    in_specs = (tok, vec, row, row, row, row, vec, row, tok, tok, tok, tok, tok)
    out_specs = (tok, tok, vec, row, row, row, row, vec, row, tok, tok, tok)
    return jax.shard_map(on_device, mesh=fine, in_specs=in_specs, out_specs=out_specs, check_vma=False)
```
